256 devices in a mesh: tensor: 8 (over x, y_lo), seq: 32 (over y_hi, z, core).
Axes of the slice: x: 4, y: 4 (y_hi: 2, y_lo: 2; y = y_hi * 2 + y_lo), z: 8, core: 2. Of those that a mesh axis runs over, the one named last changes fastest.
Arguments:
- tokens: bfloat16 [32, 1024, 5120], P('seq', 'tensor'), may hold values from -6 to 6
- query_weight: bfloat16 [5120, 1024], P(None, 'tensor'), may hold values from -0.078125 to 0.078125
- key_weight: bfloat16 [5120, 1024], P(None, 'tensor'), may hold values from -0.078125 to 0.078125
- value_weight: bfloat16 [5120, 5120], P(None, 'tensor'), may hold values from -0.078125 to 0.078125
- conv_taps: float32 [3, 5120], P(None, 'tensor'), may hold values from 0.2 to 2
- norm_gain: float32 [5120], P('tensor'), may hold values from 8 to 64
Outputs:
- mixed: bfloat16 [32, 1024, 5120], P('seq', 'tensor')
The draws below stay inside these ranges and needn't reach their ends.
All inputs are finite; a program needn't handle non-finite values.
Results may differ from the reference program's by a relative error of at most 0.012.
Values may be sent and summed in bfloat16 or wider, within the bound.
No kernel may reach another device: no remote copies, remote signals or barrier semaphores. Data moves between devices by JAX's collectives and lax.ppermute only.
A program may use at most 128 MiB of HBM per device.

```python
import math
import jax
import jax.numpy as jnp
from jax import lax

D = 5120
HEADS = 64
FEAT = 16
KW = 3
HEAD_DIM = 80
SEG_LEN = 1024
SEGS = 32


def steps_of(own_key, dims, cuts, least, top_value):
    level, own = 1.0, jax.random.fold_in(own_key, 6)
    for position, blocks in cuts:
        steps = jnp.exp(jax.random.uniform(jax.random.fold_in(own, position), (blocks,), jnp.float32, least / len(cuts), top_value / len(cuts)))
        level = level * jnp.repeat(steps, dims[position] // blocks).reshape([-1 if axis == position else 1 for axis in range(len(dims))])
    return level


def normal_values(key, extent, width, limit, cuts=(), dtype=jnp.bfloat16):
    level = steps_of(key, extent, cuts, -0.22, 0.18) if cuts else 1.0
    drawn = jax.random.normal(key, extent, jnp.float32) * width * level
    return jnp.minimum(jnp.maximum(drawn, -limit), limit).astype(dtype)


def setup_inputs(seed: int = 0) -> dict:
    seeds = jax.random.split(jax.random.key(seed), 7)
    tokens = normal_values(seeds[0], (SEGS, SEG_LEN, D), 1.0, 6.0, ((0, 32), (1, 8)))
    query_weight = normal_values(seeds[1], (D, HEADS * FEAT), D ** -0.5, 0.078125, ((1, 8),))
    key_weight = normal_values(seeds[2], (D, HEADS * FEAT), D ** -0.5, 0.078125, ((1, 8),))
    value_weight = normal_values(seeds[3], (D, D), D ** -0.5, 0.078125, ((1, 8),))
    conv_taps = jnp.clip(jnp.exp(math.log(2.0) - 2.3025851 * jax.random.uniform(seeds[4], (KW, D), jnp.float32) ** steps_of(seeds[4], (KW, D), ((1, 8),), -0.2, 0.2)), 0.2, 2.0)
    norm_gain = jnp.clip(jnp.exp(math.log(64.0) - 2.0794415 * jax.random.uniform(seeds[5], (D,), jnp.float32) ** steps_of(seeds[5], (D,), ((0, 8),), -0.2, 0.2)), 8.0, 64.0)
    return dict(tokens=tokens, query_weight=query_weight, key_weight=key_weight, value_weight=value_weight, conv_taps=conv_taps, norm_gain=norm_gain)


def expand_features(scaled):
    feat_count, row_count = scaled.shape
    outer = (scaled[:, None, :] * scaled[None, :, :]).reshape(feat_count * feat_count, row_count)
    ones_row = jnp.ones((1, row_count), jnp.float32)
    return jnp.concatenate([ones_row, scaled, outer * (0.5 ** 0.5)], axis=0)


def one_head(operands):
    query_part, key_part, value_part = operands
    feat_query = expand_features(query_part).astype(jnp.bfloat16)
    feat_key = expand_features(key_part).astype(jnp.bfloat16)
    state = jnp.dot(feat_key, value_part, preferred_element_type=jnp.float32)
    total = jnp.sum(feat_key.astype(jnp.float32), axis=1)
    state_low = state.astype(jnp.bfloat16)
    numer = jnp.dot(feat_query.T, state_low, preferred_element_type=jnp.float32)
    denom = jnp.dot(feat_query.astype(jnp.float32).T, total, precision=lax.Precision.HIGHEST)
    return numer / denom[:, None]


def reference(tokens, query_weight, key_weight, value_weight, conv_taps, norm_gain):
    inputs = tokens.reshape(-1, D)
    total_rows = inputs.shape[0]
    queries = jnp.dot(inputs, query_weight, preferred_element_type=jnp.float32)
    keys_full = jnp.dot(inputs, key_weight, preferred_element_type=jnp.float32)
    values = jnp.dot(inputs, value_weight, preferred_element_type=jnp.float32).astype(jnp.bfloat16)
    reach = KW // 2
    padded = jnp.pad(values, ((reach, reach), (0, 0)))
    conv_sum = jnp.zeros((total_rows, D), jnp.float32)
    for offset in range(KW):
        conv_sum = conv_sum + conv_taps[offset] * padded[offset:offset + total_rows].astype(jnp.float32)
    conv = conv_sum.astype(jnp.bfloat16)
    query_heads = (queries * 0.5).reshape(total_rows, HEADS, FEAT).transpose(1, 2, 0)
    key_heads = (keys_full * 0.5).reshape(total_rows, HEADS, FEAT).transpose(1, 2, 0)
    value_heads = conv.reshape(total_rows, HEADS, HEAD_DIM).transpose(1, 0, 2)
    attn = lax.map(one_head, (query_heads, key_heads, value_heads))
    attn = attn.transpose(1, 0, 2).reshape(total_rows, D)
    mixed = attn * norm_gain + conv.astype(jnp.float32)
    return mixed.astype(jnp.bfloat16).reshape(tokens.shape)
```

```python
import functools

import jax
import jax.numpy as jnp
from jax import lax
from jax.experimental import pallas as pl
from jax.experimental.pallas import tpu as pltpu
from jax.sharding import PartitionSpec as P

FEAT = 16
HEAD_DIM = 80
GROUP = 8
NX, NY, NZ = 4, 4, 8
AXES = ("tensor", "seq")
PIECE = 512
FROWS = 160
MROWS = 192
BLOCK = 128
ROWS = 4 * BLOCK
HALO = 16
VCOLS = GROUP * HEAD_DIM
QCOLS = GROUP * FEAT
GCOLS = VCOLS + 2 * QCOLS
SPLIT = MROWS // NY


def device_of(x, y, z, core):
    x, y, z = x % NX, y % NY, z % NZ
    tensor = x * 2 + (y & 1)
    seq = ((y >> 1) * NZ + z) * 2 + core
    return tensor * 32 + seq


def everywhere():
    return [
        (x, y, z, core)
        for x in range(NX)
        for y in range(NY)
        for z in range(NZ)
        for core in range(2)
    ]


def receive(array, source_of):
    pairs = [(device_of(*source_of(*place)), device_of(*place)) for place in everywhere()]
    return lax.ppermute(array, AXES, pairs)


def from_x(array, step):
    return receive(array, lambda x, y, z, c: (x + step, y, z, c))


def from_y(array, step):
    return receive(array, lambda x, y, z, c: (x, y + step, z, c))


def from_z(array, step):
    return receive(array, lambda x, y, z, c: (x, y, z + step, c))


def from_core(array):
    return receive(array, lambda x, y, z, c: (x, y, z, 1 - c))


def from_block(array, step):
    place = {}
    for spot in everywhere():
        x, y, z, core = spot
        index = (((y >> 1) * NZ + z) * 2 + core) * 8 + x * 2 + (y & 1)
        place[index] = device_of(*spot)
    pairs = [(place[b + step], place[b]) for b in place if b + step in place]
    return lax.ppermute(array, AXES, pairs)


def features(scaled, off_weight):
    root = 0.5**0.5
    rows = scaled.shape[1]
    parts = [scaled, scaled * scaled * root]
    for step in range(1, FEAT // 2):
        turned = pltpu.roll(scaled, FEAT - step, 0)
        parts.append(scaled * turned * (root * off_weight))
    half = scaled[: FEAT // 2] * scaled[FEAT // 2 :] * (root * off_weight)
    parts.append(half)
    first = lax.broadcasted_iota(jnp.int32, (FEAT // 2, rows), 0) == 0
    parts.append(jnp.where(first, 1.0, 0.0).astype(jnp.float32))
    return jnp.concatenate(parts, axis=0)


def window_of(head):
    start = head * HEAD_DIM // 128 * 128
    stop = -(-(head + 1) * HEAD_DIM // 128) * 128
    return start, stop


def head_mask(head, rows):
    start, stop = window_of(head)
    lane = lax.broadcasted_iota(jnp.int32, (rows, stop - start), 1) + start
    return (lane >= head * HEAD_DIM) & (lane < (head + 1) * HEAD_DIM)


def project_body(x_copies, w_copies, taps, conv_out, query_out, state_out, xs, ws, acc, conv_scr):
    for copy in x_copies:
        copy.start()
    for group in w_copies:
        for copy in group:
            copy.start()
    for copy in x_copies:
        copy.wait()
    for copies in w_copies:
        for copy in copies:
            copy.wait()
    depth = xs.shape[1]
    acc[...] = jnp.zeros_like(acc)

    def step(index, carry):
        span = pl.ds(pl.multiple_of(index * PIECE, PIECE), PIECE)
        acc[...] += jnp.dot(xs[:, span], ws[span, :], preferred_element_type=jnp.float32)
        return carry

    lax.fori_loop(0, depth // PIECE, step, 0)

    query_out[...] = acc[:ROWS, :QCOLS].T * 0.5
    key = acc[:ROWS, QCOLS : 2 * QCOLS].T * 0.5
    values = acc[:, 2 * QCOLS :].astype(jnp.bfloat16).astype(jnp.float32)
    row = lax.broadcasted_iota(jnp.int32, (BLOCK, VCOLS), 0)
    for block in range(4):
        mid = values[block * BLOCK : (block + 1) * BLOCK]
        before = values[ROWS + 2 * block : ROWS + 2 * block + 1]
        after = values[ROWS + 2 * block + 1 : ROWS + 2 * block + 2]
        low = jnp.where(row == 0, before, pltpu.roll(mid, 1, 0))
        high = jnp.where(row == BLOCK - 1, after, pltpu.roll(mid, BLOCK - 1, 0))
        conv = taps[0:1, :] * low + taps[1:2, :] * mid + taps[2:3, :] * high
        conv_scr[block * BLOCK : (block + 1) * BLOCK, :] = conv.astype(jnp.bfloat16)
    conv_out[...] = conv_scr[...]
    state_out[...] = jnp.zeros_like(state_out)
    ones = jnp.ones((8, ROWS), jnp.bfloat16)
    for head in range(GROUP):
        feat = features(key[head * FEAT : (head + 1) * FEAT], 1.0).astype(jnp.bfloat16)
        start, stop = window_of(head)
        state = jnp.dot(feat, conv_scr[:, start:stop], preferred_element_type=jnp.float32)
        state_out[:FROWS, start:stop] += jnp.where(head_mask(head, FROWS), state, 0.0)
        total = lax.dot_general(
            ones, feat, (((1,), (1,)), ((), ())), preferred_element_type=jnp.float32
        )
        state_out[FROWS + head : FROWS + head + 1, :FROWS] = total[0:1]


def x_copies_of(x_refs, xs, sems):
    copies, at = [], 0
    for ref in x_refs:
        rows = ref.shape[0]
        copies.append(pltpu.make_async_copy(ref, xs.at[pl.ds(at, rows)], sems.at[len(copies)]))
        at += rows
    return copies


def own_kernel(x0, x1, x2a, x2b, x3, halo, qw, kw, vw, taps, conv_out, query_out, state_out, xs, ws, acc, conv_scr, xsem, wsem):
    copies = x_copies_of((x0, x1, x2a, x2b, x3, halo), xs, xsem)
    w_copies = [[
        pltpu.make_async_copy(qw, ws.at[:, pl.ds(0, QCOLS)], wsem.at[0]),
        pltpu.make_async_copy(kw, ws.at[:, pl.ds(QCOLS, QCOLS)], wsem.at[1]),
        pltpu.make_async_copy(vw, ws.at[:, pl.ds(2 * QCOLS, VCOLS)], wsem.at[2]),
    ]]
    project_body(copies, w_copies, taps, conv_out, query_out, state_out, xs, ws, acc, conv_scr)


def other_kernel(offsets, x0, x1, x2a, x2b, x3, halo, *rest):
    pieces, (taps, conv_out, query_out, state_out, xs, ws, acc, conv_scr, xsem, wsem) = rest[:-10], rest[-10:]
    copies = x_copies_of((x0, x1, x2a, x2b, x3, halo), xs, xsem)
    w_copies = []
    for index, piece in enumerate(pieces):
        span = pl.ds(pl.multiple_of(offsets[index], PIECE), PIECE)
        w_copies.append([pltpu.make_async_copy(piece, ws.at[span], wsem.at[index])])
    project_body(copies, w_copies, taps, conv_out, query_out, state_out, xs, ws, acc, conv_scr)


def project(kernel, scalars, blocks, weights, taps):
    depth = blocks[0].shape[1]
    rows = ROWS + HALO
    hbm = pl.BlockSpec(memory_space=pl.ANY)
    vmem = pl.BlockSpec(memory_space=pltpu.VMEM)
    return pl.pallas_call(
        kernel,
        out_shape=(
            jax.ShapeDtypeStruct((ROWS, VCOLS), jnp.bfloat16),
            jax.ShapeDtypeStruct((QCOLS, ROWS), jnp.float32),
            jax.ShapeDtypeStruct((MROWS, VCOLS), jnp.float32),
        ),
        in_specs=[pl.BlockSpec(memory_space=pltpu.SMEM)] * len(scalars)
        + [hbm] * (len(blocks) + len(weights))
        + [vmem],
        out_specs=(vmem, vmem, vmem),
        scratch_shapes=[
            pltpu.VMEM((rows, depth), jnp.bfloat16),
            pltpu.VMEM((depth, GCOLS), jnp.bfloat16),
            pltpu.VMEM((rows, GCOLS), jnp.float32),
            pltpu.VMEM((ROWS, VCOLS), jnp.bfloat16),
            pltpu.SemaphoreType.DMA((len(blocks),)),
            pltpu.SemaphoreType.DMA((max(len(weights), 1),)),
        ],
        compiler_params=pltpu.CompilerParams(vmem_limit_bytes=40 * 1024 * 1024),
        cost_estimate=pl.CostEstimate(
            flops=2 * rows * depth * GCOLS, bytes_accessed=2 * depth * (rows + GCOLS), transcendentals=0
        ),
    )(*scalars, *blocks, *weights, taps)


def attend_kernel(place, query_a, query_b, state_a, state_b, conv_a, conv_b, gain_a, gain_b, *rest):
    outs, acc = rest[:4], rest[4]
    groups = ((query_a, state_a, conv_a, gain_a), (query_b, state_b, conv_b, gain_b))
    for number, (query, state, conv, gain) in enumerate(groups):
        acc[...] = jnp.zeros_like(acc)
        totals = state[FROWS : FROWS + 16, :FROWS]
        for head in range(GROUP):
            feat = features(query[head * FEAT : (head + 1) * FEAT, :], 2.0)
            denom = jnp.dot(totals, feat.astype(jnp.bfloat16), preferred_element_type=jnp.float32)
            scale = 1.0 / denom[head : head + 1, :]
            scaled = (feat * scale).astype(jnp.bfloat16)
            start, stop = window_of(head)
            part = state[:FROWS, start:stop]
            part = jnp.where(head_mask(head, FROWS), part, jnp.zeros_like(part))
            acc[:, start:stop] += lax.dot_general(
                scaled, part, (((0,), (0,)), ((), ())), preferred_element_type=jnp.float32
            )
        spot = place[0] if number == 0 else 1 - place[0]
        span = pl.ds(pl.multiple_of(spot * VCOLS, VCOLS), VCOLS)
        for block, out in enumerate(outs):
            rows = slice(block * BLOCK, (block + 1) * BLOCK)
            mixed = acc[rows, :] * gain[0:1, :] + conv[rows, :].astype(jnp.float32)
            out[:, span] = mixed.astype(jnp.bfloat16)


def attend(place, queries, states, convs, gains):
    vmem = pl.BlockSpec(memory_space=pltpu.VMEM)
    return pl.pallas_call(
        attend_kernel,
        out_shape=[jax.ShapeDtypeStruct((BLOCK, 2 * VCOLS), jnp.bfloat16)] * 4,
        in_specs=[pl.BlockSpec(memory_space=pltpu.SMEM)] + [vmem] * 8,
        out_specs=[vmem] * 4,
        scratch_shapes=[pltpu.VMEM((ROWS, VCOLS), jnp.float32)],
        compiler_params=pltpu.CompilerParams(vmem_limit_bytes=32 * 1024 * 1024),
    )(place, *queries, *states, *convs, *gains)


def pack_rows(weights, start, count):
    return jnp.concatenate(
        [lax.dynamic_slice_in_dim(w, start, count, axis=0) for w in weights], axis=1
    )


def body(tokens, query_weight, key_weight, value_weight, conv_taps, norm_gain):
    tensor, seq = lax.axis_index("tensor"), lax.axis_index("seq")
    x_at, y_low = tensor // 2, tensor % 2
    core, z_odd = seq % 2, (seq // 2) % 2
    y_at = (seq // 16) * 2 + y_low
    rows = tokens.reshape(BLOCK, tokens.shape[-1])
    weights = (query_weight, key_weight, value_weight)
    half = rows.shape[1] // 2

    one = from_x(rows, 1)
    three = from_x(rows, -1)

    def from_side(array):
        return receive(array, lambda x, y, z, c: (x, y + 2 * c - 1, z, c))

    base = core * half
    sent = [
        pack_rows(weights, base + z_odd * 2 * PIECE, PIECE),
        pack_rows(weights, base + z_odd * 2 * PIECE + PIECE, PIECE),
        pack_rows(weights, base + 4 * PIECE, PIECE),
    ]
    side = [from_side(part) for part in sent]
    low_z = from_z(side[0], -1)
    high_z = from_z(side[1], 1)
    mine = [side[0], side[1], low_z, high_z, side[2]]
    theirs = [from_core(part) for part in mine]
    steps = jnp.stack(
        [z_odd * 2, z_odd * 2 + 1, (1 - z_odd) * 2, (1 - z_odd) * 2 + 1, jnp.full_like(z_odd, 4)]
    )
    offsets = jnp.concatenate([base + steps * PIECE, (half - base) + steps * PIECE]).astype(jnp.int32)

    two_a = from_x(one[: BLOCK // 2], 1)
    two_b = from_x(three[BLOCK // 2 :], -1)

    edges = jnp.concatenate(
        [from_block(rows[BLOCK - 1 :], -1), from_block(rows[:1], 1)], axis=0
    )
    halo = jnp.concatenate(
        [edges, from_x(edges, 1), from_x(edges, 2), from_x(edges, -1), jnp.zeros((8, rows.shape[1]), rows.dtype)],
        axis=0,
    )
    small = jnp.concatenate([conv_taps, norm_gain[None]], axis=0)
    small_other = receive(small, lambda x, y, z, c: (x, y ^ 1, z, c))

    blocks = (rows, one, two_a, two_b, three, halo)
    conv_own, query_own, state_own = project(own_kernel, (), blocks, weights, small)
    conv_other, query_other, state_other = project(
        other_kernel, (offsets,), blocks, (*mine, *theirs), small_other
    )

    same = core == y_low
    keep = jnp.where(same, state_own, state_other)
    give = jnp.where(same, state_other, state_own)
    summed = keep + from_core(give)
    low = summed.astype(jnp.bfloat16)

    def quarter(array, step):
        return lax.dynamic_slice_in_dim(array, ((y_at + step) % NY) * SPLIT, SPLIT, axis=0)

    part = quarter(summed, 0)
    for step in (1, 2, 3):
        part = part + from_y(quarter(low, step), -step).astype(jnp.float32)
    low = part.astype(jnp.bfloat16)
    for step in (1, -1, 2):
        part = part + from_z(low, step).astype(jnp.float32)
    low = part.astype(jnp.bfloat16)
    part = (part + from_z(low, 4).astype(jnp.float32)).astype(jnp.bfloat16)
    ring = [part] + [from_y(part, step) for step in (1, 2, 3)]
    state_mine = lax.dynamic_slice_in_dim(
        jnp.concatenate(ring + ring[:3], axis=0), ((NY - y_at) % NY) * SPLIT, MROWS, axis=0
    )
    state_theirs = from_core(state_mine)
    full_own = jnp.where(same, state_mine, state_theirs)
    full_other = jnp.where(same, state_theirs, state_mine)

    out = attend(
        y_low.reshape(1).astype(jnp.int32),
        (query_own, query_other),
        (full_own, full_other),
        (conv_own, conv_other),
        (small[3:], small_other[3:]),
    )
    back = [out[0], from_x(out[3], 1), from_x(out[2], 2), from_x(out[1], -1)]
    doubled = jnp.stack(back + back[:3], axis=0)
    ordered = lax.dynamic_slice_in_dim(doubled, (NX - x_at) % NX, NX, axis=0)
    result = ordered.transpose(1, 0, 2).reshape(BLOCK, -1)
    return result.reshape(tokens.shape)


def solution(mesh):
    return jax.shard_map(
        body,
        mesh=mesh,
        in_specs=(
            P("seq", "tensor", None),
            P(None, "tensor"),
            P(None, "tensor"),
            P(None, "tensor"),
            P(None, "tensor"),
            P("tensor"),
        ),
        out_specs=P("seq", "tensor", None),
        check_vma=False,
    )
```

```python
import functools

import jax
import jax.numpy as jnp
from jax import lax
from jax.experimental import pallas as pl
from jax.experimental.pallas import tpu as pltpu
from jax.sharding import PartitionSpec as P

FEAT = 16
HEAD_DIM = 80
GROUP = 8
NX, NY, NZ = 4, 4, 8
AXES = ("tensor", "seq")
PIECE = 512
PIECES = (PIECE,) * 10
VMEM_LIMIT = 58 * 1024 * 1024
VMEM_SMALL = 16 * 1024 * 1024
FROWS = 160
MROWS = 192
BLOCK = 128
ROWS = 4 * BLOCK
AHEAD = 3
SLOTS = (0, 1, 3, 2)
VCOLS = GROUP * HEAD_DIM
QCOLS = GROUP * FEAT
GCOLS = VCOLS + 2 * QCOLS
SPLIT = MROWS // NY


def device_of(x, y, z, core):
    x, y, z = x % NX, y % NY, z % NZ
    tensor = x * 2 + (y & 1)
    seq = ((y >> 1) * NZ + z) * 2 + core
    return tensor * 32 + seq


def everywhere():
    return [
        (x, y, z, core)
        for x in range(NX)
        for y in range(NY)
        for z in range(NZ)
        for core in range(2)
    ]


def receive(array, source_of):
    pairs = [(device_of(*source_of(*place)), device_of(*place)) for place in everywhere()]
    return lax.ppermute(array, AXES, pairs)


def from_x(array, step):
    return receive(array, lambda x, y, z, c: (x + step, y, z, c))


def from_y(array, step):
    return receive(array, lambda x, y, z, c: (x, y + step, z, c))


def from_z(array, step):
    return receive(array, lambda x, y, z, c: (x, y, z + step, c))


def from_core(array):
    return receive(array, lambda x, y, z, c: (x, y, z, 1 - c))


def from_far(array):
    place = {}
    for x, y, z, core in everywhere():
        place[x, y & 1, ((y >> 1) * NZ + z) * 2 + core] = device_of(x, y, z, core)
    pairs = []
    for (x, odd, segment), target in place.items():
        source = place.get((x, 1 - odd, segment + (1 if odd else -1)))
        if source is not None:
            pairs.append((source, target))
    return lax.ppermute(array, AXES, pairs)


def features(scaled, off_weight):
    root = 0.5**0.5
    rows = scaled.shape[1]
    parts = [scaled, scaled * scaled * root]
    for step in range(1, FEAT // 2):
        turned = pltpu.roll(scaled, FEAT - step, 0)
        parts.append(scaled * turned * (root * off_weight))
    half = scaled[: FEAT // 2] * scaled[FEAT // 2 :] * (root * off_weight)
    parts.append(half)
    first = lax.broadcasted_iota(jnp.int32, (FEAT // 2, rows), 0) == 0
    parts.append(jnp.where(first, 1.0, 0.0).astype(jnp.float32))
    return jnp.concatenate(parts, axis=0)


def window_of(head):
    start = head * HEAD_DIM // 128 * 128
    stop = -(-(head + 1) * HEAD_DIM // 128) * 128
    return start, stop


def head_mask(head, rows):
    start, stop = window_of(head)
    lane = lax.broadcasted_iota(jnp.int32, (rows, stop - start), 1) + start
    return (lane >= head * HEAD_DIM) & (lane < (head + 1) * HEAD_DIM)


def project_kernel(other, counts, slots, *refs):
    refs = list(refs)
    offsets = refs.pop(0) if other else None
    blocks = [refs.pop(0) for _ in counts]
    weights = [refs.pop(0) for _ in range(len(PIECES) if other else 3)]
    value_out, query_key_out, edge_out, xs, ws, acc, xsem, wsem = refs
    pieces, at = [], 0
    for index, count in enumerate(PIECES):
        start = pl.multiple_of(offsets[index], 256) if other else at
        copies, row = [], 0
        for number, (ref, rows) in enumerate(zip(blocks, counts)):
            copies.append(
                pltpu.make_async_copy(
                    ref.at[:, pl.ds(start, count)],
                    xs.at[pl.ds(row, rows), pl.ds(at, count)],
                    xsem.at[index, number],
                )
            )
            row += rows
        if other:
            copies.append(pltpu.make_async_copy(weights[index], ws.at[pl.ds(at, count)], wsem.at[index, 0]))
        else:
            for kind, (col, width) in enumerate(((0, QCOLS), (QCOLS, QCOLS), (2 * QCOLS, VCOLS))):
                copies.append(
                    pltpu.make_async_copy(
                        weights[kind].at[pl.ds(at, count)],
                        ws.at[pl.ds(at, count), pl.ds(col, width)],
                        wsem.at[index, kind],
                    )
                )
        pieces.append((copies, at, count))
        at += count
    for copies, _, _ in pieces[:AHEAD]:
        for copy in copies:
            copy.start()
    for index, (copies, at, count) in enumerate(pieces):
        for copy in copies:
            copy.wait()
        if index + AHEAD < len(pieces):
            for copy in pieces[index + AHEAD][0]:
                copy.start()
        if index % 2 == 0:
            continue
        span = slice(at - count, at + count)
        part = jnp.dot(xs[:, span], ws[span, :], preferred_element_type=jnp.float32)
        if index == 1:
            acc[...] = part
        else:
            acc[...] += part
    query_key_out[...] = acc[:, : 2 * QCOLS]
    values = acc[:, 2 * QCOLS :].astype(jnp.bfloat16)
    value_out[...] = values
    edge_out[...] = jnp.zeros_like(edge_out)
    for block, slot in enumerate(slots):
        for end, row in ((0, block * BLOCK), (1, block * BLOCK + BLOCK - 1)):
            line = acc[row : row + 1, 2 * QCOLS :].astype(jnp.bfloat16).astype(jnp.float32)
            edge_out[2 * slot + end : 2 * slot + end + 1, :] = line


def project(offsets, blocks, slots, weights):
    counts = tuple(block.shape[0] for block in blocks)
    depth = blocks[0].shape[1]
    rows = sum(counts)
    hbm = pl.BlockSpec(memory_space=pltpu.HBM)
    vmem = pl.BlockSpec(memory_space=pltpu.VMEM)
    scalars = [] if offsets is None else [offsets]
    return pl.pallas_call(
        functools.partial(project_kernel, offsets is not None, counts, slots),
        out_shape=(
            jax.ShapeDtypeStruct((rows, VCOLS), jnp.bfloat16),
            jax.ShapeDtypeStruct((rows, 2 * QCOLS), jnp.float32),
            jax.ShapeDtypeStruct((8, VCOLS), jnp.float32),
        ),
        in_specs=[pl.BlockSpec(memory_space=pltpu.SMEM)] * len(scalars) + [hbm] * (len(blocks) + len(weights)),
        out_specs=(vmem,) * 3,
        scratch_shapes=[
            pltpu.VMEM((rows, depth), jnp.bfloat16),
            pltpu.VMEM((depth, GCOLS), jnp.bfloat16),
            pltpu.VMEM((rows, GCOLS), jnp.float32),
            pltpu.SemaphoreType.DMA((len(PIECES), len(blocks))),
            pltpu.SemaphoreType.DMA((len(PIECES), 3)),
        ],
        compiler_params=pltpu.CompilerParams(vmem_limit_bytes=VMEM_LIMIT),
        cost_estimate=pl.CostEstimate(
            flops=2 * rows * depth * GCOLS, bytes_accessed=2 * depth * (rows + GCOLS), transcendentals=0
        ),
    )(*scalars, *blocks, *weights)


def state_kernel(final, place, values, query_key, near, far, taps, *refs):
    refs = list(refs)
    other_state = refs.pop(0) if final else None
    conv_out, query_out = refs.pop(0), refs.pop(0)
    keep_out, give_out = (refs.pop(0), refs.pop(0)) if final else (None, None)
    state = refs.pop(0)
    x_at, even = place[0], place[1] == 0
    query_out[...] = query_key[:, :QCOLS].T * 0.5
    key = query_key[:, QCOLS:].T * 0.5
    row = lax.broadcasted_iota(jnp.int32, (BLOCK, VCOLS), 0)

    def line(array, block, end):
        at = 2 * (block % 4) + end
        return array[at : at + 1, :]

    for number, block in enumerate(SLOTS):
        span = slice(number * BLOCK, (number + 1) * BLOCK)
        mid = values[span, :].astype(jnp.float32)
        opening = jnp.where((x_at + block) % NX == 0, line(far, block - 1, 1), line(near, block - 1, 1))
        before = jnp.where(even, opening, line(near, block, 1))
        closing = jnp.where((x_at + block) % NX == NX - 1, line(far, block + 1, 0), line(near, block + 1, 0))
        after = jnp.where(even, line(near, block, 0), closing)
        low = jnp.where(row == 0, before, pltpu.roll(mid, 1, 0))
        high = jnp.where(row == BLOCK - 1, after, pltpu.roll(mid, BLOCK - 1, 0))
        conv = taps[0:1, :] * low + taps[1:2, :] * mid + taps[2:3, :] * high
        conv_out[span, :] = conv.astype(jnp.bfloat16)
    state[...] = jnp.zeros_like(state)
    ones = jnp.ones((8, ROWS), jnp.bfloat16)
    for head in range(GROUP):
        feat = features(key[head * FEAT : (head + 1) * FEAT], 1.0).astype(jnp.bfloat16)
        start, stop = window_of(head)
        share = jnp.dot(feat, conv_out[:, start:stop], preferred_element_type=jnp.float32)
        state[:FROWS, start:stop] += jnp.where(head_mask(head, FROWS), share, 0.0)
        total = lax.dot_general(
            ones, feat, (((1,), (1,)), ((), ())), preferred_element_type=jnp.float32
        )
        state[FROWS + head : FROWS + head + 1, :FROWS] = total[0:1]
    if final:
        same = place[2] == 1
        keep_out[...] = jnp.where(same, state[...], other_state[...])
        give_out[...] = jnp.where(same, other_state[...], state[...]).astype(jnp.bfloat16)


def states_of(place, values, query_key, near, far, taps, other_state=None):
    final = other_state is not None
    vmem = pl.BlockSpec(memory_space=pltpu.VMEM)
    state = jax.ShapeDtypeStruct((MROWS, VCOLS), jnp.float32)
    ends = [state, jax.ShapeDtypeStruct((MROWS, VCOLS), jnp.bfloat16)] if final else [state]
    return pl.pallas_call(
        functools.partial(state_kernel, final),
        out_shape=[
            jax.ShapeDtypeStruct((ROWS, VCOLS), jnp.bfloat16),
            jax.ShapeDtypeStruct((QCOLS, ROWS), jnp.float32),
            *ends,
        ],
        in_specs=[pl.BlockSpec(memory_space=pltpu.SMEM)] + [vmem] * (6 if final else 5),
        out_specs=[vmem] * (2 + len(ends)),
        scratch_shapes=[pltpu.VMEM((MROWS, VCOLS), jnp.float32)] if final else [],
        compiler_params=pltpu.CompilerParams(vmem_limit_bytes=VMEM_SMALL),
        cost_estimate=pl.CostEstimate(flops=3 * 10**9, bytes_accessed=4 * 10**6, transcendentals=0),
    )(place, values, query_key, near, far, taps, *([other_state] if final else []))


def pack_kernel(start, query, key, value, *refs):
    outs, sems = refs[:-1], refs[-1]
    copies = []
    for index, out in enumerate(outs):
        count = out.shape[0]
        span = pl.ds(pl.multiple_of(start[index], 256), count)
        for kind, (ref, col, width) in enumerate(
            ((query, 0, QCOLS), (key, QCOLS, QCOLS), (value, 2 * QCOLS, VCOLS))
        ):
            copies.append(
                pltpu.make_async_copy(ref.at[span], out.at[:, pl.ds(col, width)], sems.at[index, kind])
            )
    for copy in copies:
        copy.start()
    for copy in copies:
        copy.wait()


def pack(weights, starts, counts):
    hbm = pl.BlockSpec(memory_space=pltpu.HBM)
    return pl.pallas_call(
        pack_kernel,
        out_shape=[jax.ShapeDtypeStruct((count, GCOLS), jnp.bfloat16) for count in counts],
        in_specs=[pl.BlockSpec(memory_space=pltpu.SMEM)] + [hbm] * 3,
        out_specs=[pl.BlockSpec(memory_space=pltpu.VMEM)] * len(counts),
        scratch_shapes=[pltpu.SemaphoreType.DMA((len(counts), 3))],
        compiler_params=pltpu.CompilerParams(vmem_limit_bytes=VMEM_LIMIT),
    )(jnp.stack(starts).astype(jnp.int32), *weights)


def split_kernel(place, keep, got, part_out, *lows):
    for step in range(NY):
        span = pl.ds(pl.multiple_of((place[0] + step) % NY * SPLIT, SPLIT), SPLIT)
        total = keep[span, :] + got[span, :].astype(jnp.float32)
        if step == 0:
            part_out[...] = total
        else:
            lows[step - 1][...] = total.astype(jnp.bfloat16)


def split(place, keep, got):
    vmem = pl.BlockSpec(memory_space=pltpu.VMEM)
    return pl.pallas_call(
        split_kernel,
        out_shape=[jax.ShapeDtypeStruct((SPLIT, VCOLS), jnp.float32)]
        + [jax.ShapeDtypeStruct((SPLIT, VCOLS), jnp.bfloat16)] * 3,
        in_specs=[pl.BlockSpec(memory_space=pltpu.SMEM), vmem, vmem],
        out_specs=[vmem] * 4,
        compiler_params=pltpu.CompilerParams(vmem_limit_bytes=VMEM_SMALL),
    )(place, keep, got)


def join_kernel(place, *refs):
    blocks, out = refs[:NX], refs[NX]
    width = blocks[0].shape[1]
    for step, block in enumerate(blocks):
        span = pl.ds(pl.multiple_of((place[0] + step) % NX * width, 128), width)
        out[:, span] = block[...]


def join(place, blocks):
    vmem = pl.BlockSpec(memory_space=pltpu.VMEM)
    rows, width = blocks[0].shape
    return pl.pallas_call(
        join_kernel,
        out_shape=jax.ShapeDtypeStruct((rows, NX * width), blocks[0].dtype),
        in_specs=[pl.BlockSpec(memory_space=pltpu.SMEM)] + [vmem] * NX,
        out_specs=vmem,
        compiler_params=pltpu.CompilerParams(vmem_limit_bytes=VMEM_SMALL),
    )(place, *blocks)


def attend_kernel(y_place, same, *refs):
    groups = (refs[0:3], refs[3:6])
    mine, theirs = refs[6:10], refs[10:14]
    outs, acc, states = refs[14:18], refs[18], refs[19]
    for step in range(NY):
        span = pl.ds(pl.multiple_of((y_place[0] + step) % NY * SPLIT, SPLIT), SPLIT)
        states[1 - same[0], span, :] = mine[step][...]
        states[same[0], span, :] = theirs[step][...]
    for number, (query, conv, gain) in enumerate(groups):
        state = states.at[number]
        acc[...] = jnp.zeros_like(acc)
        totals = state[FROWS : FROWS + 16, :FROWS]
        for head in range(GROUP):
            feat = features(query[head * FEAT : (head + 1) * FEAT, :], 2.0)
            denom = jnp.dot(totals, feat.astype(jnp.bfloat16), preferred_element_type=jnp.float32)
            scale = 1.0 / denom[head : head + 1, :]
            scaled = (feat * scale).astype(jnp.bfloat16)
            start, stop = window_of(head)
            part = state[:FROWS, start:stop]
            part = jnp.where(head_mask(head, FROWS), part, jnp.zeros_like(part))
            acc[:, start:stop] += lax.dot_general(
                scaled, part, (((0,), (0,)), ((), ())), preferred_element_type=jnp.float32
            )
        low = y_place[0] % 2
        spot = low if number == 0 else 1 - low
        span = pl.ds(pl.multiple_of(spot * VCOLS, VCOLS), VCOLS)
        for block, slot in enumerate(SLOTS):
            rows = slice(block * BLOCK, (block + 1) * BLOCK)
            mixed = acc[rows, :] * gain[3:4, :] + conv[rows, :].astype(jnp.float32)
            outs[slot][:, span] = mixed.astype(jnp.bfloat16)


def attend(y_place, same, groups, mine, theirs):
    vmem = pl.BlockSpec(memory_space=pltpu.VMEM)
    return pl.pallas_call(
        attend_kernel,
        out_shape=[jax.ShapeDtypeStruct((BLOCK, 2 * VCOLS), jnp.bfloat16)] * 4,
        in_specs=[pl.BlockSpec(memory_space=pltpu.SMEM)] * 2 + [vmem] * 14,
        out_specs=[vmem] * 4,
        scratch_shapes=[
            pltpu.VMEM((ROWS, VCOLS), jnp.float32),
            pltpu.VMEM((2, MROWS, VCOLS), jnp.bfloat16),
        ],
        compiler_params=pltpu.CompilerParams(vmem_limit_bytes=VMEM_SMALL),
    )(y_place, same, *[array for group in groups for array in group], *mine, *theirs)


def body(tokens, query_weight, key_weight, value_weight, conv_taps, norm_gain):
    tensor, seq = lax.axis_index("tensor"), lax.axis_index("seq")
    x_at, y_low = tensor // 2, tensor % 2
    core, z_odd = seq % 2, (seq // 2) % 2
    y_at = (seq // 16) * 2 + y_low
    rows = tokens.reshape(BLOCK, tokens.shape[-1])
    weights = (query_weight, key_weight, value_weight)
    half = rows.shape[1] // 2

    y_place = y_at.reshape(1).astype(jnp.int32)
    x_place = x_at.reshape(1).astype(jnp.int32)
    same = (core == y_low).astype(jnp.int32).reshape(1)
    part = BLOCK // 2

    def from_side(array):
        return receive(array, lambda x, y, z, c: (x, y + 2 * c - 1, z, c))

    def from_other(array):
        return receive(array, lambda x, y, z, c: (x, y ^ 1, z, c))

    one = from_x(rows, 1)
    three = from_x(rows, -1)
    two_top = from_x(one[:part], 1)
    two_low = from_x(three[part:], -1)

    base = core * half
    mixed_z = z_odd * 2 * PIECE
    packed = pack(weights, (base + mixed_z, base + mixed_z + PIECE, base + 4 * PIECE), (PIECE,) * 3)
    side = [from_side(array) for array in packed]
    side_z = [receive(array, lambda x, y, z, c: (x, y, z + 2 * c - 1, c)) for array in side[:2]]
    mine = [side[0], side[1], *side_z, side[2]]
    theirs = [from_core(array) for array in mine]
    flip = 2 * PIECE - mixed_z
    steps = jnp.stack([mixed_z, mixed_z + PIECE, flip, flip + PIECE, jnp.full_like(z_odd, 4 * PIECE)])
    offsets = jnp.concatenate([base + steps, (half - base) + steps]).astype(jnp.int32)
    small = jnp.concatenate([conv_taps, norm_gain[None]], axis=0)
    small_other = from_other(small)

    blocks = (rows, one, three, two_top, two_low)
    place = jnp.concatenate([x_place, y_low.reshape(1).astype(jnp.int32), same])
    values_own, query_key_own, edge_own = project(None, blocks, SLOTS, weights)
    values_other, query_key_other, edge_other = project(offsets, blocks, SLOTS, (*mine, *theirs))
    conv_other, query_other, state_other = states_of(
        place, values_other, query_key_other, from_other(edge_own), from_far(edge_own), small_other
    )
    conv_own, query_own, keep, give = states_of(
        place, values_own, query_key_own, from_other(edge_other), from_far(edge_other), small, state_other
    )

    total, *lows = split(y_place, keep, from_core(give))
    for step, low in zip((1, 2, 3), lows):
        total = total + from_y(low, -step).astype(jnp.float32)
    low = total.astype(jnp.bfloat16)
    for step in (1, -1, 2):
        total = total + from_z(low, step).astype(jnp.float32)
    low = total.astype(jnp.bfloat16)
    quarter = (total + from_z(low, 4).astype(jnp.float32)).astype(jnp.bfloat16)
    mine = [quarter] + [from_y(quarter, step) for step in (1, 2, 3)]
    theirs = [from_core(array) for array in mine]

    out = attend(
        y_place,
        same,
        ((query_own, conv_own, small), (query_other, conv_other, small_other)),
        mine,
        theirs,
    )
    result = join(x_place, [out[0], from_x(out[3], 1), from_x(out[2], 2), from_x(out[1], -1)])
    return result.reshape(tokens.shape)


def solution(mesh):
    return jax.shard_map(
        body,
        mesh=mesh,
        in_specs=(
            P("seq", "tensor", None),
            P(None, "tensor"),
            P(None, "tensor"),
            P(None, "tensor"),
            P(None, "tensor"),
            P("tensor"),
        ),
        out_specs=P("seq", "tensor", None),
        check_vma=False,
    )
```

```python
import functools

import jax
import jax.numpy as jnp
from jax import lax
from jax.experimental import pallas as pl
from jax.experimental.pallas import tpu as pltpu
from jax.sharding import PartitionSpec as P

FEAT = 16
HEAD_DIM = 80
GROUP = 8
NX, NY, NZ = 4, 4, 8
AXES = ("tensor", "seq")
PIECE = 512
PIECES = (PIECE,) * 10
VMEM_LIMIT = 58 * 1024 * 1024
VMEM_SMALL = 16 * 1024 * 1024
FROWS = 160
MROWS = 192
BLOCK = 128
ROWS = 4 * BLOCK
PARTS = (512, 512, 1024, 1024, 1024, 1024)
AHEAD = 2
ORDER_COST = 5 * 10**9
SLOTS = (0, 1, 3, 2)
VCOLS = GROUP * HEAD_DIM
QCOLS = GROUP * FEAT
GCOLS = VCOLS + 2 * QCOLS
SPLIT = MROWS // NY


def device_of(x, y, z, core):
    x, y, z = x % NX, y % NY, z % NZ
    tensor = x * 2 + (y & 1)
    seq = ((y >> 1) * NZ + z) * 2 + core
    return tensor * 32 + seq


def everywhere():
    return [
        (x, y, z, core)
        for x in range(NX)
        for y in range(NY)
        for z in range(NZ)
        for core in range(2)
    ]


def receive(array, source_of):
    pairs = [(device_of(*source_of(*place)), device_of(*place)) for place in everywhere()]
    return lax.ppermute(array, AXES, pairs)


def from_x(array, step):
    return receive(array, lambda x, y, z, c: (x + step, y, z, c))


def from_y(array, step):
    return receive(array, lambda x, y, z, c: (x, y + step, z, c))


def from_z(array, step):
    return receive(array, lambda x, y, z, c: (x, y, z + step, c))


def from_core(array):
    return receive(array, lambda x, y, z, c: (x, y, z, 1 - c))


def from_far(array):
    place = {}
    for x, y, z, core in everywhere():
        place[x, y & 1, ((y >> 1) * NZ + z) * 2 + core] = device_of(x, y, z, core)
    pairs = []
    for (x, odd, segment), target in place.items():
        source = place.get((x, 1 - odd, segment + (1 if odd else -1)))
        if source is not None:
            pairs.append((source, target))
    return lax.ppermute(array, AXES, pairs)


def features(scaled, off_weight):
    root = 0.5**0.5
    rows = scaled.shape[1]
    parts = [scaled, scaled * scaled * root]
    for step in range(1, FEAT // 2):
        turned = pltpu.roll(scaled, FEAT - step, 0)
        parts.append(scaled * turned * (root * off_weight))
    half = scaled[: FEAT // 2] * scaled[FEAT // 2 :] * (root * off_weight)
    parts.append(half)
    first = lax.broadcasted_iota(jnp.int32, (FEAT // 2, rows), 0) == 0
    parts.append(jnp.where(first, 1.0, 0.0).astype(jnp.float32))
    return jnp.concatenate(parts, axis=0)


def window_of(head):
    start = head * HEAD_DIM // 128 * 128
    stop = -(-(head + 1) * HEAD_DIM // 128) * 128
    return start, stop


def head_mask(head, rows):
    start, stop = window_of(head)
    lane = lax.broadcasted_iota(jnp.int32, (rows, stop - start), 1) + start
    return (lane >= head * HEAD_DIM) & (lane < (head + 1) * HEAD_DIM)


def project_kernel(counts, offsets, *refs):
    refs = list(refs)
    blocks = [refs.pop(0) for _ in counts]
    weights = [refs.pop(0) for _ in range(3)]
    pieces = [refs.pop(0) for _ in PIECES]
    refs.pop(0)
    value_outs, query_key_outs, edge_out = refs[0:2], refs[2:4], refs[4]
    xs, ws, acc, xsem, wsem, psem = refs[5:]
    stages, at = [], 0
    for index, count in enumerate(PARTS):
        copies, row = [], 0
        for number, (ref, rows) in enumerate(zip(blocks, counts)):
            copies.append(
                pltpu.make_async_copy(
                    ref.at[:, pl.ds(at, count)],
                    xs.at[pl.ds(row, rows), pl.ds(at, count)],
                    xsem.at[index, number],
                )
            )
            row += rows
        for kind, (col, width) in enumerate(((0, QCOLS), (QCOLS, QCOLS), (2 * QCOLS, VCOLS))):
            copies.append(
                pltpu.make_async_copy(
                    weights[kind].at[pl.ds(at, count)],
                    ws.at[0, pl.ds(at, count), pl.ds(col, width)],
                    wsem.at[index, kind],
                )
            )
        stages.append((0, copies, at, at, count))
        at += count
    at = 0
    for index, members in enumerate(((0, 1), (2, 3), (4,), (5, 6), (7, 8), (9,))):
        copies = [
            pltpu.make_async_copy(
                pieces[member], ws.at[1, pl.ds(at + step * PIECE, PIECE)], psem.at[member]
            )
            for step, member in enumerate(members)
        ]
        count = len(members) * PIECE
        stages.append((1, copies, at, pl.multiple_of(offsets[members[0]], PIECE), count))
        at += count

    for stage in stages[:AHEAD]:
        for copy in stage[1]:
            copy.start()
    for index, (group, copies, at, start, count) in enumerate(stages):
        for copy in copies:
            copy.wait()
        if index + AHEAD < len(stages):
            for copy in stages[index + AHEAD][1]:
                copy.start()
        part = jnp.dot(
            xs[:, pl.ds(start, count)], ws[group, at : at + count, :], preferred_element_type=jnp.float32
        )
        if at == 0:
            acc[...] = part
        else:
            acc[...] += part
        if index + 1 < len(stages) and stages[index + 1][0] == group:
            continue
        query_key_outs[group][...] = acc[:, : 2 * QCOLS]
        value_outs[group][...] = acc[:, 2 * QCOLS :].astype(jnp.bfloat16)
        for block, slot in enumerate(SLOTS):
            for end, row in ((0, block * BLOCK), (1, block * BLOCK + BLOCK - 1)):
                line = acc[row : row + 1, 2 * QCOLS :].astype(jnp.bfloat16).astype(jnp.float32)
                edge_out[8 * group + 2 * slot + end : 8 * group + 2 * slot + end + 1, :] = line


def project(offsets, blocks, weights, pieces, after):
    counts = tuple(block.shape[0] for block in blocks)
    depth = blocks[0].shape[1]
    hbm = pl.BlockSpec(memory_space=pltpu.HBM)
    vmem = pl.BlockSpec(memory_space=pltpu.VMEM)
    return pl.pallas_call(
        functools.partial(project_kernel, counts),
        out_shape=[jax.ShapeDtypeStruct((ROWS, VCOLS), jnp.bfloat16)] * 2
        + [jax.ShapeDtypeStruct((ROWS, 2 * QCOLS), jnp.float32)] * 2
        + [jax.ShapeDtypeStruct((16, VCOLS), jnp.float32)],
        in_specs=[pl.BlockSpec(memory_space=pltpu.SMEM)] + [hbm] * (len(blocks) + 4 + len(pieces)),
        out_specs=[vmem] * 5,
        scratch_shapes=[
            pltpu.VMEM((ROWS, depth), jnp.bfloat16),
            pltpu.VMEM((2, depth, GCOLS), jnp.bfloat16),
            pltpu.VMEM((ROWS, GCOLS), jnp.float32),
            pltpu.SemaphoreType.DMA((len(PARTS), len(blocks))),
            pltpu.SemaphoreType.DMA((len(PARTS), 3)),
            pltpu.SemaphoreType.DMA((len(pieces),)),
        ],
        compiler_params=pltpu.CompilerParams(vmem_limit_bytes=VMEM_LIMIT),
        cost_estimate=pl.CostEstimate(
            flops=4 * ROWS * depth * GCOLS, bytes_accessed=2 * depth * (ROWS + 2 * GCOLS), transcendentals=0
        ),
    )(offsets, *blocks, *weights, *pieces, after)


def order_kernel(top, low, out, scratch, sems):
    copies = [
        pltpu.make_async_copy(ref.at[pl.ds(0, 16), pl.ds(0, 128)], scratch.at[number], sems.at[number])
        for number, ref in enumerate((top, low))
    ]
    for copy in copies:
        copy.start()
    for copy in copies:
        copy.wait()
    out[...] = scratch[0] + scratch[1]


def arrived(top, low):
    hbm = pl.BlockSpec(memory_space=pltpu.HBM)
    return pl.pallas_call(
        order_kernel,
        out_shape=jax.ShapeDtypeStruct((16, 128), top.dtype),
        in_specs=[hbm, hbm],
        out_specs=pl.BlockSpec(memory_space=pltpu.VMEM),
        scratch_shapes=[pltpu.VMEM((2, 16, 128), top.dtype), pltpu.SemaphoreType.DMA((2,))],
        compiler_params=pltpu.CompilerParams(vmem_limit_bytes=VMEM_LIMIT),
        cost_estimate=pl.CostEstimate(flops=ORDER_COST, bytes_accessed=15 * 10**6, transcendentals=0),
    )(top, low)


def state_kernel(place, *refs):
    values, query_keys, (near, far), taps = refs[0:2], refs[2:4], refs[4:6], refs[6:8]
    convs, queries, (keep_out, give_out), states = refs[8:10], refs[10:12], refs[12:14], refs[14]
    x_at, even = place[0], place[1] == 0
    row = lax.broadcasted_iota(jnp.int32, (BLOCK, VCOLS), 0)
    ones = jnp.ones((8, ROWS), jnp.bfloat16)
    states[...] = jnp.zeros_like(states)
    for group in range(2):
        state, conv_out = states.at[group], convs[group]
        queries[group][...] = query_keys[group][:, :QCOLS].T * 0.5
        key = query_keys[group][:, QCOLS:].T * 0.5

        def line(ref, block, end):
            at = 8 * (1 - group) + 2 * (block % 4) + end
            return ref[at : at + 1, :]

        for number, block in enumerate(SLOTS):
            span = slice(number * BLOCK, (number + 1) * BLOCK)
            mid = values[group][span, :].astype(jnp.float32)
            opening = jnp.where((x_at + block) % NX == 0, line(far, block - 1, 1), line(near, block - 1, 1))
            before = jnp.where(even, opening, line(near, block, 1))
            closing = jnp.where((x_at + block) % NX == NX - 1, line(far, block + 1, 0), line(near, block + 1, 0))
            after = jnp.where(even, line(near, block, 0), closing)
            low = jnp.where(row == 0, before, pltpu.roll(mid, 1, 0))
            high = jnp.where(row == BLOCK - 1, after, pltpu.roll(mid, BLOCK - 1, 0))
            tap = taps[group]
            conv = tap[0:1, :] * low + tap[1:2, :] * mid + tap[2:3, :] * high
            conv_out[span, :] = conv.astype(jnp.bfloat16)
        for head in range(GROUP):
            feat = features(key[head * FEAT : (head + 1) * FEAT], 1.0).astype(jnp.bfloat16)
            start, stop = window_of(head)
            share = jnp.dot(feat, conv_out[:, start:stop], preferred_element_type=jnp.float32)
            state[:FROWS, start:stop] += jnp.where(head_mask(head, FROWS), share, 0.0)
            total = lax.dot_general(
                ones, feat, (((1,), (1,)), ((), ())), preferred_element_type=jnp.float32
            )
            state[FROWS + head : FROWS + head + 1, :FROWS] = total[0:1]
    same = place[2] == 1
    keep_out[...] = jnp.where(same, states[0], states[1])
    give_out[...] = jnp.where(same, states[1], states[0]).astype(jnp.bfloat16)


def states_of(place, values, query_keys, near, far, taps):
    vmem = pl.BlockSpec(memory_space=pltpu.VMEM)
    return pl.pallas_call(
        state_kernel,
        out_shape=[jax.ShapeDtypeStruct((ROWS, VCOLS), jnp.bfloat16)] * 2
        + [jax.ShapeDtypeStruct((QCOLS, ROWS), jnp.float32)] * 2
        + [
            jax.ShapeDtypeStruct((MROWS, VCOLS), jnp.float32),
            jax.ShapeDtypeStruct((MROWS, VCOLS), jnp.bfloat16),
        ],
        in_specs=[pl.BlockSpec(memory_space=pltpu.SMEM)] + [vmem] * 8,
        out_specs=[vmem] * 6,
        scratch_shapes=[pltpu.VMEM((2, MROWS, VCOLS), jnp.float32)],
        compiler_params=pltpu.CompilerParams(vmem_limit_bytes=VMEM_SMALL),
        cost_estimate=pl.CostEstimate(flops=6 * 10**9, bytes_accessed=8 * 10**6, transcendentals=0),
    )(place, *values, *query_keys, near, far, *taps)


def pack_kernel(start, query, key, value, *refs):
    outs, sems = refs[:-1], refs[-1]
    copies = []
    for index, out in enumerate(outs):
        count = out.shape[0]
        span = pl.ds(pl.multiple_of(start[index], 256), count)
        for kind, (ref, col, width) in enumerate(
            ((query, 0, QCOLS), (key, QCOLS, QCOLS), (value, 2 * QCOLS, VCOLS))
        ):
            copies.append(
                pltpu.make_async_copy(ref.at[span], out.at[:, pl.ds(col, width)], sems.at[index, kind])
            )
    for copy in copies:
        copy.start()
    for copy in copies:
        copy.wait()


def pack(weights, starts, counts):
    hbm = pl.BlockSpec(memory_space=pltpu.HBM)
    return pl.pallas_call(
        pack_kernel,
        out_shape=[jax.ShapeDtypeStruct((count, GCOLS), jnp.bfloat16) for count in counts],
        in_specs=[pl.BlockSpec(memory_space=pltpu.SMEM)] + [hbm] * 3,
        out_specs=[pl.BlockSpec(memory_space=pltpu.VMEM)] * len(counts),
        scratch_shapes=[pltpu.SemaphoreType.DMA((len(counts), 3))],
        compiler_params=pltpu.CompilerParams(vmem_limit_bytes=VMEM_LIMIT),
    )(jnp.stack(starts).astype(jnp.int32), *weights)


def split_kernel(place, keep, got, part_out, *lows):
    for step in range(NY):
        span = pl.ds(pl.multiple_of((place[0] + step) % NY * SPLIT, SPLIT), SPLIT)
        total = keep[span, :] + got[span, :].astype(jnp.float32)
        if step == 0:
            part_out[...] = total
        else:
            lows[step - 1][...] = total.astype(jnp.bfloat16)


def split(place, keep, got):
    vmem = pl.BlockSpec(memory_space=pltpu.VMEM)
    return pl.pallas_call(
        split_kernel,
        out_shape=[jax.ShapeDtypeStruct((SPLIT, VCOLS), jnp.float32)]
        + [jax.ShapeDtypeStruct((SPLIT, VCOLS), jnp.bfloat16)] * 3,
        in_specs=[pl.BlockSpec(memory_space=pltpu.SMEM), vmem, vmem],
        out_specs=[vmem] * 4,
        compiler_params=pltpu.CompilerParams(vmem_limit_bytes=VMEM_SMALL),
    )(place, keep, got)


def join_kernel(place, *refs):
    blocks, out = refs[:NX], refs[NX]
    width = blocks[0].shape[1]
    for step, block in enumerate(blocks):
        span = pl.ds(pl.multiple_of((place[0] + step) % NX * width, 128), width)
        out[:, span] = block[...]


def join(place, blocks):
    vmem = pl.BlockSpec(memory_space=pltpu.VMEM)
    rows, width = blocks[0].shape
    return pl.pallas_call(
        join_kernel,
        out_shape=jax.ShapeDtypeStruct((rows, NX * width), blocks[0].dtype),
        in_specs=[pl.BlockSpec(memory_space=pltpu.SMEM)] + [vmem] * NX,
        out_specs=vmem,
        compiler_params=pltpu.CompilerParams(vmem_limit_bytes=VMEM_SMALL),
    )(place, *blocks)


def attend_kernel(y_place, same, *refs):
    groups = (refs[0:3], refs[3:6])
    mine, theirs = refs[6:10], refs[10:14]
    outs, acc, states = refs[14:18], refs[18], refs[19]
    for step in range(NY):
        span = pl.ds(pl.multiple_of((y_place[0] + step) % NY * SPLIT, SPLIT), SPLIT)
        states[1 - same[0], span, :] = mine[step][...]
        states[same[0], span, :] = theirs[step][...]
    for number, (query, conv, gain) in enumerate(groups):
        state = states.at[number]
        acc[...] = jnp.zeros_like(acc)
        totals = state[FROWS : FROWS + 16, :FROWS]
        for head in range(GROUP):
            feat = features(query[head * FEAT : (head + 1) * FEAT, :], 2.0)
            denom = jnp.dot(totals, feat.astype(jnp.bfloat16), preferred_element_type=jnp.float32)
            scale = 1.0 / denom[head : head + 1, :]
            scaled = (feat * scale).astype(jnp.bfloat16)
            start, stop = window_of(head)
            part = state[:FROWS, start:stop]
            part = jnp.where(head_mask(head, FROWS), part, jnp.zeros_like(part))
            acc[:, start:stop] += lax.dot_general(
                scaled, part, (((0,), (0,)), ((), ())), preferred_element_type=jnp.float32
            )
        low = y_place[0] % 2
        spot = low if number == 0 else 1 - low
        span = pl.ds(pl.multiple_of(spot * VCOLS, VCOLS), VCOLS)
        for block, slot in enumerate(SLOTS):
            rows = slice(block * BLOCK, (block + 1) * BLOCK)
            mixed = acc[rows, :] * gain[3:4, :] + conv[rows, :].astype(jnp.float32)
            outs[slot][:, span] = mixed.astype(jnp.bfloat16)


def attend(y_place, same, groups, mine, theirs):
    vmem = pl.BlockSpec(memory_space=pltpu.VMEM)
    return pl.pallas_call(
        attend_kernel,
        out_shape=[jax.ShapeDtypeStruct((BLOCK, 2 * VCOLS), jnp.bfloat16)] * 4,
        in_specs=[pl.BlockSpec(memory_space=pltpu.SMEM)] * 2 + [vmem] * 14,
        out_specs=[vmem] * 4,
        scratch_shapes=[
            pltpu.VMEM((ROWS, VCOLS), jnp.float32),
            pltpu.VMEM((2, MROWS, VCOLS), jnp.bfloat16),
        ],
        compiler_params=pltpu.CompilerParams(vmem_limit_bytes=VMEM_SMALL),
    )(y_place, same, *[array for group in groups for array in group], *mine, *theirs)


def body(tokens, query_weight, key_weight, value_weight, conv_taps, norm_gain):
    tensor, seq = lax.axis_index("tensor"), lax.axis_index("seq")
    x_at, y_low = tensor // 2, tensor % 2
    core, z_odd = seq % 2, (seq // 2) % 2
    y_at = (seq // 16) * 2 + y_low
    rows = tokens.reshape(BLOCK, tokens.shape[-1])
    weights = (query_weight, key_weight, value_weight)
    half = rows.shape[1] // 2

    y_place = y_at.reshape(1).astype(jnp.int32)
    x_place = x_at.reshape(1).astype(jnp.int32)
    same = (core == y_low).astype(jnp.int32).reshape(1)
    part = BLOCK // 2

    def from_side(array):
        return receive(array, lambda x, y, z, c: (x, y + 2 * c - 1, z, c))

    def from_other(array):
        return receive(array, lambda x, y, z, c: (x, y ^ 1, z, c))

    one = from_x(rows, 1)
    three = from_x(rows, -1)
    two_top = from_x(one[:part], 1)
    two_low = from_x(three[part:], -1)

    base = core * half
    mixed_z = z_odd * 2 * PIECE
    packed = pack(weights, (base + mixed_z, base + mixed_z + PIECE, base + 4 * PIECE), (PIECE,) * 3)
    side = [from_side(array) for array in packed]
    side_z = [receive(array, lambda x, y, z, c: (x, y, z + 2 * c - 1, c)) for array in side[:2]]
    mine = [side[0], side[1], *side_z, side[2]]
    theirs = [from_core(array) for array in mine]
    flip = 2 * PIECE - mixed_z
    steps = jnp.stack([mixed_z, mixed_z + PIECE, flip, flip + PIECE, jnp.full_like(z_odd, 4 * PIECE)])
    offsets = jnp.concatenate([base + steps, (half - base) + steps]).astype(jnp.int32)
    small = jnp.concatenate([conv_taps, norm_gain[None]], axis=0)
    small_other = from_other(small)

    blocks = (rows, one, three, two_top, two_low)
    place = jnp.concatenate([x_place, y_low.reshape(1).astype(jnp.int32), same])
    value_own, value_other, query_key_own, query_key_other, edge = project(
        offsets, blocks, weights, (*mine, *theirs), arrived(two_top, two_low)
    )
    conv_own, conv_other, query_own, query_other, keep, give = states_of(
        place,
        (value_own, value_other),
        (query_key_own, query_key_other),
        from_other(edge),
        from_far(edge),
        (small, small_other),
    )

    total, *lows = split(y_place, keep, from_core(give))
    for step, low in zip((1, 2, 3), lows):
        total = total + from_y(low, -step).astype(jnp.float32)
    low = total.astype(jnp.bfloat16)
    for step in (1, -1, 2):
        total = total + from_z(low, step).astype(jnp.float32)
    low = total.astype(jnp.bfloat16)
    quarter = (total + from_z(low, 4).astype(jnp.float32)).astype(jnp.bfloat16)
    mine = [quarter] + [from_y(quarter, step) for step in (1, 2, 3)]
    theirs = [from_core(array) for array in mine]

    out = attend(
        y_place,
        same,
        ((query_own, conv_own, small), (query_other, conv_other, small_other)),
        mine,
        theirs,
    )
    result = join(x_place, [out[0], from_x(out[3], 1), from_x(out[2], 2), from_x(out[1], -1)])
    return result.reshape(tokens.shape)


def solution(mesh):
    return jax.shard_map(
        body,
        mesh=mesh,
        in_specs=(
            P("seq", "tensor", None),
            P(None, "tensor"),
            P(None, "tensor"),
            P(None, "tensor"),
            P(None, "tensor"),
            P("tensor"),
        ),
        out_specs=P("seq", "tensor", None),
        check_vma=False,
    )
```

```python
import functools

import jax
import jax.numpy as jnp
from jax import lax
from jax.experimental import pallas as pl
from jax.experimental.pallas import tpu as pltpu
from jax.sharding import PartitionSpec as P

FEAT = 16
HEAD_DIM = 80
GROUP = 8
NX, NY, NZ = 4, 4, 8
AXES = ("tensor", "seq")
PIECE = 512
PIECES = (PIECE,) * 10
VMEM_LIMIT = 58 * 1024 * 1024
VMEM_SMALL = 16 * 1024 * 1024
FROWS = 160
MROWS = 192
BLOCK = 128
ROWS = 4 * BLOCK
PARTS = ((4,), (0, 1), (2, 3), (5, 6), (7, 8), (9,))
AHEAD = 2
ORDER_COST = 5 * 10**9
SLOTS = (0, 1, 3, 2)
VCOLS = GROUP * HEAD_DIM
QCOLS = GROUP * FEAT
GCOLS = VCOLS + 2 * QCOLS
SPLIT = MROWS // NY


def device_of(x, y, z, core):
    x, y, z = x % NX, y % NY, z % NZ
    tensor = x * 2 + (y & 1)
    seq = ((y >> 1) * NZ + z) * 2 + core
    return tensor * 32 + seq


def everywhere():
    return [
        (x, y, z, core)
        for x in range(NX)
        for y in range(NY)
        for z in range(NZ)
        for core in range(2)
    ]


def receive(array, source_of):
    pairs = [(device_of(*source_of(*place)), device_of(*place)) for place in everywhere()]
    return lax.ppermute(array, AXES, pairs)


def from_x(array, step):
    return receive(array, lambda x, y, z, c: (x + step, y, z, c))


def from_y(array, step):
    return receive(array, lambda x, y, z, c: (x, y + step, z, c))


def from_z(array, step):
    return receive(array, lambda x, y, z, c: (x, y, z + step, c))


def from_core(array):
    return receive(array, lambda x, y, z, c: (x, y, z, 1 - c))


def from_far(array):
    place = {}
    for x, y, z, core in everywhere():
        place[x, y & 1, ((y >> 1) * NZ + z) * 2 + core] = device_of(x, y, z, core)
    pairs = []
    for (x, odd, segment), target in place.items():
        source = place.get((x, 1 - odd, segment + (1 if odd else -1)))
        if source is not None:
            pairs.append((source, target))
    return lax.ppermute(array, AXES, pairs)


def features(scaled, off_weight):
    root = 0.5**0.5
    rows = scaled.shape[1]
    parts = [scaled, scaled * scaled * root]
    for step in range(1, FEAT // 2):
        turned = pltpu.roll(scaled, FEAT - step, 0)
        parts.append(scaled * turned * (root * off_weight))
    half = scaled[: FEAT // 2] * scaled[FEAT // 2 :] * (root * off_weight)
    parts.append(half)
    first = lax.broadcasted_iota(jnp.int32, (FEAT // 2, rows), 0) == 0
    parts.append(jnp.where(first, 1.0, 0.0).astype(jnp.float32))
    return jnp.concatenate(parts, axis=0)


def window_of(head):
    start = head * HEAD_DIM // 128 * 128
    stop = -(-(head + 1) * HEAD_DIM // 128) * 128
    return start, stop


def head_mask(head, rows):
    start, stop = window_of(head)
    lane = lax.broadcasted_iota(jnp.int32, (rows, stop - start), 1) + start
    return (lane >= head * HEAD_DIM) & (lane < (head + 1) * HEAD_DIM)


def project_kernel(counts, offsets, *refs):
    refs = list(refs)
    blocks = [refs.pop(0) for _ in counts]
    weights = [refs.pop(0) for _ in range(3)]
    pieces = [refs.pop(0) for _ in PIECES]
    refs.pop(0)
    value_outs, query_key_outs, edge_out = refs[0:2], refs[2:4], refs[4]
    xs, ws, acc, xsem, wsem, psem = refs[5:]
    stages, at = [], 0
    for index, members in enumerate(PARTS):
        count = len(members) * PIECE
        start = pl.multiple_of(offsets[members[0]], PIECE)
        copies, row = [], 0
        for number, (ref, rows) in enumerate(zip(blocks, counts)):
            copies.append(
                pltpu.make_async_copy(
                    ref.at[:, pl.ds(start, count)],
                    xs.at[pl.ds(row, rows), pl.ds(at, count)],
                    xsem.at[index, number],
                )
            )
            row += rows
        for kind, (col, width) in enumerate(((0, QCOLS), (QCOLS, QCOLS), (2 * QCOLS, VCOLS))):
            copies.append(
                pltpu.make_async_copy(
                    weights[kind].at[pl.ds(start, count)],
                    ws.at[pl.ds(at, count), pl.ds(col, width)],
                    wsem.at[index, kind],
                )
            )
        for step, member in enumerate(members):
            copies.append(
                pltpu.make_async_copy(
                    pieces[member],
                    ws.at[pl.ds(at + step * PIECE, PIECE), pl.ds(GCOLS, GCOLS)],
                    psem.at[member],
                )
            )
        stages.append((copies, at, count))
        at += count
    for copies, _, _ in stages[:AHEAD]:
        for copy in copies:
            copy.start()
    for index, (copies, at, count) in enumerate(stages):
        for copy in copies:
            copy.wait()
        if index + AHEAD < len(stages):
            for copy in stages[index + AHEAD][0]:
                copy.start()
        span = slice(at, at + count)
        part = jnp.dot(xs[:, span], ws[span, :], preferred_element_type=jnp.float32)
        if index == 0:
            acc[...] = part
        else:
            acc[...] += part
    for group in range(2):
        low = group * GCOLS
        query_key_outs[group][...] = acc[:, low : low + 2 * QCOLS]
        value_outs[group][...] = acc[:, low + 2 * QCOLS : low + GCOLS].astype(jnp.bfloat16)
        for block, slot in enumerate(SLOTS):
            for end, row in ((0, block * BLOCK), (1, block * BLOCK + BLOCK - 1)):
                line = acc[row : row + 1, low + 2 * QCOLS : low + GCOLS]
                at = 8 * group + 2 * slot + end
                edge_out[at : at + 1, :] = line.astype(jnp.bfloat16).astype(jnp.float32)


def project(offsets, blocks, weights, pieces, after):
    counts = tuple(block.shape[0] for block in blocks)
    depth = blocks[0].shape[1]
    hbm = pl.BlockSpec(memory_space=pltpu.HBM)
    vmem = pl.BlockSpec(memory_space=pltpu.VMEM)
    return pl.pallas_call(
        functools.partial(project_kernel, counts),
        out_shape=[jax.ShapeDtypeStruct((ROWS, VCOLS), jnp.bfloat16)] * 2
        + [jax.ShapeDtypeStruct((ROWS, 2 * QCOLS), jnp.float32)] * 2
        + [jax.ShapeDtypeStruct((16, VCOLS), jnp.float32)],
        in_specs=[pl.BlockSpec(memory_space=pltpu.SMEM)] + [hbm] * (len(blocks) + 4 + len(pieces)),
        out_specs=[vmem] * 5,
        scratch_shapes=[
            pltpu.VMEM((ROWS, depth), jnp.bfloat16),
            pltpu.VMEM((depth, 2 * GCOLS), jnp.bfloat16),
            pltpu.VMEM((ROWS, 2 * GCOLS), jnp.float32),
            pltpu.SemaphoreType.DMA((len(PARTS), len(blocks))),
            pltpu.SemaphoreType.DMA((len(PARTS), 3)),
            pltpu.SemaphoreType.DMA((len(pieces),)),
        ],
        compiler_params=pltpu.CompilerParams(vmem_limit_bytes=VMEM_LIMIT),
        cost_estimate=pl.CostEstimate(
            flops=4 * ROWS * depth * GCOLS, bytes_accessed=2 * depth * (ROWS + 2 * GCOLS), transcendentals=0
        ),
    )(offsets, *blocks, *weights, *pieces, after)


def order_kernel(top, low, out, scratch, sems):
    copies = [
        pltpu.make_async_copy(ref.at[pl.ds(0, 16), pl.ds(0, 128)], scratch.at[number], sems.at[number])
        for number, ref in enumerate((top, low))
    ]
    for copy in copies:
        copy.start()
    for copy in copies:
        copy.wait()
    out[...] = scratch[0] + scratch[1]


def arrived(top, low):
    hbm = pl.BlockSpec(memory_space=pltpu.HBM)
    return pl.pallas_call(
        order_kernel,
        out_shape=jax.ShapeDtypeStruct((16, 128), top.dtype),
        in_specs=[hbm, hbm],
        out_specs=pl.BlockSpec(memory_space=pltpu.VMEM),
        scratch_shapes=[pltpu.VMEM((2, 16, 128), top.dtype), pltpu.SemaphoreType.DMA((2,))],
        compiler_params=pltpu.CompilerParams(vmem_limit_bytes=VMEM_LIMIT),
        cost_estimate=pl.CostEstimate(flops=ORDER_COST, bytes_accessed=15 * 10**6, transcendentals=0),
    )(top, low)


def prepare_kernel(*refs):
    values, query_keys, taps = refs[0:2], refs[2:4], refs[4:6]
    convs, queries, feats, rim = refs[6:8], refs[8:10], refs[10:12], refs[12]
    row = lax.broadcasted_iota(jnp.int32, (BLOCK, VCOLS), 0)
    for group in range(2):
        queries[group][...] = query_keys[group][:, :QCOLS].T * 0.5
        key = query_keys[group][:, QCOLS:].T * 0.5
        for head in range(GROUP):
            feat = features(key[head * FEAT : (head + 1) * FEAT], 1.0)
            feats[group][head * FROWS : (head + 1) * FROWS, :] = feat.astype(jnp.bfloat16)
        tap = taps[group]
        for number, block in enumerate(SLOTS):
            span = slice(number * BLOCK, (number + 1) * BLOCK)
            mid = values[group][span, :].astype(jnp.float32)
            low = jnp.where(row == 0, 0.0, pltpu.roll(mid, 1, 0))
            high = jnp.where(row == BLOCK - 1, 0.0, pltpu.roll(mid, BLOCK - 1, 0))
            conv = tap[0:1, :] * low + tap[1:2, :] * mid + tap[2:3, :] * high
            convs[group][span, :] = conv.astype(jnp.bfloat16)
            at = 8 * group + 2 * block
            rim[at : at + 1, :] = conv[0:1]
            rim[at + 1 : at + 2, :] = conv[BLOCK - 1 : BLOCK]


def prepare(values, query_keys, taps):
    vmem = pl.BlockSpec(memory_space=pltpu.VMEM)
    return pl.pallas_call(
        prepare_kernel,
        out_shape=[jax.ShapeDtypeStruct((ROWS, VCOLS), jnp.bfloat16)] * 2
        + [jax.ShapeDtypeStruct((QCOLS, ROWS), jnp.float32)] * 2
        + [jax.ShapeDtypeStruct((GROUP * FROWS, ROWS), jnp.bfloat16)] * 2
        + [jax.ShapeDtypeStruct((16, VCOLS), jnp.float32)],
        in_specs=[vmem] * 6,
        out_specs=[vmem] * 7,
        compiler_params=pltpu.CompilerParams(vmem_limit_bytes=VMEM_SMALL),
        cost_estimate=pl.CostEstimate(flops=3 * 10**9, bytes_accessed=8 * 10**6, transcendentals=0),
    )(*values, *query_keys, *taps)


def state_kernel(place, *refs):
    inner, feats, (rim, near, far), taps = refs[0:2], refs[2:4], refs[4:7], refs[7:9]
    convs, (keep_out, give_out), states = refs[9:11], refs[11:13], refs[13]
    x_at, even = place[0], place[1] == 0
    row = lax.broadcasted_iota(jnp.int32, (BLOCK, VCOLS), 0)
    ones = jnp.ones((8, ROWS), jnp.bfloat16)
    states[...] = jnp.zeros_like(states)
    for group in range(2):
        state, conv_out, tap = states.at[group], convs[group], taps[group]

        def line(ref, block, end):
            at = 8 * (1 - group) + 2 * (block % 4) + end
            return ref[at : at + 1, :]

        for number, block in enumerate(SLOTS):
            span = slice(number * BLOCK, (number + 1) * BLOCK)
            at = 8 * group + 2 * block
            opening = jnp.where((x_at + block) % NX == 0, line(far, block - 1, 1), line(near, block - 1, 1))
            before = jnp.where(even, opening, line(near, block, 1))
            closing = jnp.where((x_at + block) % NX == NX - 1, line(far, block + 1, 0), line(near, block + 1, 0))
            after = jnp.where(even, line(near, block, 0), closing)
            first = rim[at : at + 1, :] + tap[0:1, :] * before
            last = rim[at + 1 : at + 2, :] + tap[2:3, :] * after
            conv = inner[group][span, :].astype(jnp.float32)
            conv = jnp.where(row == 0, first, jnp.where(row == BLOCK - 1, last, conv))
            conv_out[span, :] = conv.astype(jnp.bfloat16)
        for head in range(GROUP):
            feat = feats[group][head * FROWS : (head + 1) * FROWS, :]
            start, stop = window_of(head)
            share = jnp.dot(feat, conv_out[:, start:stop], preferred_element_type=jnp.float32)
            state[:FROWS, start:stop] += jnp.where(head_mask(head, FROWS), share, 0.0)
            total = lax.dot_general(
                ones, feat, (((1,), (1,)), ((), ())), preferred_element_type=jnp.float32
            )
            state[FROWS + head : FROWS + head + 1, :FROWS] = total[0:1]
    same = place[2] == 1
    keep_out[...] = jnp.where(same, states[0], states[1])
    give_out[...] = jnp.where(same, states[1], states[0]).astype(jnp.bfloat16)


def states_of(place, inner, feats, rim, near, far, taps):
    vmem = pl.BlockSpec(memory_space=pltpu.VMEM)
    return pl.pallas_call(
        state_kernel,
        out_shape=[jax.ShapeDtypeStruct((ROWS, VCOLS), jnp.bfloat16)] * 2
        + [
            jax.ShapeDtypeStruct((MROWS, VCOLS), jnp.float32),
            jax.ShapeDtypeStruct((MROWS, VCOLS), jnp.bfloat16),
        ],
        in_specs=[pl.BlockSpec(memory_space=pltpu.SMEM)] + [vmem] * 9,
        out_specs=[vmem] * 4,
        scratch_shapes=[pltpu.VMEM((2, MROWS, VCOLS), jnp.float32)],
        compiler_params=pltpu.CompilerParams(vmem_limit_bytes=VMEM_SMALL),
        cost_estimate=pl.CostEstimate(flops=3 * 10**9, bytes_accessed=8 * 10**6, transcendentals=0),
    )(place, *inner, *feats, rim, near, far, *taps)


def pack_kernel(start, query, key, value, *refs):
    outs, sems = refs[:-1], refs[-1]
    copies = []
    for index, out in enumerate(outs):
        count = out.shape[0]
        span = pl.ds(pl.multiple_of(start[index], 256), count)
        for kind, (ref, col, width) in enumerate(
            ((query, 0, QCOLS), (key, QCOLS, QCOLS), (value, 2 * QCOLS, VCOLS))
        ):
            copies.append(
                pltpu.make_async_copy(ref.at[span], out.at[:, pl.ds(col, width)], sems.at[index, kind])
            )
    for copy in copies:
        copy.start()
    for copy in copies:
        copy.wait()


def pack(weights, starts, counts):
    hbm = pl.BlockSpec(memory_space=pltpu.HBM)
    return pl.pallas_call(
        pack_kernel,
        out_shape=[jax.ShapeDtypeStruct((count, GCOLS), jnp.bfloat16) for count in counts],
        in_specs=[pl.BlockSpec(memory_space=pltpu.SMEM)] + [hbm] * 3,
        out_specs=[pl.BlockSpec(memory_space=pltpu.VMEM)] * len(counts),
        scratch_shapes=[pltpu.SemaphoreType.DMA((len(counts), 3))],
        compiler_params=pltpu.CompilerParams(vmem_limit_bytes=VMEM_LIMIT),
    )(jnp.stack(starts).astype(jnp.int32), *weights)


def split_kernel(place, keep, got, part_out, *lows):
    for step in range(NY):
        span = pl.ds(pl.multiple_of((place[0] + step) % NY * SPLIT, SPLIT), SPLIT)
        total = keep[span, :] + got[span, :].astype(jnp.float32)
        if step == 0:
            part_out[...] = total
        else:
            lows[step - 1][...] = total.astype(jnp.bfloat16)


def split(place, keep, got):
    vmem = pl.BlockSpec(memory_space=pltpu.VMEM)
    return pl.pallas_call(
        split_kernel,
        out_shape=[jax.ShapeDtypeStruct((SPLIT, VCOLS), jnp.float32)]
        + [jax.ShapeDtypeStruct((SPLIT, VCOLS), jnp.bfloat16)] * 3,
        in_specs=[pl.BlockSpec(memory_space=pltpu.SMEM), vmem, vmem],
        out_specs=[vmem] * 4,
        compiler_params=pltpu.CompilerParams(vmem_limit_bytes=VMEM_SMALL),
    )(place, keep, got)


def join_kernel(place, *refs):
    blocks, out = refs[:NX], refs[NX]
    width = blocks[0].shape[1]
    for step, block in enumerate(blocks):
        span = pl.ds(pl.multiple_of((place[0] + step) % NX * width, 128), width)
        out[:, span] = block[...]


def join(place, blocks):
    vmem = pl.BlockSpec(memory_space=pltpu.VMEM)
    rows, width = blocks[0].shape
    return pl.pallas_call(
        join_kernel,
        out_shape=jax.ShapeDtypeStruct((rows, NX * width), blocks[0].dtype),
        in_specs=[pl.BlockSpec(memory_space=pltpu.SMEM)] + [vmem] * NX,
        out_specs=vmem,
        compiler_params=pltpu.CompilerParams(vmem_limit_bytes=VMEM_SMALL),
    )(place, *blocks)


def attend_kernel(y_place, same, *refs):
    groups = (refs[0:3], refs[3:6])
    mine, theirs = refs[6:10], refs[10:14]
    outs, acc, states = refs[14:18], refs[18], refs[19]
    for step in range(NY):
        span = pl.ds(pl.multiple_of((y_place[0] + step) % NY * SPLIT, SPLIT), SPLIT)
        states[1 - same[0], span, :] = mine[step][...]
        states[same[0], span, :] = theirs[step][...]
    for number, (query, conv, gain) in enumerate(groups):
        state = states.at[number]
        acc[...] = jnp.zeros_like(acc)
        totals = state[FROWS : FROWS + 16, :FROWS]
        for head in range(GROUP):
            feat = features(query[head * FEAT : (head + 1) * FEAT, :], 2.0)
            denom = jnp.dot(totals, feat.astype(jnp.bfloat16), preferred_element_type=jnp.float32)
            scale = 1.0 / denom[head : head + 1, :]
            scaled = (feat * scale).astype(jnp.bfloat16)
            start, stop = window_of(head)
            part = state[:FROWS, start:stop]
            part = jnp.where(head_mask(head, FROWS), part, jnp.zeros_like(part))
            acc[:, start:stop] += lax.dot_general(
                scaled, part, (((0,), (0,)), ((), ())), preferred_element_type=jnp.float32
            )
        low = y_place[0] % 2
        spot = low if number == 0 else 1 - low
        span = pl.ds(pl.multiple_of(spot * VCOLS, VCOLS), VCOLS)
        for block, slot in enumerate(SLOTS):
            rows = slice(block * BLOCK, (block + 1) * BLOCK)
            mixed = acc[rows, :] * gain[3:4, :] + conv[rows, :].astype(jnp.float32)
            outs[slot][:, span] = mixed.astype(jnp.bfloat16)


def attend(y_place, same, groups, mine, theirs):
    vmem = pl.BlockSpec(memory_space=pltpu.VMEM)
    return pl.pallas_call(
        attend_kernel,
        out_shape=[jax.ShapeDtypeStruct((BLOCK, 2 * VCOLS), jnp.bfloat16)] * 4,
        in_specs=[pl.BlockSpec(memory_space=pltpu.SMEM)] * 2 + [vmem] * 14,
        out_specs=[vmem] * 4,
        scratch_shapes=[
            pltpu.VMEM((ROWS, VCOLS), jnp.float32),
            pltpu.VMEM((2, MROWS, VCOLS), jnp.bfloat16),
        ],
        compiler_params=pltpu.CompilerParams(vmem_limit_bytes=VMEM_SMALL),
    )(y_place, same, *[array for group in groups for array in group], *mine, *theirs)


def body(tokens, query_weight, key_weight, value_weight, conv_taps, norm_gain):
    tensor, seq = lax.axis_index("tensor"), lax.axis_index("seq")
    x_at, y_low = tensor // 2, tensor % 2
    core, z_odd = seq % 2, (seq // 2) % 2
    y_at = (seq // 16) * 2 + y_low
    rows = tokens.reshape(BLOCK, tokens.shape[-1])
    weights = (query_weight, key_weight, value_weight)
    half = rows.shape[1] // 2

    y_place = y_at.reshape(1).astype(jnp.int32)
    x_place = x_at.reshape(1).astype(jnp.int32)
    same = (core == y_low).astype(jnp.int32).reshape(1)
    part = BLOCK // 2

    def from_side(array):
        return receive(array, lambda x, y, z, c: (x, y + 2 * c - 1, z, c))

    def from_other(array):
        return receive(array, lambda x, y, z, c: (x, y ^ 1, z, c))

    one = from_x(rows, 1)
    three = from_x(rows, -1)
    two_top = from_x(one[:part], 1)
    two_low = from_x(three[part:], -1)

    base = core * half
    mixed_z = z_odd * 2 * PIECE
    packed = pack(weights, (base + mixed_z, base + mixed_z + PIECE, base + 4 * PIECE), (PIECE,) * 3)
    side = [from_side(array) for array in packed]
    side_z = [receive(array, lambda x, y, z, c: (x, y, z + 2 * c - 1, c)) for array in side[:2]]
    mine = [side[0], side[1], *side_z, side[2]]
    theirs = [from_core(array) for array in mine]
    flip = 2 * PIECE - mixed_z
    steps = jnp.stack([mixed_z, mixed_z + PIECE, flip, flip + PIECE, jnp.full_like(z_odd, 4 * PIECE)])
    offsets = jnp.concatenate([base + steps, (half - base) + steps]).astype(jnp.int32)
    small = jnp.concatenate([conv_taps, norm_gain[None]], axis=0)
    small_other = from_other(small)

    blocks = (rows, one, three, two_top, two_low)
    place = jnp.concatenate([x_place, y_low.reshape(1).astype(jnp.int32), same])
    value_own, value_other, query_key_own, query_key_other, edge = project(
        offsets, blocks, weights, (*mine, *theirs), arrived(two_top, two_low)
    )
    taps = (small, small_other)
    inner_own, inner_other, query_own, query_other, feat_own, feat_other, rim = prepare(
        (value_own, value_other), (query_key_own, query_key_other), taps
    )
    conv_own, conv_other, keep, give = states_of(
        place, (inner_own, inner_other), (feat_own, feat_other), rim, from_other(edge), from_far(edge), taps
    )

    total, *lows = split(y_place, keep, from_core(give))
    for step, low in zip((1, 2, 3), lows):
        total = total + from_y(low, -step).astype(jnp.float32)
    low = total.astype(jnp.bfloat16)
    for step in (1, -1, 2):
        total = total + from_z(low, step).astype(jnp.float32)
    low = total.astype(jnp.bfloat16)
    quarter = (total + from_z(low, 4).astype(jnp.float32)).astype(jnp.bfloat16)
    mine = [quarter] + [from_y(quarter, step) for step in (1, 2, 3)]
    theirs = [from_core(array) for array in mine]

    out = attend(
        y_place,
        same,
        ((query_own, conv_own, small), (query_other, conv_other, small_other)),
        mine,
        theirs,
    )
    result = join(x_place, [out[0], from_x(out[3], 1), from_x(out[2], 2), from_x(out[1], -1)])
    return result.reshape(tokens.shape)


def solution(mesh):
    return jax.shard_map(
        body,
        mesh=mesh,
        in_specs=(
            P("seq", "tensor", None),
            P(None, "tensor"),
            P(None, "tensor"),
            P(None, "tensor"),
            P(None, "tensor"),
            P("tensor"),
        ),
        out_specs=P("seq", "tensor", None),
        check_vma=False,
    )
```

```python
import functools

import jax
import jax.numpy as jnp
from jax import lax
from jax.experimental import pallas as pl
from jax.experimental.pallas import tpu as pltpu
from jax.sharding import PartitionSpec as P

FEAT = 16
HEAD_DIM = 80
GROUP = 8
NX, NY, NZ = 4, 4, 8
AXES = ("tensor", "seq")
PIECE = 512
PIECES = (PIECE,) * 10
VMEM_LIMIT = 58 * 1024 * 1024
VMEM_SMALL = 16 * 1024 * 1024
FROWS = 160
MROWS = 192
BLOCK = 128
ROWS = 4 * BLOCK
PARTS = ((4,), (0, 1), (2, 3), (5, 6), (7, 8), (9,))
AHEAD = 2
EARLY_PARTS = (512, 512, 1024, 1024, 1024, 1024)
EARLY_COST = 3 * 10**9
ORDER_COST = 5 * 10**9
SLOTS = (0, 1, 3, 2)
VCOLS = GROUP * HEAD_DIM
QCOLS = GROUP * FEAT
GCOLS = VCOLS + 2 * QCOLS
SPLIT = MROWS // NY


def device_of(x, y, z, core):
    x, y, z = x % NX, y % NY, z % NZ
    tensor = x * 2 + (y & 1)
    seq = ((y >> 1) * NZ + z) * 2 + core
    return tensor * 32 + seq


def everywhere():
    return [
        (x, y, z, core)
        for x in range(NX)
        for y in range(NY)
        for z in range(NZ)
        for core in range(2)
    ]


def receive(array, source_of):
    pairs = [(device_of(*source_of(*place)), device_of(*place)) for place in everywhere()]
    return lax.ppermute(array, AXES, pairs)


def from_x(array, step):
    return receive(array, lambda x, y, z, c: (x + step, y, z, c))


def from_y(array, step):
    return receive(array, lambda x, y, z, c: (x, y + step, z, c))


def from_z(array, step):
    return receive(array, lambda x, y, z, c: (x, y, z + step, c))


def from_core(array):
    return receive(array, lambda x, y, z, c: (x, y, z, 1 - c))


def from_far(array):
    place = {}
    for x, y, z, core in everywhere():
        place[x, y & 1, ((y >> 1) * NZ + z) * 2 + core] = device_of(x, y, z, core)
    pairs = []
    for (x, odd, segment), target in place.items():
        source = place.get((x, 1 - odd, segment + (1 if odd else -1)))
        if source is not None:
            pairs.append((source, target))
    return lax.ppermute(array, AXES, pairs)


def features(scaled, off_weight):
    root = 0.5**0.5
    rows = scaled.shape[1]
    parts = [scaled, scaled * scaled * root]
    for step in range(1, FEAT // 2):
        turned = pltpu.roll(scaled, FEAT - step, 0)
        parts.append(scaled * turned * (root * off_weight))
    half = scaled[: FEAT // 2] * scaled[FEAT // 2 :] * (root * off_weight)
    parts.append(half)
    first = lax.broadcasted_iota(jnp.int32, (FEAT // 2, rows), 0) == 0
    parts.append(jnp.where(first, 1.0, 0.0).astype(jnp.float32))
    return jnp.concatenate(parts, axis=0)


def window_of(head):
    start = head * HEAD_DIM // 128 * 128
    stop = -(-(head + 1) * HEAD_DIM // 128) * 128
    return start, stop


def head_mask(head, rows):
    start, stop = window_of(head)
    lane = lax.broadcasted_iota(jnp.int32, (rows, stop - start), 1) + start
    return (lane >= head * HEAD_DIM) & (lane < (head + 1) * HEAD_DIM)


def early_kernel(counts, *refs):
    refs = list(refs)
    blocks = [refs.pop(0) for _ in counts]
    weights = [refs.pop(0) for _ in range(3)]
    taps, gain = refs.pop(0), refs.pop(0)
    value_out, query_key_out, edge_out, small_out, xs, ws, acc, xsem, wsem = refs
    small_out[: taps.shape[0], :] = taps[...]
    small_out[taps.shape[0] :, :] = gain[...]
    stages, at = [], 0
    for index, count in enumerate(EARLY_PARTS):
        copies, row = [], 0
        for number, (ref, rows) in enumerate(zip(blocks, counts)):
            copies.append(
                pltpu.make_async_copy(
                    ref.at[:, pl.ds(at, count)], xs.at[pl.ds(row, rows), pl.ds(at, count)], xsem.at[index, number]
                )
            )
            row += rows
        for kind, (col, width) in enumerate(((0, QCOLS), (QCOLS, QCOLS), (2 * QCOLS, VCOLS))):
            copies.append(
                pltpu.make_async_copy(
                    weights[kind].at[pl.ds(at, count)],
                    ws.at[pl.ds(at, count), pl.ds(col, width)],
                    wsem.at[index, kind],
                )
            )
        stages.append((copies, at, count))
        at += count
    for copies, _, _ in stages[:AHEAD]:
        for copy in copies:
            copy.start()
    for index, (copies, at, count) in enumerate(stages):
        for copy in copies:
            copy.wait()
        if index + AHEAD < len(stages):
            for copy in stages[index + AHEAD][0]:
                copy.start()
        span = slice(at, at + count)
        part = jnp.dot(xs[:, span], ws[span, :], preferred_element_type=jnp.float32)
        if index == 0:
            acc[...] = part
        else:
            acc[...] += part
    query_key_out[...] = acc[:, : 2 * QCOLS]
    value_out[...] = acc[:, 2 * QCOLS :].astype(jnp.bfloat16)
    edge_out[...] = jnp.zeros_like(edge_out)
    for block, slot in enumerate(SLOTS[:3]):
        for end, row in ((0, block * BLOCK), (1, block * BLOCK + BLOCK - 1)):
            line = acc[row : row + 1, 2 * QCOLS :]
            edge_out[2 * slot + end : 2 * slot + end + 1, :] = line.astype(jnp.bfloat16).astype(jnp.float32)


def project_early(blocks, weights, taps, gain):
    counts = tuple(block.shape[0] for block in blocks)
    depth, rows = blocks[0].shape[1], sum(counts)
    hbm = pl.BlockSpec(memory_space=pltpu.HBM)
    vmem = pl.BlockSpec(memory_space=pltpu.VMEM)
    return pl.pallas_call(
        functools.partial(early_kernel, counts),
        out_shape=[
            jax.ShapeDtypeStruct((rows, VCOLS), jnp.bfloat16),
            jax.ShapeDtypeStruct((rows, 2 * QCOLS), jnp.float32),
            jax.ShapeDtypeStruct((8, VCOLS), jnp.float32),
            jax.ShapeDtypeStruct((taps.shape[0] + 1, VCOLS), jnp.float32),
        ],
        in_specs=[hbm] * (len(blocks) + 3) + [vmem] * 2,
        out_specs=[vmem] * 4,
        scratch_shapes=[
            pltpu.VMEM((rows, depth), jnp.bfloat16),
            pltpu.VMEM((depth, GCOLS), jnp.bfloat16),
            pltpu.VMEM((rows, GCOLS), jnp.float32),
            pltpu.SemaphoreType.DMA((len(EARLY_PARTS), len(blocks))),
            pltpu.SemaphoreType.DMA((len(EARLY_PARTS), 3)),
        ],
        compiler_params=pltpu.CompilerParams(vmem_limit_bytes=VMEM_LIMIT),
        cost_estimate=pl.CostEstimate(flops=EARLY_COST, bytes_accessed=EARLY_COST // 1000, transcendentals=0),
    )(*blocks, *weights, taps, gain)


def project_kernel(counts, offsets, *refs):
    refs = list(refs)
    blocks = [refs.pop(0) for _ in counts]
    weights = [refs.pop(0) for _ in range(3)]
    pieces = [refs.pop(0) for _ in PIECES]
    edge_early = refs.pop(0)
    refs.pop(0)
    value_outs, query_key_outs, edge_out = refs[0:2], refs[2:4], refs[4]
    xs, ws, acc, late, xsem, wsem, psem = refs[5:]
    stages, at = [], 0
    for index, members in enumerate(PARTS):
        count = len(members) * PIECE
        start = pl.multiple_of(offsets[members[0]], PIECE)
        copies, row = [], 0
        for number, (ref, rows) in enumerate(zip(blocks, counts)):
            copies.append(
                pltpu.make_async_copy(
                    ref.at[:, pl.ds(start, count)],
                    xs.at[pl.ds(row, rows), pl.ds(at, count)],
                    xsem.at[index, number],
                )
            )
            row += rows
        for kind, (col, width) in enumerate(((0, QCOLS), (QCOLS, QCOLS), (2 * QCOLS, VCOLS))):
            copies.append(
                pltpu.make_async_copy(
                    weights[kind].at[pl.ds(start, count)],
                    ws.at[pl.ds(at, count), pl.ds(col, width)],
                    wsem.at[index, kind],
                )
            )
        for step, member in enumerate(members):
            copies.append(
                pltpu.make_async_copy(
                    pieces[member],
                    ws.at[pl.ds(at + step * PIECE, PIECE), pl.ds(GCOLS, GCOLS)],
                    psem.at[member],
                )
            )
        stages.append((copies, at, count))
        at += count
    for copies, _, _ in stages[:AHEAD]:
        for copy in copies:
            copy.start()
    for index, (copies, at, count) in enumerate(stages):
        for copy in copies:
            copy.wait()
        if index + AHEAD < len(stages):
            for copy in stages[index + AHEAD][0]:
                copy.start()
        span = slice(at, at + count)
        part = jnp.dot(xs[:, span], ws[span, GCOLS:], preferred_element_type=jnp.float32)
        last = jnp.dot(xs[ROWS - BLOCK :, span], ws[span, :GCOLS], preferred_element_type=jnp.float32)
        if index == 0:
            acc[...] = part
            late[...] = last
        else:
            acc[...] += part
            late[...] += last
    edge_out[:8, :] = edge_early[...]
    for group, (total, slots) in enumerate(((late, SLOTS[3:]), (acc, SLOTS))):
        query_key_outs[group][...] = total[:, : 2 * QCOLS]
        value_outs[group][...] = total[:, 2 * QCOLS :].astype(jnp.bfloat16)
        for block, slot in enumerate(slots):
            for end, row in ((0, block * BLOCK), (1, block * BLOCK + BLOCK - 1)):
                line = total[row : row + 1, 2 * QCOLS :]
                at = 8 * group + 2 * slot + end
                edge_out[at : at + 1, :] = line.astype(jnp.bfloat16).astype(jnp.float32)


def project(offsets, blocks, weights, pieces, edge_early, after):
    counts = tuple(block.shape[0] for block in blocks)
    depth = blocks[0].shape[1]
    hbm = pl.BlockSpec(memory_space=pltpu.HBM)
    vmem = pl.BlockSpec(memory_space=pltpu.VMEM)
    return pl.pallas_call(
        functools.partial(project_kernel, counts),
        out_shape=[jax.ShapeDtypeStruct((rows, VCOLS), jnp.bfloat16) for rows in (BLOCK, ROWS)]
        + [jax.ShapeDtypeStruct((rows, 2 * QCOLS), jnp.float32) for rows in (BLOCK, ROWS)]
        + [jax.ShapeDtypeStruct((16, VCOLS), jnp.float32)],
        in_specs=[pl.BlockSpec(memory_space=pltpu.SMEM)] + [hbm] * (len(blocks) + 3 + len(pieces)) + [vmem, hbm],
        out_specs=[vmem] * 5,
        scratch_shapes=[
            pltpu.VMEM((ROWS, depth), jnp.bfloat16),
            pltpu.VMEM((depth, 2 * GCOLS), jnp.bfloat16),
            pltpu.VMEM((ROWS, GCOLS), jnp.float32),
            pltpu.VMEM((BLOCK, GCOLS), jnp.float32),
            pltpu.SemaphoreType.DMA((len(PARTS), len(blocks))),
            pltpu.SemaphoreType.DMA((len(PARTS), 3)),
            pltpu.SemaphoreType.DMA((len(pieces),)),
        ],
        compiler_params=pltpu.CompilerParams(vmem_limit_bytes=VMEM_LIMIT),
        cost_estimate=pl.CostEstimate(
            flops=3 * ROWS * depth * GCOLS, bytes_accessed=2 * depth * (ROWS + 2 * GCOLS), transcendentals=0
        ),
    )(offsets, *blocks, *weights, *pieces, edge_early, after)


def order_kernel(top, low, early, out):
    del top, low, early
    out[...] = jnp.zeros_like(out)


def arrived(top, low, early):
    hbm = pl.BlockSpec(memory_space=pltpu.HBM)
    return pl.pallas_call(
        order_kernel,
        out_shape=jax.ShapeDtypeStruct((8, 128), jnp.float32),
        in_specs=[hbm] * 3,
        out_specs=pl.BlockSpec(memory_space=pltpu.VMEM),
        compiler_params=pltpu.CompilerParams(vmem_limit_bytes=VMEM_LIMIT),
        cost_estimate=pl.CostEstimate(flops=ORDER_COST, bytes_accessed=15 * 10**6, transcendentals=0),
    )(top, low, early)


def prepare_kernel(*refs):
    values, query_keys, taps = ((refs[0], refs[1]), (refs[2],)), ((refs[3], refs[4]), (refs[5],)), refs[6:8]
    convs, queries, feats, rim = refs[8:10], refs[10:12], refs[12:14], refs[14]
    row = lax.broadcasted_iota(jnp.int32, (BLOCK, VCOLS), 0)
    for group in range(2):
        turned = [array[...].T * 0.5 for array in query_keys[group]]
        turned = turned[0] if len(turned) == 1 else jnp.concatenate(turned, axis=1)
        queries[group][...] = turned[:QCOLS]
        key = turned[QCOLS:]
        pieces = [
            array[start : start + BLOCK, :]
            for array in values[group]
            for start in range(0, array.shape[0], BLOCK)
        ]
        for head in range(GROUP):
            feat = features(key[head * FEAT : (head + 1) * FEAT], 1.0)
            feats[group][head * FROWS : (head + 1) * FROWS, :] = feat.astype(jnp.bfloat16)
        tap = taps[group]
        for number, block in enumerate(SLOTS):
            span = slice(number * BLOCK, (number + 1) * BLOCK)
            mid = pieces[number].astype(jnp.float32)
            low = jnp.where(row == 0, 0.0, pltpu.roll(mid, 1, 0))
            high = jnp.where(row == BLOCK - 1, 0.0, pltpu.roll(mid, BLOCK - 1, 0))
            conv = tap[0:1, :] * low + tap[1:2, :] * mid + tap[2:3, :] * high
            convs[group][span, :] = conv.astype(jnp.bfloat16)
            at = 8 * group + 2 * block
            rim[at : at + 1, :] = conv[0:1]
            rim[at + 1 : at + 2, :] = conv[BLOCK - 1 : BLOCK]


def prepare(values, query_keys, taps):
    vmem = pl.BlockSpec(memory_space=pltpu.VMEM)
    return pl.pallas_call(
        prepare_kernel,
        out_shape=[jax.ShapeDtypeStruct((ROWS, VCOLS), jnp.bfloat16)] * 2
        + [jax.ShapeDtypeStruct((QCOLS, ROWS), jnp.float32)] * 2
        + [jax.ShapeDtypeStruct((GROUP * FROWS, ROWS), jnp.bfloat16)] * 2
        + [jax.ShapeDtypeStruct((16, VCOLS), jnp.float32)],
        in_specs=[vmem] * 8,
        out_specs=[vmem] * 7,
        compiler_params=pltpu.CompilerParams(vmem_limit_bytes=VMEM_SMALL),
        cost_estimate=pl.CostEstimate(flops=3 * 10**9, bytes_accessed=8 * 10**6, transcendentals=0),
    )(*values, *query_keys, *taps)


def state_kernel(place, *refs):
    inner, feats, (rim, near, far), taps = refs[0:2], refs[2:4], refs[4:7], refs[7:9]
    convs, (keep_out, give_out), states = refs[9:11], refs[11:13], refs[13]
    x_at, even = place[0], place[1] == 0
    row = lax.broadcasted_iota(jnp.int32, (BLOCK, VCOLS), 0)
    ones = jnp.ones((8, ROWS), jnp.bfloat16)
    states[...] = jnp.zeros_like(states)
    for group in range(2):
        state, conv_out, tap = states.at[group], convs[group], taps[group]

        def line(ref, block, end):
            at = 8 * (1 - group) + 2 * (block % 4) + end
            return ref[at : at + 1, :]

        for number, block in enumerate(SLOTS):
            span = slice(number * BLOCK, (number + 1) * BLOCK)
            at = 8 * group + 2 * block
            opening = jnp.where((x_at + block) % NX == 0, line(far, block - 1, 1), line(near, block - 1, 1))
            before = jnp.where(even, opening, line(near, block, 1))
            closing = jnp.where((x_at + block) % NX == NX - 1, line(far, block + 1, 0), line(near, block + 1, 0))
            after = jnp.where(even, line(near, block, 0), closing)
            first = rim[at : at + 1, :] + tap[0:1, :] * before
            last = rim[at + 1 : at + 2, :] + tap[2:3, :] * after
            conv = inner[group][span, :].astype(jnp.float32)
            conv = jnp.where(row == 0, first, jnp.where(row == BLOCK - 1, last, conv))
            conv_out[span, :] = conv.astype(jnp.bfloat16)
        for head in range(GROUP):
            feat = feats[group][head * FROWS : (head + 1) * FROWS, :]
            start, stop = window_of(head)
            share = jnp.dot(feat, conv_out[:, start:stop], preferred_element_type=jnp.float32)
            state[:FROWS, start:stop] += jnp.where(head_mask(head, FROWS), share, 0.0)
            total = lax.dot_general(
                ones, feat, (((1,), (1,)), ((), ())), preferred_element_type=jnp.float32
            )
            state[FROWS + head : FROWS + head + 1, :FROWS] = total[0:1]
    same = place[2] == 1
    keep_out[...] = jnp.where(same, states[0], states[1])
    give_out[...] = jnp.where(same, states[1], states[0]).astype(jnp.bfloat16)


def states_of(place, inner, feats, rim, near, far, taps):
    vmem = pl.BlockSpec(memory_space=pltpu.VMEM)
    return pl.pallas_call(
        state_kernel,
        out_shape=[jax.ShapeDtypeStruct((ROWS, VCOLS), jnp.bfloat16)] * 2
        + [
            jax.ShapeDtypeStruct((MROWS, VCOLS), jnp.float32),
            jax.ShapeDtypeStruct((MROWS, VCOLS), jnp.bfloat16),
        ],
        in_specs=[pl.BlockSpec(memory_space=pltpu.SMEM)] + [vmem] * 9,
        out_specs=[vmem] * 4,
        scratch_shapes=[pltpu.VMEM((2, MROWS, VCOLS), jnp.float32)],
        compiler_params=pltpu.CompilerParams(vmem_limit_bytes=VMEM_SMALL),
        cost_estimate=pl.CostEstimate(flops=3 * 10**9, bytes_accessed=8 * 10**6, transcendentals=0),
    )(place, *inner, *feats, rim, near, far, *taps)


def pack_kernel(start, query, key, value, *refs):
    outs, sems = refs[:-1], refs[-1]
    copies = []
    for index, out in enumerate(outs):
        count = out.shape[0]
        span = pl.ds(pl.multiple_of(start[index], 256), count)
        for kind, (ref, col, width) in enumerate(
            ((query, 0, QCOLS), (key, QCOLS, QCOLS), (value, 2 * QCOLS, VCOLS))
        ):
            copies.append(
                pltpu.make_async_copy(ref.at[span], out.at[:, pl.ds(col, width)], sems.at[index, kind])
            )
    for copy in copies:
        copy.start()
    for copy in copies:
        copy.wait()


def pack(weights, starts, counts):
    hbm = pl.BlockSpec(memory_space=pltpu.HBM)
    return pl.pallas_call(
        pack_kernel,
        out_shape=[jax.ShapeDtypeStruct((count, GCOLS), jnp.bfloat16) for count in counts],
        in_specs=[pl.BlockSpec(memory_space=pltpu.SMEM)] + [hbm] * 3,
        out_specs=[pl.BlockSpec(memory_space=pltpu.VMEM)] * len(counts),
        scratch_shapes=[pltpu.SemaphoreType.DMA((len(counts), 3))],
        compiler_params=pltpu.CompilerParams(vmem_limit_bytes=VMEM_LIMIT),
    )(jnp.stack(starts).astype(jnp.int32), *weights)


def split_kernel(place, keep, got, part_out, *lows):
    for step in range(NY):
        span = pl.ds(pl.multiple_of((place[0] + step) % NY * SPLIT, SPLIT), SPLIT)
        total = keep[span, :] + got[span, :].astype(jnp.float32)
        if step == 0:
            part_out[...] = total
        else:
            lows[step - 1][...] = total.astype(jnp.bfloat16)


def split(place, keep, got):
    vmem = pl.BlockSpec(memory_space=pltpu.VMEM)
    return pl.pallas_call(
        split_kernel,
        out_shape=[jax.ShapeDtypeStruct((SPLIT, VCOLS), jnp.float32)]
        + [jax.ShapeDtypeStruct((SPLIT, VCOLS), jnp.bfloat16)] * 3,
        in_specs=[pl.BlockSpec(memory_space=pltpu.SMEM), vmem, vmem],
        out_specs=[vmem] * 4,
        compiler_params=pltpu.CompilerParams(vmem_limit_bytes=VMEM_SMALL),
    )(place, keep, got)


def join_kernel(place, *refs):
    blocks, out = refs[:NX], refs[NX]
    width = blocks[0].shape[1]
    for step, block in enumerate(blocks):
        span = pl.ds(pl.multiple_of((place[0] + step) % NX * width, 128), width)
        out[:, span] = block[...]


def join(place, blocks):
    vmem = pl.BlockSpec(memory_space=pltpu.VMEM)
    rows, width = blocks[0].shape
    return pl.pallas_call(
        join_kernel,
        out_shape=jax.ShapeDtypeStruct((rows, NX * width), blocks[0].dtype),
        in_specs=[pl.BlockSpec(memory_space=pltpu.SMEM)] + [vmem] * NX,
        out_specs=vmem,
        compiler_params=pltpu.CompilerParams(vmem_limit_bytes=VMEM_SMALL),
    )(place, *blocks)


def attend_kernel(y_place, same, *refs):
    groups = (refs[0:3], refs[3:6])
    mine, theirs = refs[6:10], refs[10:14]
    outs, acc, states = refs[14:18], refs[18], refs[19]
    for step in range(NY):
        span = pl.ds(pl.multiple_of((y_place[0] + step) % NY * SPLIT, SPLIT), SPLIT)
        states[1 - same[0], span, :] = mine[step][...]
        states[same[0], span, :] = theirs[step][...]
    for number, (query, conv, gain) in enumerate(groups):
        state = states.at[number]
        acc[...] = jnp.zeros_like(acc)
        totals = state[FROWS : FROWS + 16, :FROWS]
        for head in range(GROUP):
            feat = features(query[head * FEAT : (head + 1) * FEAT, :], 2.0)
            denom = jnp.dot(totals, feat.astype(jnp.bfloat16), preferred_element_type=jnp.float32)
            scale = 1.0 / denom[head : head + 1, :]
            scaled = (feat * scale).astype(jnp.bfloat16)
            start, stop = window_of(head)
            part = state[:FROWS, start:stop]
            part = jnp.where(head_mask(head, FROWS), part, jnp.zeros_like(part))
            acc[:, start:stop] += lax.dot_general(
                scaled, part, (((0,), (0,)), ((), ())), preferred_element_type=jnp.float32
            )
        low = y_place[0] % 2
        spot = low if number == 0 else 1 - low
        span = pl.ds(pl.multiple_of(spot * VCOLS, VCOLS), VCOLS)
        for block, slot in enumerate(SLOTS):
            rows = slice(block * BLOCK, (block + 1) * BLOCK)
            mixed = acc[rows, :] * gain[3:4, :] + conv[rows, :].astype(jnp.float32)
            outs[slot][:, span] = mixed.astype(jnp.bfloat16)


def attend(y_place, same, groups, mine, theirs):
    vmem = pl.BlockSpec(memory_space=pltpu.VMEM)
    return pl.pallas_call(
        attend_kernel,
        out_shape=[jax.ShapeDtypeStruct((BLOCK, 2 * VCOLS), jnp.bfloat16)] * 4,
        in_specs=[pl.BlockSpec(memory_space=pltpu.SMEM)] * 2 + [vmem] * 14,
        out_specs=[vmem] * 4,
        scratch_shapes=[
            pltpu.VMEM((ROWS, VCOLS), jnp.float32),
            pltpu.VMEM((2, MROWS, VCOLS), jnp.bfloat16),
        ],
        compiler_params=pltpu.CompilerParams(vmem_limit_bytes=VMEM_SMALL),
    )(y_place, same, *[array for group in groups for array in group], *mine, *theirs)


def body(tokens, query_weight, key_weight, value_weight, conv_taps, norm_gain):
    tensor, seq = lax.axis_index("tensor"), lax.axis_index("seq")
    x_at, y_low = tensor // 2, tensor % 2
    core, z_odd = seq % 2, (seq // 2) % 2
    y_at = (seq // 16) * 2 + y_low
    rows = tokens.reshape(BLOCK, tokens.shape[-1])
    weights = (query_weight, key_weight, value_weight)
    half = rows.shape[1] // 2

    y_place = y_at.reshape(1).astype(jnp.int32)
    x_place = x_at.reshape(1).astype(jnp.int32)
    same = (core == y_low).astype(jnp.int32).reshape(1)
    part = BLOCK // 2

    def from_side(array):
        return receive(array, lambda x, y, z, c: (x, y + 2 * c - 1, z, c))

    def from_other(array):
        return receive(array, lambda x, y, z, c: (x, y ^ 1, z, c))

    one = from_x(rows, 1)
    three = from_x(rows, -1)
    two_top = from_x(one[:part], 1)
    two_low = from_x(three[part:], -1)

    base = core * half
    mixed_z = z_odd * 2 * PIECE
    packed = pack(weights, (base + mixed_z, base + mixed_z + PIECE, base + 4 * PIECE), (PIECE,) * 3)
    side = [from_side(array) for array in packed]
    side_z = [receive(array, lambda x, y, z, c: (x, y, z + 2 * c - 1, c)) for array in side[:2]]
    mine = [side[0], side[1], *side_z, side[2]]
    theirs = [from_core(array) for array in mine]
    flip = 2 * PIECE - mixed_z
    steps = jnp.stack([mixed_z, mixed_z + PIECE, flip, flip + PIECE, jnp.full_like(z_odd, 4 * PIECE)])
    offsets = jnp.concatenate([base + steps, (half - base) + steps]).astype(jnp.int32)

    blocks = (rows, one, three, two_top, two_low)
    place = jnp.concatenate([x_place, y_low.reshape(1).astype(jnp.int32), same])
    value_early, query_key_early, edge_early, small = project_early(
        blocks[:3], weights, conv_taps, norm_gain[None]
    )
    small_other = from_other(small)
    value_late, value_other, query_key_late, query_key_other, edge = project(
        offsets, blocks, weights, (*mine, *theirs), edge_early, arrived(two_top, two_low, small_other)
    )
    taps = (small, small_other)
    inner_own, inner_other, query_own, query_other, feat_own, feat_other, rim = prepare(
        (value_early, value_late, value_other), (query_key_early, query_key_late, query_key_other), taps
    )
    conv_own, conv_other, keep, give = states_of(
        place, (inner_own, inner_other), (feat_own, feat_other), rim, from_other(edge), from_far(edge), taps
    )

    total, *lows = split(y_place, keep, from_core(give))
    for step, low in zip((1, 2, 3), lows):
        total = total + from_y(low, -step).astype(jnp.float32)
    low = total.astype(jnp.bfloat16)
    for step in (1, -1, 2):
        total = total + from_z(low, step).astype(jnp.float32)
    low = total.astype(jnp.bfloat16)
    quarter = (total + from_z(low, 4).astype(jnp.float32)).astype(jnp.bfloat16)
    mine = [quarter] + [from_y(quarter, step) for step in (1, 2, 3)]
    theirs = [from_core(array) for array in mine]

    out = attend(
        y_place,
        same,
        ((query_own, conv_own, small), (query_other, conv_other, small_other)),
        mine,
        theirs,
    )
    result = join(x_place, [out[0], from_x(out[3], 1), from_x(out[2], 2), from_x(out[1], -1)])
    return result.reshape(tokens.shape)


def solution(mesh):
    return jax.shard_map(
        body,
        mesh=mesh,
        in_specs=(
            P("seq", "tensor", None),
            P(None, "tensor"),
            P(None, "tensor"),
            P(None, "tensor"),
            P(None, "tensor"),
            P("tensor"),
        ),
        out_specs=P("seq", "tensor", None),
        check_vma=False,
    )
```

```python
import functools

import jax
import jax.numpy as jnp
from jax import lax
from jax.experimental import pallas as pl
from jax.experimental.pallas import tpu as pltpu
from jax.sharding import PartitionSpec as P

FEAT = 16
HEAD_DIM = 80
GROUP = 8
NX, NY, NZ = 4, 4, 8
AXES = ("tensor", "seq")
PIECE = 512
PIECES = (PIECE,) * 10
VMEM_LIMIT = 58 * 1024 * 1024
VMEM_SMALL = 16 * 1024 * 1024
FROWS = 160
MROWS = 192
BLOCK = 128
ROWS = 4 * BLOCK
PARTS = ((4,), (0, 1), (2, 3), (5, 6), (7, 8), (9,))
AHEAD = 2
EARLY = 1024
EARLY_COST = 3 * 10**9
ORDER_COST = 5 * 10**9
SLOTS = (0, 1, 3, 2)
VCOLS = GROUP * HEAD_DIM
QCOLS = GROUP * FEAT
GCOLS = VCOLS + 2 * QCOLS
SPLIT = MROWS // NY


def device_of(x, y, z, core):
    x, y, z = x % NX, y % NY, z % NZ
    tensor = x * 2 + (y & 1)
    seq = ((y >> 1) * NZ + z) * 2 + core
    return tensor * 32 + seq


def everywhere():
    return [
        (x, y, z, core)
        for x in range(NX)
        for y in range(NY)
        for z in range(NZ)
        for core in range(2)
    ]


def receive(array, source_of):
    pairs = [(device_of(*source_of(*place)), device_of(*place)) for place in everywhere()]
    return lax.ppermute(array, AXES, pairs)


def from_x(array, step):
    return receive(array, lambda x, y, z, c: (x + step, y, z, c))


def from_y(array, step):
    return receive(array, lambda x, y, z, c: (x, y + step, z, c))


def from_z(array, step):
    return receive(array, lambda x, y, z, c: (x, y, z + step, c))


def from_core(array):
    return receive(array, lambda x, y, z, c: (x, y, z, 1 - c))


def from_far(array):
    place = {}
    for x, y, z, core in everywhere():
        place[x, y & 1, ((y >> 1) * NZ + z) * 2 + core] = device_of(x, y, z, core)
    pairs = []
    for (x, odd, segment), target in place.items():
        source = place.get((x, 1 - odd, segment + (1 if odd else -1)))
        if source is not None:
            pairs.append((source, target))
    return lax.ppermute(array, AXES, pairs)


def features(scaled, off_weight):
    root = 0.5**0.5
    rows = scaled.shape[1]
    parts = [scaled, scaled * scaled * root]
    for step in range(1, FEAT // 2):
        turned = pltpu.roll(scaled, FEAT - step, 0)
        parts.append(scaled * turned * (root * off_weight))
    half = scaled[: FEAT // 2] * scaled[FEAT // 2 :] * (root * off_weight)
    parts.append(half)
    first = lax.broadcasted_iota(jnp.int32, (FEAT // 2, rows), 0) == 0
    parts.append(jnp.where(first, 1.0, 0.0).astype(jnp.float32))
    return jnp.concatenate(parts, axis=0)


def window_of(head):
    start = head * HEAD_DIM // 128 * 128
    stop = -(-(head + 1) * HEAD_DIM // 128) * 128
    return start, stop


def head_mask(head, rows):
    start, stop = window_of(head)
    lane = lax.broadcasted_iota(jnp.int32, (rows, stop - start), 1) + start
    return (lane >= head * HEAD_DIM) & (lane < (head + 1) * HEAD_DIM)


def early_kernel(counts, *refs):
    refs = list(refs)
    blocks = [refs.pop(0) for _ in counts]
    weights = [refs.pop(0) for _ in range(3)]
    taps, gain = refs.pop(0), refs.pop(0)
    value_out, query_key_out, edge_out, small_out, xs, ws, acc, xsem, wsem = refs
    small_out[: taps.shape[0], :] = taps[...]
    small_out[taps.shape[0] :, :] = gain[...]

    def copies_of(index):
        span, copies, row = pl.ds(pl.multiple_of(index * EARLY, EARLY), EARLY), [], 0
        for number, (ref, rows) in enumerate(zip(blocks, counts)):
            copies.append(
                pltpu.make_async_copy(ref.at[:, span], xs.at[pl.ds(row, rows), span], xsem.at[index, number])
            )
            row += rows
        for kind, (col, width) in enumerate(((0, QCOLS), (QCOLS, QCOLS), (2 * QCOLS, VCOLS))):
            copies.append(
                pltpu.make_async_copy(
                    weights[kind].at[span], ws.at[span, pl.ds(col, width)], wsem.at[index, kind]
                )
            )
        return copies

    count = xs.shape[1] // EARLY
    for index in range(AHEAD):
        for copy in copies_of(index):
            copy.start()
    acc[...] = jnp.zeros_like(acc)

    def step(index, carry):
        for copy in copies_of(index):
            copy.wait()

        @pl.when(index + AHEAD < count)
        def _():
            for copy in copies_of(index + AHEAD):
                copy.start()

        span = pl.ds(pl.multiple_of(index * EARLY, EARLY), EARLY)
        acc[...] += jnp.dot(xs[:, span], ws[span, :], preferred_element_type=jnp.float32)
        return carry

    lax.fori_loop(0, count, step, 0)
    query_key_out[...] = acc[:, : 2 * QCOLS]
    value_out[...] = acc[:, 2 * QCOLS :].astype(jnp.bfloat16)
    edge_out[...] = jnp.zeros_like(edge_out)
    for block, slot in enumerate(SLOTS[:3]):
        for end, row in ((0, block * BLOCK), (1, block * BLOCK + BLOCK - 1)):
            line = acc[row : row + 1, 2 * QCOLS :]
            edge_out[2 * slot + end : 2 * slot + end + 1, :] = line.astype(jnp.bfloat16).astype(jnp.float32)


def project_early(blocks, weights, taps, gain):
    counts = tuple(block.shape[0] for block in blocks)
    depth, rows = blocks[0].shape[1], sum(counts)
    hbm = pl.BlockSpec(memory_space=pltpu.HBM)
    vmem = pl.BlockSpec(memory_space=pltpu.VMEM)
    return pl.pallas_call(
        functools.partial(early_kernel, counts),
        out_shape=[
            jax.ShapeDtypeStruct((rows, VCOLS), jnp.bfloat16),
            jax.ShapeDtypeStruct((rows, 2 * QCOLS), jnp.float32),
            jax.ShapeDtypeStruct((8, VCOLS), jnp.float32),
            jax.ShapeDtypeStruct((taps.shape[0] + 1, VCOLS), jnp.float32),
        ],
        in_specs=[hbm] * (len(blocks) + 3) + [vmem] * 2,
        out_specs=[vmem] * 4,
        scratch_shapes=[
            pltpu.VMEM((rows, depth), jnp.bfloat16),
            pltpu.VMEM((depth, GCOLS), jnp.bfloat16),
            pltpu.VMEM((rows, GCOLS), jnp.float32),
            pltpu.SemaphoreType.DMA((depth // EARLY, len(blocks))),
            pltpu.SemaphoreType.DMA((depth // EARLY, 3)),
        ],
        compiler_params=pltpu.CompilerParams(vmem_limit_bytes=VMEM_LIMIT),
        cost_estimate=pl.CostEstimate(flops=EARLY_COST, bytes_accessed=EARLY_COST // 1000, transcendentals=0),
    )(*blocks, *weights, taps, gain)


def project_kernel(counts, offsets, *refs):
    refs = list(refs)
    blocks = [refs.pop(0) for _ in counts]
    weights = [refs.pop(0) for _ in range(3)]
    pieces = [refs.pop(0) for _ in PIECES]
    edge_early = refs.pop(0)
    refs.pop(0)
    value_outs, query_key_outs, edge_out = refs[0:2], refs[2:4], refs[4]
    xs, ws, acc, late, xsem, wsem, psem = refs[5:]
    stages, at = [], 0
    for index, members in enumerate(PARTS):
        count = len(members) * PIECE
        start = pl.multiple_of(offsets[members[0]], PIECE)
        copies, row = [], 0
        for number, (ref, rows) in enumerate(zip(blocks, counts)):
            copies.append(
                pltpu.make_async_copy(
                    ref.at[:, pl.ds(start, count)],
                    xs.at[pl.ds(row, rows), pl.ds(at, count)],
                    xsem.at[index, number],
                )
            )
            row += rows
        for kind, (col, width) in enumerate(((0, QCOLS), (QCOLS, QCOLS), (2 * QCOLS, VCOLS))):
            copies.append(
                pltpu.make_async_copy(
                    weights[kind].at[pl.ds(start, count)],
                    ws.at[pl.ds(at, count), pl.ds(col, width)],
                    wsem.at[index, kind],
                )
            )
        for step, member in enumerate(members):
            copies.append(
                pltpu.make_async_copy(
                    pieces[member],
                    ws.at[pl.ds(at + step * PIECE, PIECE), pl.ds(GCOLS, GCOLS)],
                    psem.at[member],
                )
            )
        stages.append((copies, at, count))
        at += count
    for copies, _, _ in stages[:AHEAD]:
        for copy in copies:
            copy.start()
    for index, (copies, at, count) in enumerate(stages):
        for copy in copies:
            copy.wait()
        if index + AHEAD < len(stages):
            for copy in stages[index + AHEAD][0]:
                copy.start()
        span = slice(at, at + count)
        part = jnp.dot(xs[:, span], ws[span, GCOLS:], preferred_element_type=jnp.float32)
        last = jnp.dot(xs[ROWS - BLOCK :, span], ws[span, :GCOLS], preferred_element_type=jnp.float32)
        if index == 0:
            acc[...] = part
            late[...] = last
        else:
            acc[...] += part
            late[...] += last
    edge_out[:8, :] = edge_early[...]
    for group, (total, slots) in enumerate(((late, SLOTS[3:]), (acc, SLOTS))):
        query_key_outs[group][...] = total[:, : 2 * QCOLS]
        value_outs[group][...] = total[:, 2 * QCOLS :].astype(jnp.bfloat16)
        for block, slot in enumerate(slots):
            for end, row in ((0, block * BLOCK), (1, block * BLOCK + BLOCK - 1)):
                line = total[row : row + 1, 2 * QCOLS :]
                at = 8 * group + 2 * slot + end
                edge_out[at : at + 1, :] = line.astype(jnp.bfloat16).astype(jnp.float32)


def project(offsets, blocks, weights, pieces, edge_early, after):
    counts = tuple(block.shape[0] for block in blocks)
    depth = blocks[0].shape[1]
    hbm = pl.BlockSpec(memory_space=pltpu.HBM)
    vmem = pl.BlockSpec(memory_space=pltpu.VMEM)
    return pl.pallas_call(
        functools.partial(project_kernel, counts),
        out_shape=[jax.ShapeDtypeStruct((rows, VCOLS), jnp.bfloat16) for rows in (BLOCK, ROWS)]
        + [jax.ShapeDtypeStruct((rows, 2 * QCOLS), jnp.float32) for rows in (BLOCK, ROWS)]
        + [jax.ShapeDtypeStruct((16, VCOLS), jnp.float32)],
        in_specs=[pl.BlockSpec(memory_space=pltpu.SMEM)] + [hbm] * (len(blocks) + 3 + len(pieces)) + [vmem, hbm],
        out_specs=[vmem] * 5,
        scratch_shapes=[
            pltpu.VMEM((ROWS, depth), jnp.bfloat16),
            pltpu.VMEM((depth, 2 * GCOLS), jnp.bfloat16),
            pltpu.VMEM((ROWS, GCOLS), jnp.float32),
            pltpu.VMEM((BLOCK, GCOLS), jnp.float32),
            pltpu.SemaphoreType.DMA((len(PARTS), len(blocks))),
            pltpu.SemaphoreType.DMA((len(PARTS), 3)),
            pltpu.SemaphoreType.DMA((len(pieces),)),
        ],
        compiler_params=pltpu.CompilerParams(vmem_limit_bytes=VMEM_LIMIT),
        cost_estimate=pl.CostEstimate(
            flops=3 * ROWS * depth * GCOLS, bytes_accessed=2 * depth * (ROWS + 2 * GCOLS), transcendentals=0
        ),
    )(offsets, *blocks, *weights, *pieces, edge_early, after)


def order_kernel(top, low, early, out):
    del top, low, early
    out[...] = jnp.zeros_like(out)


def arrived(top, low, early):
    hbm = pl.BlockSpec(memory_space=pltpu.HBM)
    return pl.pallas_call(
        order_kernel,
        out_shape=jax.ShapeDtypeStruct((8, 128), jnp.float32),
        in_specs=[hbm] * 3,
        out_specs=pl.BlockSpec(memory_space=pltpu.VMEM),
        compiler_params=pltpu.CompilerParams(vmem_limit_bytes=VMEM_LIMIT),
        cost_estimate=pl.CostEstimate(flops=ORDER_COST, bytes_accessed=15 * 10**6, transcendentals=0),
    )(top, low, early)


def state_kernel(place, *refs):
    values, query_keys = ((refs[0], refs[1]), (refs[2],)), ((refs[3], refs[4]), (refs[5],))
    (near, far), taps = refs[6:8], refs[8:10]
    convs, queries, (keep_out, give_out), states = refs[10:12], refs[12:14], refs[14:16], refs[16]
    x_at, even = place[0], place[1] == 0
    row = lax.broadcasted_iota(jnp.int32, (BLOCK, VCOLS), 0)
    ones = jnp.ones((8, ROWS), jnp.bfloat16)
    states[...] = jnp.zeros_like(states)
    for group in range(2):
        state, conv_out = states.at[group], convs[group]
        turned = [array[...].T * 0.5 for array in query_keys[group]]
        turned = turned[0] if len(turned) == 1 else jnp.concatenate(turned, axis=1)
        queries[group][...] = turned[:QCOLS]
        key = turned[QCOLS:]
        pieces = [
            array[start : start + BLOCK, :]
            for array in values[group]
            for start in range(0, array.shape[0], BLOCK)
        ]

        def line(ref, block, end):
            at = 8 * (1 - group) + 2 * (block % 4) + end
            return ref[at : at + 1, :]

        for number, block in enumerate(SLOTS):
            span = slice(number * BLOCK, (number + 1) * BLOCK)
            mid = pieces[number].astype(jnp.float32)
            opening = jnp.where((x_at + block) % NX == 0, line(far, block - 1, 1), line(near, block - 1, 1))
            before = jnp.where(even, opening, line(near, block, 1))
            closing = jnp.where((x_at + block) % NX == NX - 1, line(far, block + 1, 0), line(near, block + 1, 0))
            after = jnp.where(even, line(near, block, 0), closing)
            low = jnp.where(row == 0, before, pltpu.roll(mid, 1, 0))
            high = jnp.where(row == BLOCK - 1, after, pltpu.roll(mid, BLOCK - 1, 0))
            tap = taps[group]
            conv = tap[0:1, :] * low + tap[1:2, :] * mid + tap[2:3, :] * high
            conv_out[span, :] = conv.astype(jnp.bfloat16)
        for head in range(GROUP):
            feat = features(key[head * FEAT : (head + 1) * FEAT], 1.0).astype(jnp.bfloat16)
            start, stop = window_of(head)
            share = jnp.dot(feat, conv_out[:, start:stop], preferred_element_type=jnp.float32)
            state[:FROWS, start:stop] += jnp.where(head_mask(head, FROWS), share, 0.0)
            total = lax.dot_general(
                ones, feat, (((1,), (1,)), ((), ())), preferred_element_type=jnp.float32
            )
            state[FROWS + head : FROWS + head + 1, :FROWS] = total[0:1]
    same = place[2] == 1
    keep_out[...] = jnp.where(same, states[0], states[1])
    give_out[...] = jnp.where(same, states[1], states[0]).astype(jnp.bfloat16)


def states_of(place, values, query_keys, near, far, taps):
    vmem = pl.BlockSpec(memory_space=pltpu.VMEM)
    return pl.pallas_call(
        state_kernel,
        out_shape=[jax.ShapeDtypeStruct((ROWS, VCOLS), jnp.bfloat16)] * 2
        + [jax.ShapeDtypeStruct((QCOLS, ROWS), jnp.float32)] * 2
        + [
            jax.ShapeDtypeStruct((MROWS, VCOLS), jnp.float32),
            jax.ShapeDtypeStruct((MROWS, VCOLS), jnp.bfloat16),
        ],
        in_specs=[pl.BlockSpec(memory_space=pltpu.SMEM)] + [vmem] * 10,
        out_specs=[vmem] * 6,
        scratch_shapes=[pltpu.VMEM((2, MROWS, VCOLS), jnp.float32)],
        compiler_params=pltpu.CompilerParams(vmem_limit_bytes=VMEM_SMALL),
        cost_estimate=pl.CostEstimate(flops=6 * 10**9, bytes_accessed=8 * 10**6, transcendentals=0),
    )(place, *values, *query_keys, near, far, *taps)


def pack_kernel(start, query, key, value, *refs):
    outs, sems = refs[:-1], refs[-1]
    copies = []
    for index, out in enumerate(outs):
        count = out.shape[0]
        span = pl.ds(pl.multiple_of(start[index], 256), count)
        for kind, (ref, col, width) in enumerate(
            ((query, 0, QCOLS), (key, QCOLS, QCOLS), (value, 2 * QCOLS, VCOLS))
        ):
            copies.append(
                pltpu.make_async_copy(ref.at[span], out.at[:, pl.ds(col, width)], sems.at[index, kind])
            )
    for copy in copies:
        copy.start()
    for copy in copies:
        copy.wait()


def pack(weights, starts, counts):
    hbm = pl.BlockSpec(memory_space=pltpu.HBM)
    return pl.pallas_call(
        pack_kernel,
        out_shape=[jax.ShapeDtypeStruct((count, GCOLS), jnp.bfloat16) for count in counts],
        in_specs=[pl.BlockSpec(memory_space=pltpu.SMEM)] + [hbm] * 3,
        out_specs=[pl.BlockSpec(memory_space=pltpu.VMEM)] * len(counts),
        scratch_shapes=[pltpu.SemaphoreType.DMA((len(counts), 3))],
        compiler_params=pltpu.CompilerParams(vmem_limit_bytes=VMEM_LIMIT),
    )(jnp.stack(starts).astype(jnp.int32), *weights)


def split_kernel(place, keep, got, part_out, *lows):
    for step in range(NY):
        span = pl.ds(pl.multiple_of((place[0] + step) % NY * SPLIT, SPLIT), SPLIT)
        total = keep[span, :] + got[span, :].astype(jnp.float32)
        if step == 0:
            part_out[...] = total
        else:
            lows[step - 1][...] = total.astype(jnp.bfloat16)


def split(place, keep, got):
    vmem = pl.BlockSpec(memory_space=pltpu.VMEM)
    return pl.pallas_call(
        split_kernel,
        out_shape=[jax.ShapeDtypeStruct((SPLIT, VCOLS), jnp.float32)]
        + [jax.ShapeDtypeStruct((SPLIT, VCOLS), jnp.bfloat16)] * 3,
        in_specs=[pl.BlockSpec(memory_space=pltpu.SMEM), vmem, vmem],
        out_specs=[vmem] * 4,
        compiler_params=pltpu.CompilerParams(vmem_limit_bytes=VMEM_SMALL),
    )(place, keep, got)


def join_kernel(place, *refs):
    blocks, out = refs[:NX], refs[NX]
    width = blocks[0].shape[1]
    for step, block in enumerate(blocks):
        span = pl.ds(pl.multiple_of((place[0] + step) % NX * width, 128), width)
        out[:, span] = block[...]


def join(place, blocks):
    vmem = pl.BlockSpec(memory_space=pltpu.VMEM)
    rows, width = blocks[0].shape
    return pl.pallas_call(
        join_kernel,
        out_shape=jax.ShapeDtypeStruct((rows, NX * width), blocks[0].dtype),
        in_specs=[pl.BlockSpec(memory_space=pltpu.SMEM)] + [vmem] * NX,
        out_specs=vmem,
        compiler_params=pltpu.CompilerParams(vmem_limit_bytes=VMEM_SMALL),
    )(place, *blocks)


def attend_kernel(y_place, same, *refs):
    groups = (refs[0:3], refs[3:6])
    mine, theirs = refs[6:10], refs[10:14]
    outs, acc, states = refs[14:18], refs[18], refs[19]
    for step in range(NY):
        span = pl.ds(pl.multiple_of((y_place[0] + step) % NY * SPLIT, SPLIT), SPLIT)
        states[1 - same[0], span, :] = mine[step][...]
        states[same[0], span, :] = theirs[step][...]
    for number, (query, conv, gain) in enumerate(groups):
        state = states.at[number]
        acc[...] = jnp.zeros_like(acc)
        totals = state[FROWS : FROWS + 16, :FROWS]
        for head in range(GROUP):
            feat = features(query[head * FEAT : (head + 1) * FEAT, :], 2.0)
            denom = jnp.dot(totals, feat.astype(jnp.bfloat16), preferred_element_type=jnp.float32)
            scale = 1.0 / denom[head : head + 1, :]
            scaled = (feat * scale).astype(jnp.bfloat16)
            start, stop = window_of(head)
            part = state[:FROWS, start:stop]
            part = jnp.where(head_mask(head, FROWS), part, jnp.zeros_like(part))
            acc[:, start:stop] += lax.dot_general(
                scaled, part, (((0,), (0,)), ((), ())), preferred_element_type=jnp.float32
            )
        low = y_place[0] % 2
        spot = low if number == 0 else 1 - low
        span = pl.ds(pl.multiple_of(spot * VCOLS, VCOLS), VCOLS)
        for block, slot in enumerate(SLOTS):
            rows = slice(block * BLOCK, (block + 1) * BLOCK)
            mixed = acc[rows, :] * gain[3:4, :] + conv[rows, :].astype(jnp.float32)
            outs[slot][:, span] = mixed.astype(jnp.bfloat16)


def attend(y_place, same, groups, mine, theirs):
    vmem = pl.BlockSpec(memory_space=pltpu.VMEM)
    return pl.pallas_call(
        attend_kernel,
        out_shape=[jax.ShapeDtypeStruct((BLOCK, 2 * VCOLS), jnp.bfloat16)] * 4,
        in_specs=[pl.BlockSpec(memory_space=pltpu.SMEM)] * 2 + [vmem] * 14,
        out_specs=[vmem] * 4,
        scratch_shapes=[
            pltpu.VMEM((ROWS, VCOLS), jnp.float32),
            pltpu.VMEM((2, MROWS, VCOLS), jnp.bfloat16),
        ],
        compiler_params=pltpu.CompilerParams(vmem_limit_bytes=VMEM_SMALL),
    )(y_place, same, *[array for group in groups for array in group], *mine, *theirs)


def body(tokens, query_weight, key_weight, value_weight, conv_taps, norm_gain):
    tensor, seq = lax.axis_index("tensor"), lax.axis_index("seq")
    x_at, y_low = tensor // 2, tensor % 2
    core, z_odd = seq % 2, (seq // 2) % 2
    y_at = (seq // 16) * 2 + y_low
    rows = tokens.reshape(BLOCK, tokens.shape[-1])
    weights = (query_weight, key_weight, value_weight)
    half = rows.shape[1] // 2

    y_place = y_at.reshape(1).astype(jnp.int32)
    x_place = x_at.reshape(1).astype(jnp.int32)
    same = (core == y_low).astype(jnp.int32).reshape(1)
    part = BLOCK // 2

    def from_side(array):
        return receive(array, lambda x, y, z, c: (x, y + 2 * c - 1, z, c))

    def from_other(array):
        return receive(array, lambda x, y, z, c: (x, y ^ 1, z, c))

    one = from_x(rows, 1)
    three = from_x(rows, -1)
    two_top = from_x(one[:part], 1)
    two_low = from_x(three[part:], -1)

    base = core * half
    mixed_z = z_odd * 2 * PIECE
    packed = pack(weights, (base + mixed_z, base + mixed_z + PIECE, base + 4 * PIECE), (PIECE,) * 3)
    side = [from_side(array) for array in packed]
    side_z = [receive(array, lambda x, y, z, c: (x, y, z + 2 * c - 1, c)) for array in side[:2]]
    mine = [side[0], side[1], *side_z, side[2]]
    theirs = [from_core(array) for array in mine]
    flip = 2 * PIECE - mixed_z
    steps = jnp.stack([mixed_z, mixed_z + PIECE, flip, flip + PIECE, jnp.full_like(z_odd, 4 * PIECE)])
    offsets = jnp.concatenate([base + steps, (half - base) + steps]).astype(jnp.int32)

    blocks = (rows, one, three, two_top, two_low)
    place = jnp.concatenate([x_place, y_low.reshape(1).astype(jnp.int32), same])
    value_early, query_key_early, edge_early, small = project_early(
        blocks[:3], weights, conv_taps, norm_gain[None]
    )
    small_other = from_other(small)
    value_late, value_other, query_key_late, query_key_other, edge = project(
        offsets, blocks, weights, (*mine, *theirs), edge_early, arrived(two_top, two_low, small_other)
    )
    conv_own, conv_other, query_own, query_other, keep, give = states_of(
        place,
        (value_early, value_late, value_other),
        (query_key_early, query_key_late, query_key_other),
        from_other(edge),
        from_far(edge),
        (small, small_other),
    )

    total, *lows = split(y_place, keep, from_core(give))
    for step, low in zip((1, 2, 3), lows):
        total = total + from_y(low, -step).astype(jnp.float32)
    low = total.astype(jnp.bfloat16)
    for step in (1, -1, 2):
        total = total + from_z(low, step).astype(jnp.float32)
    low = total.astype(jnp.bfloat16)
    quarter = (total + from_z(low, 4).astype(jnp.float32)).astype(jnp.bfloat16)
    mine = [quarter] + [from_y(quarter, step) for step in (1, 2, 3)]
    theirs = [from_core(array) for array in mine]

    out = attend(
        y_place,
        same,
        ((query_own, conv_own, small), (query_other, conv_other, small_other)),
        mine,
        theirs,
    )
    result = join(x_place, [out[0], from_x(out[3], 1), from_x(out[2], 2), from_x(out[1], -1)])
    return result.reshape(tokens.shape)


def solution(mesh):
    return jax.shard_map(
        body,
        mesh=mesh,
        in_specs=(
            P("seq", "tensor", None),
            P(None, "tensor"),
            P(None, "tensor"),
            P(None, "tensor"),
            P(None, "tensor"),
            P("tensor"),
        ),
        out_specs=P("seq", "tensor", None),
        check_vma=False,
    )
```

```python
import functools

import jax
import jax.numpy as jnp
from jax import lax
from jax.experimental import pallas as pl
from jax.experimental.pallas import tpu as pltpu
from jax.sharding import PartitionSpec as P

FEAT = 16
HEAD_DIM = 80
GROUP = 8
NX, NY, NZ = 4, 4, 8
AXES = ("tensor", "seq")
PIECE = 512
PIECES = (PIECE,) * 10
X_AT, Y_LOW, SAME, Y_AT = 10, 11, 12, 13
VMEM_LIMIT = 58 * 1024 * 1024
VMEM_SMALL = 16 * 1024 * 1024
FROWS = 160
MROWS = 192
BLOCK = 128
ROWS = 4 * BLOCK
PARTS = ((4,), (0, 1), (2, 3), (5, 6), (7, 8), (9,))
AHEAD = 2
EARLY = 1024
EARLY_COST = 3 * 10**9
ORDER_COST = 5 * 10**9
SLOTS = (0, 1, 3, 2)
VCOLS = GROUP * HEAD_DIM
QCOLS = GROUP * FEAT
GCOLS = VCOLS + 2 * QCOLS
SPLIT = MROWS // NY


def device_of(x, y, z, core):
    x, y, z = x % NX, y % NY, z % NZ
    tensor = x * 2 + (y & 1)
    seq = ((y >> 1) * NZ + z) * 2 + core
    return tensor * 32 + seq


def everywhere():
    return [
        (x, y, z, core)
        for x in range(NX)
        for y in range(NY)
        for z in range(NZ)
        for core in range(2)
    ]


def receive(array, source_of):
    pairs = [(device_of(*source_of(*place)), device_of(*place)) for place in everywhere()]
    return lax.ppermute(array, AXES, pairs)


def from_x(array, step):
    return receive(array, lambda x, y, z, c: (x + step, y, z, c))


def from_y(array, step):
    return receive(array, lambda x, y, z, c: (x, y + step, z, c))


def from_z(array, step):
    return receive(array, lambda x, y, z, c: (x, y, z + step, c))


def from_core(array):
    return receive(array, lambda x, y, z, c: (x, y, z, 1 - c))


def from_far(array):
    place = {}
    for x, y, z, core in everywhere():
        place[x, y & 1, ((y >> 1) * NZ + z) * 2 + core] = device_of(x, y, z, core)
    pairs = []
    for (x, odd, segment), target in place.items():
        source = place.get((x, 1 - odd, segment + (1 if odd else -1)))
        if source is not None:
            pairs.append((source, target))
    return lax.ppermute(array, AXES, pairs)


def features(scaled, off_weight):
    root = 0.5**0.5
    rows = scaled.shape[1]
    parts = [scaled, scaled * scaled * root]
    for step in range(1, FEAT // 2):
        turned = pltpu.roll(scaled, FEAT - step, 0)
        parts.append(scaled * turned * (root * off_weight))
    half = scaled[: FEAT // 2] * scaled[FEAT // 2 :] * (root * off_weight)
    parts.append(half)
    first = lax.broadcasted_iota(jnp.int32, (FEAT // 2, rows), 0) == 0
    parts.append(jnp.where(first, 1.0, 0.0).astype(jnp.float32))
    return jnp.concatenate(parts, axis=0)


def window_of(head):
    start = head * HEAD_DIM // 128 * 128
    stop = -(-(head + 1) * HEAD_DIM // 128) * 128
    return start, stop


def head_mask(head, rows):
    start, stop = window_of(head)
    lane = lax.broadcasted_iota(jnp.int32, (rows, stop - start), 1) + start
    return (lane >= head * HEAD_DIM) & (lane < (head + 1) * HEAD_DIM)


def early_kernel(counts, idle, *refs):
    refs = list(refs)
    blocks = [refs.pop(0) for _ in counts]
    weights = [refs.pop(0) for _ in range(3)]
    taps, gain = refs.pop(0), refs.pop(0)
    del refs[:idle]
    value_out, query_key_out, edge_out, small_out, xs, ws, acc, xsem, wsem = refs
    small_out[: taps.shape[0], :] = taps[...]
    small_out[taps.shape[0] :, :] = gain[...]

    def copies_of(index):
        span, copies, row = pl.ds(pl.multiple_of(index * EARLY, EARLY), EARLY), [], 0
        for number, (ref, rows) in enumerate(zip(blocks, counts)):
            copies.append(
                pltpu.make_async_copy(ref.at[:, span], xs.at[pl.ds(row, rows), span], xsem.at[index, number])
            )
            row += rows
        for kind, (col, width) in enumerate(((0, QCOLS), (QCOLS, QCOLS), (2 * QCOLS, VCOLS))):
            copies.append(
                pltpu.make_async_copy(
                    weights[kind].at[span], ws.at[span, pl.ds(col, width)], wsem.at[index, kind]
                )
            )
        return copies

    count = xs.shape[1] // EARLY
    for index in range(AHEAD):
        for copy in copies_of(index):
            copy.start()
    acc[...] = jnp.zeros_like(acc)

    def step(index, carry):
        for copy in copies_of(index):
            copy.wait()

        @pl.when(index + AHEAD < count)
        def _():
            for copy in copies_of(index + AHEAD):
                copy.start()

        span = pl.ds(pl.multiple_of(index * EARLY, EARLY), EARLY)
        acc[...] += jnp.dot(xs[:, span], ws[span, :], preferred_element_type=jnp.float32)
        return carry

    lax.fori_loop(0, count, step, 0)
    query_key_out[...] = acc[:, : 2 * QCOLS]
    value_out[...] = acc[:, 2 * QCOLS :].astype(jnp.bfloat16)
    edge_out[...] = jnp.zeros_like(edge_out)
    for block, slot in enumerate(SLOTS[:3]):
        for end, row in ((0, block * BLOCK), (1, block * BLOCK + BLOCK - 1)):
            line = acc[row : row + 1, 2 * QCOLS :]
            edge_out[2 * slot + end : 2 * slot + end + 1, :] = line.astype(jnp.bfloat16).astype(jnp.float32)


def project_early(blocks, weights, taps, gain, after):
    counts = tuple(block.shape[0] for block in blocks)
    depth, rows = blocks[0].shape[1], sum(counts)
    hbm = pl.BlockSpec(memory_space=pltpu.HBM)
    vmem = pl.BlockSpec(memory_space=pltpu.VMEM)
    return pl.pallas_call(
        functools.partial(early_kernel, counts, len(after)),
        out_shape=[
            jax.ShapeDtypeStruct((rows, VCOLS), jnp.bfloat16),
            jax.ShapeDtypeStruct((rows, 2 * QCOLS), jnp.float32),
            jax.ShapeDtypeStruct((8, VCOLS), jnp.float32),
            jax.ShapeDtypeStruct((taps.shape[0] + 1, VCOLS), jnp.float32),
        ],
        in_specs=[hbm] * (len(blocks) + 3) + [vmem] * 2 + [hbm] * len(after),
        out_specs=[vmem] * 4,
        scratch_shapes=[
            pltpu.VMEM((rows, depth), jnp.bfloat16),
            pltpu.VMEM((depth, GCOLS), jnp.bfloat16),
            pltpu.VMEM((rows, GCOLS), jnp.float32),
            pltpu.SemaphoreType.DMA((depth // EARLY, len(blocks))),
            pltpu.SemaphoreType.DMA((depth // EARLY, 3)),
        ],
        compiler_params=pltpu.CompilerParams(vmem_limit_bytes=VMEM_LIMIT),
        cost_estimate=pl.CostEstimate(flops=EARLY_COST, bytes_accessed=EARLY_COST // 1000, transcendentals=0),
    )(*blocks, *weights, taps, gain, *after)


def project_kernel(counts, offsets, *refs):
    refs = list(refs)
    blocks = [refs.pop(0) for _ in counts]
    weights = [refs.pop(0) for _ in range(3)]
    pieces = [refs.pop(0) for _ in PIECES]
    edge_early = refs.pop(0)
    refs.pop(0)
    value_outs, query_key_outs, edge_out = refs[0:2], refs[2:4], refs[4]
    xs, ws, acc, late, xsem, wsem, psem = refs[5:]
    stages, at = [], 0
    for index, members in enumerate(PARTS):
        count = len(members) * PIECE
        start = pl.multiple_of(offsets[members[0]], PIECE)
        copies, row = [], 0
        for number, (ref, rows) in enumerate(zip(blocks, counts)):
            copies.append(
                pltpu.make_async_copy(
                    ref.at[:, pl.ds(start, count)],
                    xs.at[pl.ds(row, rows), pl.ds(at, count)],
                    xsem.at[index, number],
                )
            )
            row += rows
        for kind, (col, width) in enumerate(((0, QCOLS), (QCOLS, QCOLS), (2 * QCOLS, VCOLS))):
            copies.append(
                pltpu.make_async_copy(
                    weights[kind].at[pl.ds(start, count)],
                    ws.at[pl.ds(at, count), pl.ds(col, width)],
                    wsem.at[index, kind],
                )
            )
        for step, member in enumerate(members):
            copies.append(
                pltpu.make_async_copy(
                    pieces[member],
                    ws.at[pl.ds(at + step * PIECE, PIECE), pl.ds(GCOLS, GCOLS)],
                    psem.at[member],
                )
            )
        stages.append((copies, at, count))
        at += count
    for copies, _, _ in stages[:AHEAD]:
        for copy in copies:
            copy.start()
    for index, (copies, at, count) in enumerate(stages):
        for copy in copies:
            copy.wait()
        if index + AHEAD < len(stages):
            for copy in stages[index + AHEAD][0]:
                copy.start()
        span = slice(at, at + count)
        part = jnp.dot(xs[:, span], ws[span, GCOLS:], preferred_element_type=jnp.float32)
        last = jnp.dot(xs[ROWS - BLOCK :, span], ws[span, :GCOLS], preferred_element_type=jnp.float32)
        if index == 0:
            acc[...] = part
            late[...] = last
        else:
            acc[...] += part
            late[...] += last
    edge_out[:8, :] = edge_early[...]
    for group, (total, slots) in enumerate(((late, SLOTS[3:]), (acc, SLOTS))):
        query_key_outs[group][...] = total[:, : 2 * QCOLS]
        value_outs[group][...] = total[:, 2 * QCOLS :].astype(jnp.bfloat16)
        for block, slot in enumerate(slots):
            for end, row in ((0, block * BLOCK), (1, block * BLOCK + BLOCK - 1)):
                line = total[row : row + 1, 2 * QCOLS :]
                at = 8 * group + 2 * slot + end
                edge_out[at : at + 1, :] = line.astype(jnp.bfloat16).astype(jnp.float32)


def project(offsets, blocks, weights, pieces, edge_early, after):
    counts = tuple(block.shape[0] for block in blocks)
    depth = blocks[0].shape[1]
    hbm = pl.BlockSpec(memory_space=pltpu.HBM)
    vmem = pl.BlockSpec(memory_space=pltpu.VMEM)
    return pl.pallas_call(
        functools.partial(project_kernel, counts),
        out_shape=[jax.ShapeDtypeStruct((rows, VCOLS), jnp.bfloat16) for rows in (BLOCK, ROWS)]
        + [jax.ShapeDtypeStruct((rows, 2 * QCOLS), jnp.float32) for rows in (BLOCK, ROWS)]
        + [jax.ShapeDtypeStruct((16, VCOLS), jnp.float32)],
        in_specs=[pl.BlockSpec(memory_space=pltpu.SMEM)] + [hbm] * (len(blocks) + 3 + len(pieces)) + [vmem, hbm],
        out_specs=[vmem] * 5,
        scratch_shapes=[
            pltpu.VMEM((ROWS, depth), jnp.bfloat16),
            pltpu.VMEM((depth, 2 * GCOLS), jnp.bfloat16),
            pltpu.VMEM((ROWS, GCOLS), jnp.float32),
            pltpu.VMEM((BLOCK, GCOLS), jnp.float32),
            pltpu.SemaphoreType.DMA((len(PARTS), len(blocks))),
            pltpu.SemaphoreType.DMA((len(PARTS), 3)),
            pltpu.SemaphoreType.DMA((len(pieces),)),
        ],
        compiler_params=pltpu.CompilerParams(vmem_limit_bytes=VMEM_LIMIT),
        cost_estimate=pl.CostEstimate(
            flops=3 * ROWS * depth * GCOLS, bytes_accessed=2 * depth * (ROWS + 2 * GCOLS), transcendentals=0
        ),
    )(offsets, *blocks, *weights, *pieces, edge_early, after)


def order_kernel(top, low, early, out):
    del top, low, early
    out[...] = jnp.zeros_like(out)


def arrived(top, low, early):
    hbm = pl.BlockSpec(memory_space=pltpu.HBM)
    return pl.pallas_call(
        order_kernel,
        out_shape=jax.ShapeDtypeStruct((8, 128), jnp.float32),
        in_specs=[hbm] * 3,
        out_specs=pl.BlockSpec(memory_space=pltpu.VMEM),
        compiler_params=pltpu.CompilerParams(vmem_limit_bytes=VMEM_LIMIT),
        cost_estimate=pl.CostEstimate(flops=ORDER_COST, bytes_accessed=15 * 10**6, transcendentals=0),
    )(top, low, early)


def state_kernel(place, *refs):
    values, query_keys = ((refs[0], refs[1]), (refs[2],)), ((refs[3], refs[4]), (refs[5],))
    (near, far), taps = refs[6:8], refs[8:10]
    convs, queries, (keep_out, give_out), states = refs[10:12], refs[12:14], refs[14:16], refs[16]
    x_at, even = place[X_AT], place[Y_LOW] == 0
    row = lax.broadcasted_iota(jnp.int32, (BLOCK, VCOLS), 0)
    ones = jnp.ones((8, ROWS), jnp.bfloat16)
    states[...] = jnp.zeros_like(states)
    for group in range(2):
        state, conv_out = states.at[group], convs[group]
        turned = [array[...].T * 0.5 for array in query_keys[group]]
        turned = turned[0] if len(turned) == 1 else jnp.concatenate(turned, axis=1)
        queries[group][...] = turned[:QCOLS]
        key = turned[QCOLS:]
        pieces = [
            array[start : start + BLOCK, :]
            for array in values[group]
            for start in range(0, array.shape[0], BLOCK)
        ]

        def line(ref, block, end):
            at = 8 * (1 - group) + 2 * (block % 4) + end
            return ref[at : at + 1, :]

        for number, block in enumerate(SLOTS):
            span = slice(number * BLOCK, (number + 1) * BLOCK)
            mid = pieces[number].astype(jnp.float32)
            opening = jnp.where((x_at + block) % NX == 0, line(far, block - 1, 1), line(near, block - 1, 1))
            before = jnp.where(even, opening, line(near, block, 1))
            closing = jnp.where((x_at + block) % NX == NX - 1, line(far, block + 1, 0), line(near, block + 1, 0))
            after = jnp.where(even, line(near, block, 0), closing)
            low = jnp.where(row == 0, before, pltpu.roll(mid, 1, 0))
            high = jnp.where(row == BLOCK - 1, after, pltpu.roll(mid, BLOCK - 1, 0))
            tap = taps[group]
            conv = tap[0:1, :] * low + tap[1:2, :] * mid + tap[2:3, :] * high
            conv_out[span, :] = conv.astype(jnp.bfloat16)
        for head in range(GROUP):
            feat = features(key[head * FEAT : (head + 1) * FEAT], 1.0).astype(jnp.bfloat16)
            start, stop = window_of(head)
            share = jnp.dot(feat, conv_out[:, start:stop], preferred_element_type=jnp.float32)
            state[:FROWS, start:stop] += jnp.where(head_mask(head, FROWS), share, 0.0)
            total = lax.dot_general(
                ones, feat, (((1,), (1,)), ((), ())), preferred_element_type=jnp.float32
            )
            state[FROWS + head : FROWS + head + 1, :FROWS] = total[0:1]
    same = place[SAME] == 1
    keep_out[...] = jnp.where(same, states[0], states[1])
    give_out[...] = jnp.where(same, states[1], states[0]).astype(jnp.bfloat16)


def states_of(place, values, query_keys, near, far, taps):
    vmem = pl.BlockSpec(memory_space=pltpu.VMEM)
    return pl.pallas_call(
        state_kernel,
        out_shape=[jax.ShapeDtypeStruct((ROWS, VCOLS), jnp.bfloat16)] * 2
        + [jax.ShapeDtypeStruct((QCOLS, ROWS), jnp.float32)] * 2
        + [
            jax.ShapeDtypeStruct((MROWS, VCOLS), jnp.float32),
            jax.ShapeDtypeStruct((MROWS, VCOLS), jnp.bfloat16),
        ],
        in_specs=[pl.BlockSpec(memory_space=pltpu.SMEM)] + [vmem] * 10,
        out_specs=[vmem] * 6,
        scratch_shapes=[pltpu.VMEM((2, MROWS, VCOLS), jnp.float32)],
        compiler_params=pltpu.CompilerParams(vmem_limit_bytes=VMEM_SMALL),
        cost_estimate=pl.CostEstimate(flops=6 * 10**9, bytes_accessed=8 * 10**6, transcendentals=0),
    )(place, *values, *query_keys, near, far, *taps)


def pack_kernel(members, control, query, key, value, *refs):
    outs, sems = refs[:-1], refs[-1]
    copies = []
    for index, out in enumerate(outs):
        count = out.shape[0]
        span = pl.ds(pl.multiple_of(control[members[index]], 512), count)
        for kind, (ref, col, width) in enumerate(
            ((query, 0, QCOLS), (key, QCOLS, QCOLS), (value, 2 * QCOLS, VCOLS))
        ):
            copies.append(
                pltpu.make_async_copy(ref.at[span], out.at[:, pl.ds(col, width)], sems.at[index, kind])
            )
    for copy in copies:
        copy.start()
    for copy in copies:
        copy.wait()


def pack(control, weights, members):
    counts = [PIECES[member] for member in members]
    hbm = pl.BlockSpec(memory_space=pltpu.HBM)
    return pl.pallas_call(
        functools.partial(pack_kernel, members),
        out_shape=[jax.ShapeDtypeStruct((count, GCOLS), jnp.bfloat16) for count in counts],
        in_specs=[pl.BlockSpec(memory_space=pltpu.SMEM)] + [hbm] * 3,
        out_specs=[pl.BlockSpec(memory_space=pltpu.VMEM)] * len(counts),
        scratch_shapes=[pltpu.SemaphoreType.DMA((len(counts), 3))],
        compiler_params=pltpu.CompilerParams(vmem_limit_bytes=VMEM_LIMIT),
    )(control, *weights)


def split_kernel(place, keep, got, part_out, *lows):
    for step in range(NY):
        span = pl.ds(pl.multiple_of((place[Y_AT] + step) % NY * SPLIT, SPLIT), SPLIT)
        total = keep[span, :] + got[span, :].astype(jnp.float32)
        if step == 0:
            part_out[...] = total
        else:
            lows[step - 1][...] = total.astype(jnp.bfloat16)


def split(place, keep, got):
    vmem = pl.BlockSpec(memory_space=pltpu.VMEM)
    return pl.pallas_call(
        split_kernel,
        out_shape=[jax.ShapeDtypeStruct((SPLIT, VCOLS), jnp.float32)]
        + [jax.ShapeDtypeStruct((SPLIT, VCOLS), jnp.bfloat16)] * 3,
        in_specs=[pl.BlockSpec(memory_space=pltpu.SMEM), vmem, vmem],
        out_specs=[vmem] * 4,
        compiler_params=pltpu.CompilerParams(vmem_limit_bytes=VMEM_SMALL),
    )(place, keep, got)


def join_kernel(place, *refs):
    blocks, out = refs[:NX], refs[NX]
    width = blocks[0].shape[1]
    for step, block in enumerate(blocks):
        span = pl.ds(pl.multiple_of((place[X_AT] + step) % NX * width, 128), width)
        out[:, span] = block[...]


def join(place, blocks):
    vmem = pl.BlockSpec(memory_space=pltpu.VMEM)
    rows, width = blocks[0].shape
    return pl.pallas_call(
        join_kernel,
        out_shape=jax.ShapeDtypeStruct((rows, NX * width), blocks[0].dtype),
        in_specs=[pl.BlockSpec(memory_space=pltpu.SMEM)] + [vmem] * NX,
        out_specs=vmem,
        compiler_params=pltpu.CompilerParams(vmem_limit_bytes=VMEM_SMALL),
    )(place, *blocks)


def attend_kernel(place, *refs):
    groups = (refs[0:3], refs[3:6])
    mine, theirs = refs[6:10], refs[10:14]
    outs, acc, states = refs[14:18], refs[18], refs[19]
    for step in range(NY):
        span = pl.ds(pl.multiple_of((place[Y_AT] + step) % NY * SPLIT, SPLIT), SPLIT)
        states[1 - place[SAME], span, :] = mine[step][...]
        states[place[SAME], span, :] = theirs[step][...]
    for number, (query, conv, gain) in enumerate(groups):
        state = states.at[number]
        acc[...] = jnp.zeros_like(acc)
        totals = state[FROWS : FROWS + 16, :FROWS]
        for head in range(GROUP):
            feat = features(query[head * FEAT : (head + 1) * FEAT, :], 2.0)
            denom = jnp.dot(totals, feat.astype(jnp.bfloat16), preferred_element_type=jnp.float32)
            scale = 1.0 / denom[head : head + 1, :]
            scaled = (feat * scale).astype(jnp.bfloat16)
            start, stop = window_of(head)
            part = state[:FROWS, start:stop]
            part = jnp.where(head_mask(head, FROWS), part, jnp.zeros_like(part))
            acc[:, start:stop] += lax.dot_general(
                scaled, part, (((0,), (0,)), ((), ())), preferred_element_type=jnp.float32
            )
        low = place[Y_LOW]
        spot = low if number == 0 else 1 - low
        span = pl.ds(pl.multiple_of(spot * VCOLS, VCOLS), VCOLS)
        for block, slot in enumerate(SLOTS):
            rows = slice(block * BLOCK, (block + 1) * BLOCK)
            mixed = acc[rows, :] * gain[3:4, :] + conv[rows, :].astype(jnp.float32)
            outs[slot][:, span] = mixed.astype(jnp.bfloat16)


def attend(place, groups, mine, theirs):
    vmem = pl.BlockSpec(memory_space=pltpu.VMEM)
    return pl.pallas_call(
        attend_kernel,
        out_shape=[jax.ShapeDtypeStruct((BLOCK, 2 * VCOLS), jnp.bfloat16)] * 4,
        in_specs=[pl.BlockSpec(memory_space=pltpu.SMEM)] + [vmem] * 14,
        out_specs=[vmem] * 4,
        scratch_shapes=[
            pltpu.VMEM((ROWS, VCOLS), jnp.float32),
            pltpu.VMEM((2, MROWS, VCOLS), jnp.bfloat16),
        ],
        compiler_params=pltpu.CompilerParams(vmem_limit_bytes=VMEM_SMALL),
    )(place, *[array for group in groups for array in group], *mine, *theirs)


def body(tokens, query_weight, key_weight, value_weight, conv_taps, norm_gain):
    tensor, seq = lax.axis_index("tensor"), lax.axis_index("seq")
    x_at, y_low = tensor // 2, tensor % 2
    core, z_odd = seq % 2, (seq // 2) % 2
    y_at = (seq // 16) * 2 + y_low
    rows = tokens.reshape(BLOCK, tokens.shape[-1])
    weights = (query_weight, key_weight, value_weight)
    half = rows.shape[1] // 2

    base = core * half
    mixed_z = z_odd * 2 * PIECE
    flip = 2 * PIECE - mixed_z
    parts = (mixed_z, mixed_z + PIECE, flip, flip + PIECE, jnp.full_like(z_odd, 4 * PIECE))
    control = jnp.stack(
        [start + shift for start in (base, half - base) for shift in parts]
        + [x_at, y_low, (core == y_low).astype(x_at.dtype), y_at]
    ).astype(jnp.int32)
    part = BLOCK // 2

    def from_side(array):
        return receive(array, lambda x, y, z, c: (x, y + 2 * c - 1, z, c))

    def from_other(array):
        return receive(array, lambda x, y, z, c: (x, y ^ 1, z, c))

    one = from_x(rows, 1)
    three = from_x(rows, -1)
    two_top = from_x(one[:part], 1)
    two_low = from_x(three[part:], -1)

    packed = pack(control, weights, (0, 1, 4))
    side = [from_side(array) for array in packed]
    side_z = [receive(array, lambda x, y, z, c: (x, y, z + 2 * c - 1, c)) for array in side[:2]]
    mine = [side[0], side[1], *side_z, side[2]]
    theirs = [from_core(array) for array in mine]

    blocks = (rows, one, three, two_top, two_low)
    value_early, query_key_early, edge_early, small = project_early(
        blocks[:3], weights, conv_taps, norm_gain[None], (theirs[0], theirs[1])
    )
    small_other = from_other(small)
    value_late, value_other, query_key_late, query_key_other, edge = project(
        control, blocks, weights, (*mine, *theirs), edge_early, arrived(two_top, two_low, small_other)
    )
    conv_own, conv_other, query_own, query_other, keep, give = states_of(
        control,
        (value_early, value_late, value_other),
        (query_key_early, query_key_late, query_key_other),
        from_other(edge),
        from_far(edge),
        (small, small_other),
    )

    total, *lows = split(control, keep, from_core(give))
    for step, low in zip((1, 2, 3), lows):
        total = total + from_y(low, -step).astype(jnp.float32)
    low = total.astype(jnp.bfloat16)
    for step in (1, -1, 2):
        total = total + from_z(low, step).astype(jnp.float32)
    low = total.astype(jnp.bfloat16)
    quarter = (total + from_z(low, 4).astype(jnp.float32)).astype(jnp.bfloat16)
    mine = [quarter] + [from_y(quarter, step) for step in (1, 2, 3)]
    theirs = [from_core(array) for array in mine]

    out = attend(
        control,
        ((query_own, conv_own, small), (query_other, conv_other, small_other)),
        mine,
        theirs,
    )
    result = join(control, [out[0], from_x(out[3], 1), from_x(out[2], 2), from_x(out[1], -1)])
    return result.reshape(tokens.shape)


def solution(mesh):
    return jax.shard_map(
        body,
        mesh=mesh,
        in_specs=(
            P("seq", "tensor", None),
            P(None, "tensor"),
            P(None, "tensor"),
            P(None, "tensor"),
            P(None, "tensor"),
            P("tensor"),
        ),
        out_specs=P("seq", "tensor", None),
        check_vma=False,
    )
```

```python
import functools

import jax
import jax.numpy as jnp
from jax import lax
from jax.experimental import pallas as pl
from jax.experimental.pallas import tpu as pltpu
from jax.sharding import PartitionSpec as P

FEAT = 16
HEAD_DIM = 80
GROUP = 8
NX, NY, NZ = 4, 4, 8
AXES = ("tensor", "seq")
PIECE = 512
PIECES = (PIECE,) * 10
X_AT, Y_LOW, SAME, Y_AT = 10, 11, 12, 13
VMEM_LIMIT = 58 * 1024 * 1024
VMEM_LATE = 44 * 1024 * 1024
VMEM_SMALL = 16 * 1024 * 1024
FROWS = 160
MROWS = 192
BLOCK = 128
ROWS = 4 * BLOCK
PARTS = ((4,), (0, 1), (2, 3), (5, 6), (7, 8), (9,))
AHEAD = 2
EARLY = 1024
EARLY_COST = 3 * 10**9
ORDER_COST = 5 * 10**9
SLOTS = (0, 1, 3, 2)
VCOLS = GROUP * HEAD_DIM
QCOLS = GROUP * FEAT
GCOLS = VCOLS + 2 * QCOLS
SPLIT = MROWS // NY


def device_of(x, y, z, core):
    x, y, z = x % NX, y % NY, z % NZ
    tensor = x * 2 + (y & 1)
    seq = ((y >> 1) * NZ + z) * 2 + core
    return tensor * 32 + seq


def everywhere():
    return [
        (x, y, z, core)
        for x in range(NX)
        for y in range(NY)
        for z in range(NZ)
        for core in range(2)
    ]


def receive(array, source_of):
    pairs = [(device_of(*source_of(*place)), device_of(*place)) for place in everywhere()]
    return lax.ppermute(array, AXES, pairs)


def from_x(array, step):
    return receive(array, lambda x, y, z, c: (x + step, y, z, c))


def from_y(array, step):
    return receive(array, lambda x, y, z, c: (x, y + step, z, c))


def from_z(array, step):
    return receive(array, lambda x, y, z, c: (x, y, z + step, c))


def from_core(array):
    return receive(array, lambda x, y, z, c: (x, y, z, 1 - c))


def from_far(array):
    place = {}
    for x, y, z, core in everywhere():
        place[x, y & 1, ((y >> 1) * NZ + z) * 2 + core] = device_of(x, y, z, core)
    pairs = []
    for (x, odd, segment), target in place.items():
        source = place.get((x, 1 - odd, segment + (1 if odd else -1)))
        if source is not None:
            pairs.append((source, target))
    return lax.ppermute(array, AXES, pairs)


def features(scaled, off_weight):
    root = 0.5**0.5
    rows = scaled.shape[1]
    parts = [scaled, scaled * scaled * root]
    for step in range(1, FEAT // 2):
        turned = pltpu.roll(scaled, FEAT - step, 0)
        parts.append(scaled * turned * (root * off_weight))
    half = scaled[: FEAT // 2] * scaled[FEAT // 2 :] * (root * off_weight)
    parts.append(half)
    first = lax.broadcasted_iota(jnp.int32, (FEAT // 2, rows), 0) == 0
    parts.append(jnp.where(first, 1.0, 0.0).astype(jnp.float32))
    return jnp.concatenate(parts, axis=0)


def window_of(head):
    start = head * HEAD_DIM // 128 * 128
    stop = -(-(head + 1) * HEAD_DIM // 128) * 128
    return start, stop


def head_mask(head, rows):
    start, stop = window_of(head)
    lane = lax.broadcasted_iota(jnp.int32, (rows, stop - start), 1) + start
    return (lane >= head * HEAD_DIM) & (lane < (head + 1) * HEAD_DIM)


def early_kernel(counts, idle, *refs):
    refs = list(refs)
    blocks = [refs.pop(0) for _ in counts]
    weights = [refs.pop(0) for _ in range(3)]
    taps, gain = refs.pop(0), refs.pop(0)
    del refs[:idle]
    value_out, query_key_out, edge_out, small_out, xs, ws, acc, xsem, wsem = refs
    small_out[: taps.shape[0], :] = taps[...]
    small_out[taps.shape[0] :, :] = gain[...]

    def copies_of(index):
        span, copies, row = pl.ds(pl.multiple_of(index * EARLY, EARLY), EARLY), [], 0
        for number, (ref, rows) in enumerate(zip(blocks, counts)):
            copies.append(
                pltpu.make_async_copy(ref.at[:, span], xs.at[pl.ds(row, rows), span], xsem.at[index, number])
            )
            row += rows
        for kind, (col, width) in enumerate(((0, QCOLS), (QCOLS, QCOLS), (2 * QCOLS, VCOLS))):
            copies.append(
                pltpu.make_async_copy(
                    weights[kind].at[span], ws.at[span, pl.ds(col, width)], wsem.at[index, kind]
                )
            )
        return copies

    count = xs.shape[1] // EARLY
    for index in range(AHEAD):
        for copy in copies_of(index):
            copy.start()
    acc[...] = jnp.zeros_like(acc)

    def step(index, carry):
        for copy in copies_of(index):
            copy.wait()

        @pl.when(index + AHEAD < count)
        def _():
            for copy in copies_of(index + AHEAD):
                copy.start()

        span = pl.ds(pl.multiple_of(index * EARLY, EARLY), EARLY)
        acc[...] += jnp.dot(xs[:, span], ws[span, :], preferred_element_type=jnp.float32)
        return carry

    lax.fori_loop(0, count, step, 0)
    query_key_out[...] = acc[:, : 2 * QCOLS]
    value_out[...] = acc[:, 2 * QCOLS :].astype(jnp.bfloat16)
    edge_out[...] = jnp.zeros_like(edge_out)
    for block, slot in enumerate(SLOTS[:3]):
        for end, row in ((0, block * BLOCK), (1, block * BLOCK + BLOCK - 1)):
            line = acc[row : row + 1, 2 * QCOLS :]
            edge_out[2 * slot + end : 2 * slot + end + 1, :] = line.astype(jnp.bfloat16).astype(jnp.float32)


def project_early(blocks, weights, taps, gain, after):
    counts = tuple(block.shape[0] for block in blocks)
    depth, rows = blocks[0].shape[1], sum(counts)
    hbm = pl.BlockSpec(memory_space=pltpu.HBM)
    vmem = pl.BlockSpec(memory_space=pltpu.VMEM)
    return pl.pallas_call(
        functools.partial(early_kernel, counts, len(after)),
        out_shape=[
            jax.ShapeDtypeStruct((rows, VCOLS), jnp.bfloat16),
            jax.ShapeDtypeStruct((rows, 2 * QCOLS), jnp.float32),
            jax.ShapeDtypeStruct((8, VCOLS), jnp.float32),
            jax.ShapeDtypeStruct((taps.shape[0] + 1, VCOLS), jnp.float32),
        ],
        in_specs=[hbm] * (len(blocks) + 3) + [vmem] * 2 + [hbm] * len(after),
        out_specs=[vmem] * 4,
        scratch_shapes=[
            pltpu.VMEM((rows, depth), jnp.bfloat16),
            pltpu.VMEM((depth, GCOLS), jnp.bfloat16),
            pltpu.VMEM((rows, GCOLS), jnp.float32),
            pltpu.SemaphoreType.DMA((depth // EARLY, len(blocks))),
            pltpu.SemaphoreType.DMA((depth // EARLY, 3)),
        ],
        compiler_params=pltpu.CompilerParams(vmem_limit_bytes=VMEM_LIMIT),
        cost_estimate=pl.CostEstimate(flops=EARLY_COST, bytes_accessed=EARLY_COST // 1000, transcendentals=0),
    )(*blocks, *weights, taps, gain, *after)


def project_kernel(counts, offsets, *refs):
    refs = list(refs)
    blocks = [refs.pop(0) for _ in counts]
    weights = [refs.pop(0) for _ in range(3)]
    pieces = [refs.pop(0) for _ in PIECES]
    edge_early = refs.pop(0)
    refs.pop(0)
    value_outs, query_key_outs, edge_out = refs[0:2], refs[2:4], refs[4]
    xs, ws, acc, late, xsem, wsem, psem = refs[5:]
    stages, at = [], 0
    for index, members in enumerate(PARTS):
        count = len(members) * PIECE
        start = pl.multiple_of(offsets[members[0]], PIECE)
        copies, row = [], 0
        for number, (ref, rows) in enumerate(zip(blocks, counts)):
            copies.append(
                pltpu.make_async_copy(
                    ref.at[:, pl.ds(start, count)],
                    xs.at[pl.ds(row, rows), pl.ds(at, count)],
                    xsem.at[index, number],
                )
            )
            row += rows
        for kind, (col, width) in enumerate(((0, QCOLS), (QCOLS, QCOLS), (2 * QCOLS, VCOLS))):
            copies.append(
                pltpu.make_async_copy(
                    weights[kind].at[pl.ds(start, count)],
                    ws.at[pl.ds(at, count), pl.ds(col, width)],
                    wsem.at[index, kind],
                )
            )
        for step, member in enumerate(members):
            copies.append(
                pltpu.make_async_copy(
                    pieces[member],
                    ws.at[pl.ds(at + step * PIECE, PIECE), pl.ds(GCOLS, GCOLS)],
                    psem.at[member],
                )
            )
        stages.append((copies, at, count))
        at += count
    for copies, _, _ in stages[:AHEAD]:
        for copy in copies:
            copy.start()
    for index, (copies, at, count) in enumerate(stages):
        for copy in copies:
            copy.wait()
        if index + AHEAD < len(stages):
            for copy in stages[index + AHEAD][0]:
                copy.start()
        span = slice(at, at + count)
        part = jnp.dot(xs[:, span], ws[span, GCOLS:], preferred_element_type=jnp.float32)
        last = jnp.dot(xs[ROWS - BLOCK :, span], ws[span, :GCOLS], preferred_element_type=jnp.float32)
        if index == 0:
            acc[...] = part
            late[...] = last
        else:
            acc[...] += part
            late[...] += last
    edge_out[:8, :] = edge_early[...]
    for group, (total, slots) in enumerate(((late, SLOTS[3:]), (acc, SLOTS))):
        query_key_outs[group][...] = total[:, : 2 * QCOLS]
        value_outs[group][...] = total[:, 2 * QCOLS :].astype(jnp.bfloat16)
        for block, slot in enumerate(slots):
            for end, row in ((0, block * BLOCK), (1, block * BLOCK + BLOCK - 1)):
                line = total[row : row + 1, 2 * QCOLS :]
                at = 8 * group + 2 * slot + end
                edge_out[at : at + 1, :] = line.astype(jnp.bfloat16).astype(jnp.float32)


def project(offsets, blocks, weights, pieces, edge_early, after):
    counts = tuple(block.shape[0] for block in blocks)
    depth = blocks[0].shape[1]
    hbm = pl.BlockSpec(memory_space=pltpu.HBM)
    vmem = pl.BlockSpec(memory_space=pltpu.VMEM)
    return pl.pallas_call(
        functools.partial(project_kernel, counts),
        out_shape=[jax.ShapeDtypeStruct((rows, VCOLS), jnp.bfloat16) for rows in (BLOCK, ROWS)]
        + [jax.ShapeDtypeStruct((rows, 2 * QCOLS), jnp.float32) for rows in (BLOCK, ROWS)]
        + [jax.ShapeDtypeStruct((16, VCOLS), jnp.float32)],
        in_specs=[pl.BlockSpec(memory_space=pltpu.SMEM)] + [hbm] * (len(blocks) + 3 + len(pieces)) + [vmem, hbm],
        out_specs=[vmem] * 5,
        scratch_shapes=[
            pltpu.VMEM((ROWS, depth), jnp.bfloat16),
            pltpu.VMEM((depth, 2 * GCOLS), jnp.bfloat16),
            pltpu.VMEM((ROWS, GCOLS), jnp.float32),
            pltpu.VMEM((BLOCK, GCOLS), jnp.float32),
            pltpu.SemaphoreType.DMA((len(PARTS), len(blocks))),
            pltpu.SemaphoreType.DMA((len(PARTS), 3)),
            pltpu.SemaphoreType.DMA((len(pieces),)),
        ],
        compiler_params=pltpu.CompilerParams(vmem_limit_bytes=VMEM_LATE),
        cost_estimate=pl.CostEstimate(
            flops=3 * ROWS * depth * GCOLS, bytes_accessed=2 * depth * (ROWS + 2 * GCOLS), transcendentals=0
        ),
    )(offsets, *blocks, *weights, *pieces, edge_early, after)


def order_kernel(top, low, early, out):
    del top, low, early
    out[...] = jnp.zeros_like(out)


def arrived(top, low, early):
    hbm = pl.BlockSpec(memory_space=pltpu.HBM)
    return pl.pallas_call(
        order_kernel,
        out_shape=jax.ShapeDtypeStruct((8, 128), jnp.float32),
        in_specs=[hbm] * 3,
        out_specs=pl.BlockSpec(memory_space=pltpu.VMEM),
        compiler_params=pltpu.CompilerParams(vmem_limit_bytes=VMEM_LIMIT),
        cost_estimate=pl.CostEstimate(flops=ORDER_COST, bytes_accessed=15 * 10**6, transcendentals=0),
    )(top, low, early)


def state_kernel(place, *refs):
    values, query_keys = ((refs[0], refs[1]), (refs[2],)), ((refs[3], refs[4]), (refs[5],))
    (near, far), taps = refs[6:8], refs[8:10]
    convs, queries, (keep_out, give_out), states = refs[10:12], refs[12:14], refs[14:16], refs[16]
    x_at, even = place[X_AT], place[Y_LOW] == 0
    row = lax.broadcasted_iota(jnp.int32, (BLOCK, VCOLS), 0)
    ones = jnp.ones((8, ROWS), jnp.bfloat16)
    states[...] = jnp.zeros_like(states)
    for group in range(2):
        state, conv_out = states.at[group], convs[group]
        turned = [array[...].T * 0.5 for array in query_keys[group]]
        turned = turned[0] if len(turned) == 1 else jnp.concatenate(turned, axis=1)
        queries[group][...] = turned[:QCOLS]
        key = turned[QCOLS:]
        pieces = [
            array[start : start + BLOCK, :]
            for array in values[group]
            for start in range(0, array.shape[0], BLOCK)
        ]

        def line(ref, block, end):
            at = 8 * (1 - group) + 2 * (block % 4) + end
            return ref[at : at + 1, :]

        for number, block in enumerate(SLOTS):
            span = slice(number * BLOCK, (number + 1) * BLOCK)
            mid = pieces[number].astype(jnp.float32)
            opening = jnp.where((x_at + block) % NX == 0, line(far, block - 1, 1), line(near, block - 1, 1))
            before = jnp.where(even, opening, line(near, block, 1))
            closing = jnp.where((x_at + block) % NX == NX - 1, line(far, block + 1, 0), line(near, block + 1, 0))
            after = jnp.where(even, line(near, block, 0), closing)
            low = jnp.where(row == 0, before, pltpu.roll(mid, 1, 0))
            high = jnp.where(row == BLOCK - 1, after, pltpu.roll(mid, BLOCK - 1, 0))
            tap = taps[group]
            conv = tap[0:1, :] * low + tap[1:2, :] * mid + tap[2:3, :] * high
            conv_out[span, :] = conv.astype(jnp.bfloat16)
        for head in range(GROUP):
            feat = features(key[head * FEAT : (head + 1) * FEAT], 1.0).astype(jnp.bfloat16)
            start, stop = window_of(head)
            share = jnp.dot(feat, conv_out[:, start:stop], preferred_element_type=jnp.float32)
            state[:FROWS, start:stop] += jnp.where(head_mask(head, FROWS), share, 0.0)
            total = lax.dot_general(
                ones, feat, (((1,), (1,)), ((), ())), preferred_element_type=jnp.float32
            )
            state[FROWS + head : FROWS + head + 1, :FROWS] = total[0:1]
    same = place[SAME] == 1
    keep_out[...] = jnp.where(same, states[0], states[1])
    give_out[...] = jnp.where(same, states[1], states[0]).astype(jnp.bfloat16)


def states_of(place, values, query_keys, near, far, taps):
    vmem = pl.BlockSpec(memory_space=pltpu.VMEM)
    return pl.pallas_call(
        state_kernel,
        out_shape=[jax.ShapeDtypeStruct((ROWS, VCOLS), jnp.bfloat16)] * 2
        + [jax.ShapeDtypeStruct((QCOLS, ROWS), jnp.float32)] * 2
        + [
            jax.ShapeDtypeStruct((MROWS, VCOLS), jnp.float32),
            jax.ShapeDtypeStruct((MROWS, VCOLS), jnp.bfloat16),
        ],
        in_specs=[pl.BlockSpec(memory_space=pltpu.SMEM)] + [vmem] * 10,
        out_specs=[vmem] * 6,
        scratch_shapes=[pltpu.VMEM((2, MROWS, VCOLS), jnp.float32)],
        compiler_params=pltpu.CompilerParams(vmem_limit_bytes=VMEM_SMALL),
        cost_estimate=pl.CostEstimate(flops=6 * 10**9, bytes_accessed=8 * 10**6, transcendentals=0),
    )(place, *values, *query_keys, near, far, *taps)


def pack_kernel(members, control, query, key, value, *refs):
    outs, sems = refs[:-1], refs[-1]
    copies = []
    for index, out in enumerate(outs):
        count = out.shape[0]
        span = pl.ds(pl.multiple_of(control[members[index]], 512), count)
        for kind, (ref, col, width) in enumerate(
            ((query, 0, QCOLS), (key, QCOLS, QCOLS), (value, 2 * QCOLS, VCOLS))
        ):
            copies.append(
                pltpu.make_async_copy(ref.at[span], out.at[:, pl.ds(col, width)], sems.at[index, kind])
            )
    for copy in copies:
        copy.start()
    for copy in copies:
        copy.wait()


def pack(control, weights, members):
    counts = [PIECES[member] for member in members]
    hbm = pl.BlockSpec(memory_space=pltpu.HBM)
    return pl.pallas_call(
        functools.partial(pack_kernel, members),
        out_shape=[jax.ShapeDtypeStruct((count, GCOLS), jnp.bfloat16) for count in counts],
        in_specs=[pl.BlockSpec(memory_space=pltpu.SMEM)] + [hbm] * 3,
        out_specs=[pl.BlockSpec(memory_space=pltpu.VMEM)] * len(counts),
        scratch_shapes=[pltpu.SemaphoreType.DMA((len(counts), 3))],
        compiler_params=pltpu.CompilerParams(vmem_limit_bytes=VMEM_LIMIT),
    )(control, *weights)


def split_kernel(place, keep, got, part_out, *lows):
    for step in range(NY):
        span = pl.ds(pl.multiple_of((place[Y_AT] + step) % NY * SPLIT, SPLIT), SPLIT)
        total = keep[span, :] + got[span, :].astype(jnp.float32)
        if step == 0:
            part_out[...] = total
        else:
            lows[step - 1][...] = total.astype(jnp.bfloat16)


def split(place, keep, got):
    vmem = pl.BlockSpec(memory_space=pltpu.VMEM)
    return pl.pallas_call(
        split_kernel,
        out_shape=[jax.ShapeDtypeStruct((SPLIT, VCOLS), jnp.float32)]
        + [jax.ShapeDtypeStruct((SPLIT, VCOLS), jnp.bfloat16)] * 3,
        in_specs=[pl.BlockSpec(memory_space=pltpu.SMEM), vmem, vmem],
        out_specs=[vmem] * 4,
        compiler_params=pltpu.CompilerParams(vmem_limit_bytes=VMEM_SMALL),
    )(place, keep, got)


def join_kernel(place, *refs):
    blocks, out = refs[:NX], refs[NX]
    width = blocks[0].shape[1]
    for step, block in enumerate(blocks):
        span = pl.ds(pl.multiple_of((place[X_AT] + step) % NX * width, 128), width)
        out[:, span] = block[...]


def join(place, blocks):
    vmem = pl.BlockSpec(memory_space=pltpu.VMEM)
    rows, width = blocks[0].shape
    return pl.pallas_call(
        join_kernel,
        out_shape=jax.ShapeDtypeStruct((rows, NX * width), blocks[0].dtype),
        in_specs=[pl.BlockSpec(memory_space=pltpu.SMEM)] + [vmem] * NX,
        out_specs=vmem,
        compiler_params=pltpu.CompilerParams(vmem_limit_bytes=VMEM_SMALL),
    )(place, *blocks)


def attend_kernel(place, *refs):
    groups = (refs[0:3], refs[3:6])
    mine, theirs = refs[6:10], refs[10:14]
    outs, acc, states = refs[14:18], refs[18], refs[19]
    for step in range(NY):
        span = pl.ds(pl.multiple_of((place[Y_AT] + step) % NY * SPLIT, SPLIT), SPLIT)
        states[1 - place[SAME], span, :] = mine[step][...]
        states[place[SAME], span, :] = theirs[step][...]
    for number, (query, conv, gain) in enumerate(groups):
        state = states.at[number]
        acc[...] = jnp.zeros_like(acc)
        totals = state[FROWS : FROWS + 16, :FROWS]
        for head in range(GROUP):
            feat = features(query[head * FEAT : (head + 1) * FEAT, :], 2.0)
            denom = jnp.dot(totals, feat.astype(jnp.bfloat16), preferred_element_type=jnp.float32)
            scale = 1.0 / denom[head : head + 1, :]
            scaled = (feat * scale).astype(jnp.bfloat16)
            start, stop = window_of(head)
            part = state[:FROWS, start:stop]
            part = jnp.where(head_mask(head, FROWS), part, jnp.zeros_like(part))
            acc[:, start:stop] += lax.dot_general(
                scaled, part, (((0,), (0,)), ((), ())), preferred_element_type=jnp.float32
            )
        low = place[Y_LOW]
        spot = low if number == 0 else 1 - low
        span = pl.ds(pl.multiple_of(spot * VCOLS, VCOLS), VCOLS)
        for block, slot in enumerate(SLOTS):
            rows = slice(block * BLOCK, (block + 1) * BLOCK)
            mixed = acc[rows, :] * gain[3:4, :] + conv[rows, :].astype(jnp.float32)
            outs[slot][:, span] = mixed.astype(jnp.bfloat16)


def attend(place, groups, mine, theirs):
    vmem = pl.BlockSpec(memory_space=pltpu.VMEM)
    return pl.pallas_call(
        attend_kernel,
        out_shape=[jax.ShapeDtypeStruct((BLOCK, 2 * VCOLS), jnp.bfloat16)] * 4,
        in_specs=[pl.BlockSpec(memory_space=pltpu.SMEM)] + [vmem] * 14,
        out_specs=[vmem] * 4,
        scratch_shapes=[
            pltpu.VMEM((ROWS, VCOLS), jnp.float32),
            pltpu.VMEM((2, MROWS, VCOLS), jnp.bfloat16),
        ],
        compiler_params=pltpu.CompilerParams(vmem_limit_bytes=VMEM_SMALL),
    )(place, *[array for group in groups for array in group], *mine, *theirs)


def body(tokens, query_weight, key_weight, value_weight, conv_taps, norm_gain):
    tensor, seq = lax.axis_index("tensor"), lax.axis_index("seq")
    x_at, y_low = tensor // 2, tensor % 2
    core, z_odd = seq % 2, (seq // 2) % 2
    y_at = (seq // 16) * 2 + y_low
    rows = tokens.reshape(BLOCK, tokens.shape[-1])
    weights = (query_weight, key_weight, value_weight)
    half = rows.shape[1] // 2

    base = core * half
    mixed_z = z_odd * 2 * PIECE
    flip = 2 * PIECE - mixed_z
    parts = (mixed_z, mixed_z + PIECE, flip, flip + PIECE, jnp.full_like(z_odd, 4 * PIECE))
    control = jnp.stack(
        [start + shift for start in (base, half - base) for shift in parts]
        + [x_at, y_low, (core == y_low).astype(x_at.dtype), y_at]
    ).astype(jnp.int32)
    part = BLOCK // 2

    def from_side(array):
        return receive(array, lambda x, y, z, c: (x, y + 2 * c - 1, z, c))

    def from_other(array):
        return receive(array, lambda x, y, z, c: (x, y ^ 1, z, c))

    one = from_x(rows, 1)
    three = from_x(rows, -1)
    two_top = from_x(one[:part], 1)
    two_low = from_x(three[part:], -1)

    packed = pack(control, weights, (0, 1, 4))
    side = [from_side(array) for array in packed]
    side_z = [receive(array, lambda x, y, z, c: (x, y, z + 2 * c - 1, c)) for array in side[:2]]
    mine = [side[0], side[1], *side_z, side[2]]
    theirs = [from_core(array) for array in mine]

    blocks = (rows, one, three, two_top, two_low)
    value_early, query_key_early, edge_early, small = project_early(
        blocks[:3], weights, conv_taps, norm_gain[None], ()
    )
    small_other = from_other(small)
    value_late, value_other, query_key_late, query_key_other, edge = project(
        control, blocks, weights, (*mine, *theirs), edge_early, arrived(two_top, two_low, small_other)
    )
    conv_own, conv_other, query_own, query_other, keep, give = states_of(
        control,
        (value_early, value_late, value_other),
        (query_key_early, query_key_late, query_key_other),
        from_other(edge),
        from_far(edge),
        (small, small_other),
    )

    total, *lows = split(control, keep, from_core(give))
    for step, low in zip((1, 2, 3), lows):
        total = total + from_y(low, -step).astype(jnp.float32)
    low = total.astype(jnp.bfloat16)
    for step in (1, -1, 2):
        total = total + from_z(low, step).astype(jnp.float32)
    low = total.astype(jnp.bfloat16)
    quarter = (total + from_z(low, 4).astype(jnp.float32)).astype(jnp.bfloat16)
    mine = [quarter] + [from_y(quarter, step) for step in (1, 2, 3)]
    theirs = [from_core(array) for array in mine]

    out = attend(
        control,
        ((query_own, conv_own, small), (query_other, conv_other, small_other)),
        mine,
        theirs,
    )
    result = join(control, [out[0], from_x(out[3], 1), from_x(out[2], 2), from_x(out[1], -1)])
    return result.reshape(tokens.shape)


def solution(mesh):
    return jax.shard_map(
        body,
        mesh=mesh,
        in_specs=(
            P("seq", "tensor", None),
            P(None, "tensor"),
            P(None, "tensor"),
            P(None, "tensor"),
            P(None, "tensor"),
            P("tensor"),
        ),
        out_specs=P("seq", "tensor", None),
        check_vma=False,
    )
```

```python
import functools

import jax
import jax.numpy as jnp
from jax import lax
from jax.experimental import pallas as pl
from jax.experimental.pallas import tpu as pltpu
from jax.sharding import PartitionSpec as P

FEAT = 16
HEAD_DIM = 80
GROUP = 8
NX, NY, NZ = 4, 4, 8
AXES = ("tensor", "seq")
PIECE = 512
PIECES = (PIECE,) * 10
X_AT, Y_LOW, SAME, Y_AT = 10, 11, 12, 13
VMEM_LIMIT = 58 * 1024 * 1024
VMEM_LATE = 40 * 1024 * 1024
VMEM_SMALL = 16 * 1024 * 1024
FROWS = 160
MROWS = 192
BLOCK = 128
ROWS = 4 * BLOCK
PARTS = ((4,), (0, 1), (2, 3), (5, 6), (7, 8), (9,))
AHEAD = 2
EARLY = 1024
EARLY_COST = 3 * 10**9
ORDER_COST = 5 * 10**9
SLOTS = (0, 1, 3, 2)
VCOLS = GROUP * HEAD_DIM
QCOLS = GROUP * FEAT
GCOLS = VCOLS + 2 * QCOLS
SPLIT = MROWS // NY


def device_of(x, y, z, core):
    x, y, z = x % NX, y % NY, z % NZ
    tensor = x * 2 + (y & 1)
    seq = ((y >> 1) * NZ + z) * 2 + core
    return tensor * 32 + seq


def everywhere():
    return [
        (x, y, z, core)
        for x in range(NX)
        for y in range(NY)
        for z in range(NZ)
        for core in range(2)
    ]


def receive(array, source_of):
    pairs = [(device_of(*source_of(*place)), device_of(*place)) for place in everywhere()]
    return lax.ppermute(array, AXES, pairs)


def from_x(array, step):
    return receive(array, lambda x, y, z, c: (x + step, y, z, c))


def from_y(array, step):
    return receive(array, lambda x, y, z, c: (x, y + step, z, c))


def from_z(array, step):
    return receive(array, lambda x, y, z, c: (x, y, z + step, c))


def from_core(array):
    return receive(array, lambda x, y, z, c: (x, y, z, 1 - c))


def from_far(array):
    place = {}
    for x, y, z, core in everywhere():
        place[x, y & 1, ((y >> 1) * NZ + z) * 2 + core] = device_of(x, y, z, core)
    pairs = []
    for (x, odd, segment), target in place.items():
        source = place.get((x, 1 - odd, segment + (1 if odd else -1)))
        if source is not None:
            pairs.append((source, target))
    return lax.ppermute(array, AXES, pairs)


def features(scaled, off_weight):
    root = 0.5**0.5
    rows = scaled.shape[1]
    parts = [scaled, scaled * scaled * root]
    for step in range(1, FEAT // 2):
        turned = pltpu.roll(scaled, FEAT - step, 0)
        parts.append(scaled * turned * (root * off_weight))
    half = scaled[: FEAT // 2] * scaled[FEAT // 2 :] * (root * off_weight)
    parts.append(half)
    first = lax.broadcasted_iota(jnp.int32, (FEAT // 2, rows), 0) == 0
    parts.append(jnp.where(first, 1.0, 0.0).astype(jnp.float32))
    return jnp.concatenate(parts, axis=0)


def window_of(head):
    start = head * HEAD_DIM // 128 * 128
    stop = -(-(head + 1) * HEAD_DIM // 128) * 128
    return start, stop


def head_mask(head, rows):
    start, stop = window_of(head)
    lane = lax.broadcasted_iota(jnp.int32, (rows, stop - start), 1) + start
    return (lane >= head * HEAD_DIM) & (lane < (head + 1) * HEAD_DIM)


def early_kernel(counts, idle, *refs):
    refs = list(refs)
    blocks = [refs.pop(0) for _ in counts]
    weights = [refs.pop(0) for _ in range(3)]
    taps, gain = refs.pop(0), refs.pop(0)
    del refs[:idle]
    value_out, query_key_out, edge_out, small_out, xs, ws, acc, xsem, wsem = refs
    small_out[: taps.shape[0], :] = taps[...]
    small_out[taps.shape[0] :, :] = gain[...]

    def copies_of(index):
        span, copies, row = pl.ds(pl.multiple_of(index * EARLY, EARLY), EARLY), [], 0
        for number, (ref, rows) in enumerate(zip(blocks, counts)):
            copies.append(
                pltpu.make_async_copy(ref.at[:, span], xs.at[pl.ds(row, rows), span], xsem.at[index, number])
            )
            row += rows
        for kind, (col, width) in enumerate(((0, QCOLS), (QCOLS, QCOLS), (2 * QCOLS, VCOLS))):
            copies.append(
                pltpu.make_async_copy(
                    weights[kind].at[span], ws.at[span, pl.ds(col, width)], wsem.at[index, kind]
                )
            )
        return copies

    count = xs.shape[1] // EARLY
    for index in range(AHEAD):
        for copy in copies_of(index):
            copy.start()
    acc[...] = jnp.zeros_like(acc)

    def step(index, carry):
        for copy in copies_of(index):
            copy.wait()

        @pl.when(index + AHEAD < count)
        def _():
            for copy in copies_of(index + AHEAD):
                copy.start()

        span = pl.ds(pl.multiple_of(index * EARLY, EARLY), EARLY)
        acc[...] += jnp.dot(xs[:, span], ws[span, :], preferred_element_type=jnp.float32)
        return carry

    lax.fori_loop(0, count, step, 0)
    query_key_out[...] = acc[:, : 2 * QCOLS]
    value_out[...] = acc[:, 2 * QCOLS :].astype(jnp.bfloat16)
    edge_out[...] = jnp.zeros_like(edge_out)
    for block, slot in enumerate(SLOTS[:3]):
        for end, row in ((0, block * BLOCK), (1, block * BLOCK + BLOCK - 1)):
            line = acc[row : row + 1, 2 * QCOLS :]
            edge_out[2 * slot + end : 2 * slot + end + 1, :] = line.astype(jnp.bfloat16).astype(jnp.float32)


def project_early(blocks, weights, taps, gain, after):
    counts = tuple(block.shape[0] for block in blocks)
    depth, rows = blocks[0].shape[1], sum(counts)
    hbm = pl.BlockSpec(memory_space=pltpu.HBM)
    vmem = pl.BlockSpec(memory_space=pltpu.VMEM)
    return pl.pallas_call(
        functools.partial(early_kernel, counts, len(after)),
        out_shape=[
            jax.ShapeDtypeStruct((rows, VCOLS), jnp.bfloat16),
            jax.ShapeDtypeStruct((rows, 2 * QCOLS), jnp.float32),
            jax.ShapeDtypeStruct((8, VCOLS), jnp.float32),
            jax.ShapeDtypeStruct((taps.shape[0] + 1, VCOLS), jnp.float32),
        ],
        in_specs=[hbm] * (len(blocks) + 3) + [vmem] * 2 + [hbm] * len(after),
        out_specs=[vmem] * 4,
        scratch_shapes=[
            pltpu.VMEM((rows, depth), jnp.bfloat16),
            pltpu.VMEM((depth, GCOLS), jnp.bfloat16),
            pltpu.VMEM((rows, GCOLS), jnp.float32),
            pltpu.SemaphoreType.DMA((depth // EARLY, len(blocks))),
            pltpu.SemaphoreType.DMA((depth // EARLY, 3)),
        ],
        compiler_params=pltpu.CompilerParams(vmem_limit_bytes=VMEM_LIMIT),
        cost_estimate=pl.CostEstimate(flops=EARLY_COST, bytes_accessed=EARLY_COST // 1000, transcendentals=0),
    )(*blocks, *weights, taps, gain, *after)


def project_kernel(counts, offsets, *refs):
    refs = list(refs)
    blocks = [refs.pop(0) for _ in counts]
    weights = [refs.pop(0) for _ in range(3)]
    pieces = [refs.pop(0) for _ in PIECES]
    edge_early = refs.pop(0)
    refs.pop(0)
    value_outs, query_key_outs, edge_out = refs[0:2], refs[2:4], refs[4]
    xs, ws, acc, late, xsem, wsem, psem = refs[5:]
    stages, at = [], 0
    for index, members in enumerate(PARTS):
        count = len(members) * PIECE
        start = pl.multiple_of(offsets[members[0]], PIECE)
        copies, row = [], 0
        for number, (ref, rows) in enumerate(zip(blocks, counts)):
            copies.append(
                pltpu.make_async_copy(
                    ref.at[:, pl.ds(start, count)],
                    xs.at[pl.ds(row, rows), pl.ds(at, count)],
                    xsem.at[index, number],
                )
            )
            row += rows
        for kind, (col, width) in enumerate(((0, QCOLS), (QCOLS, QCOLS), (2 * QCOLS, VCOLS))):
            copies.append(
                pltpu.make_async_copy(
                    weights[kind].at[pl.ds(start, count)],
                    ws.at[pl.ds(at, count), pl.ds(col, width)],
                    wsem.at[index, kind],
                )
            )
        for step, member in enumerate(members):
            copies.append(
                pltpu.make_async_copy(
                    pieces[member],
                    ws.at[pl.ds(at + step * PIECE, PIECE), pl.ds(GCOLS, GCOLS)],
                    psem.at[member],
                )
            )
        stages.append((copies, at, count))
        at += count
    for copies, _, _ in stages[:AHEAD]:
        for copy in copies:
            copy.start()
    for index, (copies, at, count) in enumerate(stages):
        for copy in copies:
            copy.wait()
        if index + AHEAD < len(stages):
            for copy in stages[index + AHEAD][0]:
                copy.start()
        span = slice(at, at + count)
        part = jnp.dot(xs[:, span], ws[span, GCOLS:], preferred_element_type=jnp.float32)
        last = jnp.dot(xs[ROWS - BLOCK :, span], ws[span, :GCOLS], preferred_element_type=jnp.float32)
        if index == 0:
            acc[...] = part
            late[...] = last
        else:
            acc[...] += part
            late[...] += last
    edge_out[:8, :] = edge_early[...]
    for group, (total, slots) in enumerate(((late, SLOTS[3:]), (acc, SLOTS))):
        query_key_outs[group][...] = total[:, : 2 * QCOLS]
        value_outs[group][...] = total[:, 2 * QCOLS :].astype(jnp.bfloat16)
        for block, slot in enumerate(slots):
            for end, row in ((0, block * BLOCK), (1, block * BLOCK + BLOCK - 1)):
                line = total[row : row + 1, 2 * QCOLS :]
                at = 8 * group + 2 * slot + end
                edge_out[at : at + 1, :] = line.astype(jnp.bfloat16).astype(jnp.float32)


def project(offsets, blocks, weights, pieces, edge_early, after):
    counts = tuple(block.shape[0] for block in blocks)
    depth = blocks[0].shape[1]
    hbm = pl.BlockSpec(memory_space=pltpu.HBM)
    vmem = pl.BlockSpec(memory_space=pltpu.VMEM)
    return pl.pallas_call(
        functools.partial(project_kernel, counts),
        out_shape=[jax.ShapeDtypeStruct((rows, VCOLS), jnp.bfloat16) for rows in (BLOCK, ROWS)]
        + [jax.ShapeDtypeStruct((rows, 2 * QCOLS), jnp.float32) for rows in (BLOCK, ROWS)]
        + [jax.ShapeDtypeStruct((16, VCOLS), jnp.float32)],
        in_specs=[pl.BlockSpec(memory_space=pltpu.SMEM)] + [hbm] * (len(blocks) + 3 + len(pieces)) + [vmem, hbm],
        out_specs=[vmem] * 5,
        scratch_shapes=[
            pltpu.VMEM((ROWS, depth), jnp.bfloat16),
            pltpu.VMEM((depth, 2 * GCOLS), jnp.bfloat16),
            pltpu.VMEM((ROWS, GCOLS), jnp.float32),
            pltpu.VMEM((BLOCK, GCOLS), jnp.float32),
            pltpu.SemaphoreType.DMA((len(PARTS), len(blocks))),
            pltpu.SemaphoreType.DMA((len(PARTS), 3)),
            pltpu.SemaphoreType.DMA((len(pieces),)),
        ],
        compiler_params=pltpu.CompilerParams(vmem_limit_bytes=VMEM_LATE),
        cost_estimate=pl.CostEstimate(
            flops=3 * ROWS * depth * GCOLS, bytes_accessed=2 * depth * (ROWS + 2 * GCOLS), transcendentals=0
        ),
    )(offsets, *blocks, *weights, *pieces, edge_early, after)


def order_kernel(top, low, early, out):
    del top, low, early
    out[...] = jnp.zeros_like(out)


def arrived(top, low, early):
    hbm = pl.BlockSpec(memory_space=pltpu.HBM)
    return pl.pallas_call(
        order_kernel,
        out_shape=jax.ShapeDtypeStruct((8, 128), jnp.float32),
        in_specs=[hbm] * 3,
        out_specs=pl.BlockSpec(memory_space=pltpu.VMEM),
        compiler_params=pltpu.CompilerParams(vmem_limit_bytes=VMEM_LIMIT),
        cost_estimate=pl.CostEstimate(flops=ORDER_COST, bytes_accessed=15 * 10**6, transcendentals=0),
    )(top, low, early)


def state_kernel(place, *refs):
    values, query_keys = ((refs[0], refs[1]), (refs[2],)), ((refs[3], refs[4]), (refs[5],))
    (near, far), taps = refs[6:8], refs[8:10]
    convs, queries, (keep_out, give_out), states = refs[10:12], refs[12:14], refs[14:16], refs[16]
    x_at, even = place[X_AT], place[Y_LOW] == 0
    row = lax.broadcasted_iota(jnp.int32, (BLOCK, VCOLS), 0)
    ones = jnp.ones((8, ROWS), jnp.bfloat16)
    states[...] = jnp.zeros_like(states)
    for group in range(2):
        state, conv_out = states.at[group], convs[group]
        turned = [array[...].T * 0.5 for array in query_keys[group]]
        turned = turned[0] if len(turned) == 1 else jnp.concatenate(turned, axis=1)
        queries[group][...] = turned[:QCOLS]
        key = turned[QCOLS:]
        pieces = [
            array[start : start + BLOCK, :]
            for array in values[group]
            for start in range(0, array.shape[0], BLOCK)
        ]

        def line(ref, block, end):
            at = 8 * (1 - group) + 2 * (block % 4) + end
            return ref[at : at + 1, :]

        for number, block in enumerate(SLOTS):
            span = slice(number * BLOCK, (number + 1) * BLOCK)
            mid = pieces[number].astype(jnp.float32)
            opening = jnp.where((x_at + block) % NX == 0, line(far, block - 1, 1), line(near, block - 1, 1))
            before = jnp.where(even, opening, line(near, block, 1))
            closing = jnp.where((x_at + block) % NX == NX - 1, line(far, block + 1, 0), line(near, block + 1, 0))
            after = jnp.where(even, line(near, block, 0), closing)
            low = jnp.where(row == 0, before, pltpu.roll(mid, 1, 0))
            high = jnp.where(row == BLOCK - 1, after, pltpu.roll(mid, BLOCK - 1, 0))
            tap = taps[group]
            conv = tap[0:1, :] * low + tap[1:2, :] * mid + tap[2:3, :] * high
            conv_out[span, :] = conv.astype(jnp.bfloat16)
        for head in range(GROUP):
            feat = features(key[head * FEAT : (head + 1) * FEAT], 1.0).astype(jnp.bfloat16)
            start, stop = window_of(head)
            share = jnp.dot(feat, conv_out[:, start:stop], preferred_element_type=jnp.float32)
            state[:FROWS, start:stop] += jnp.where(head_mask(head, FROWS), share, 0.0)
            total = lax.dot_general(
                ones, feat, (((1,), (1,)), ((), ())), preferred_element_type=jnp.float32
            )
            state[FROWS + head : FROWS + head + 1, :FROWS] = total[0:1]
    same = place[SAME] == 1
    keep_out[...] = jnp.where(same, states[0], states[1])
    give_out[...] = jnp.where(same, states[1], states[0]).astype(jnp.bfloat16)


def states_of(place, values, query_keys, near, far, taps):
    vmem = pl.BlockSpec(memory_space=pltpu.VMEM)
    return pl.pallas_call(
        state_kernel,
        out_shape=[jax.ShapeDtypeStruct((ROWS, VCOLS), jnp.bfloat16)] * 2
        + [jax.ShapeDtypeStruct((QCOLS, ROWS), jnp.float32)] * 2
        + [
            jax.ShapeDtypeStruct((MROWS, VCOLS), jnp.float32),
            jax.ShapeDtypeStruct((MROWS, VCOLS), jnp.bfloat16),
        ],
        in_specs=[pl.BlockSpec(memory_space=pltpu.SMEM)] + [vmem] * 10,
        out_specs=[vmem] * 6,
        scratch_shapes=[pltpu.VMEM((2, MROWS, VCOLS), jnp.float32)],
        compiler_params=pltpu.CompilerParams(vmem_limit_bytes=VMEM_SMALL),
        cost_estimate=pl.CostEstimate(flops=6 * 10**9, bytes_accessed=8 * 10**6, transcendentals=0),
    )(place, *values, *query_keys, near, far, *taps)


def pack_kernel(members, control, query, key, value, *refs):
    outs, sems = refs[:-1], refs[-1]
    copies = []
    for index, out in enumerate(outs):
        count = out.shape[0]
        span = pl.ds(pl.multiple_of(control[members[index]], 512), count)
        for kind, (ref, col, width) in enumerate(
            ((query, 0, QCOLS), (key, QCOLS, QCOLS), (value, 2 * QCOLS, VCOLS))
        ):
            copies.append(
                pltpu.make_async_copy(ref.at[span], out.at[:, pl.ds(col, width)], sems.at[index, kind])
            )
    for copy in copies:
        copy.start()
    for copy in copies:
        copy.wait()


def pack(control, weights, members):
    counts = [PIECES[member] for member in members]
    hbm = pl.BlockSpec(memory_space=pltpu.HBM)
    return pl.pallas_call(
        functools.partial(pack_kernel, members),
        out_shape=[jax.ShapeDtypeStruct((count, GCOLS), jnp.bfloat16) for count in counts],
        in_specs=[pl.BlockSpec(memory_space=pltpu.SMEM)] + [hbm] * 3,
        out_specs=[pl.BlockSpec(memory_space=pltpu.VMEM)] * len(counts),
        scratch_shapes=[pltpu.SemaphoreType.DMA((len(counts), 3))],
        compiler_params=pltpu.CompilerParams(vmem_limit_bytes=VMEM_LIMIT),
    )(control, *weights)


def split_kernel(place, keep, got, part_out, *lows):
    for step in range(NY):
        span = pl.ds(pl.multiple_of((place[Y_AT] + step) % NY * SPLIT, SPLIT), SPLIT)
        total = keep[span, :] + got[span, :].astype(jnp.float32)
        if step == 0:
            part_out[...] = total
        else:
            lows[step - 1][...] = total.astype(jnp.bfloat16)


def split(place, keep, got):
    vmem = pl.BlockSpec(memory_space=pltpu.VMEM)
    return pl.pallas_call(
        split_kernel,
        out_shape=[jax.ShapeDtypeStruct((SPLIT, VCOLS), jnp.float32)]
        + [jax.ShapeDtypeStruct((SPLIT, VCOLS), jnp.bfloat16)] * 3,
        in_specs=[pl.BlockSpec(memory_space=pltpu.SMEM), vmem, vmem],
        out_specs=[vmem] * 4,
        compiler_params=pltpu.CompilerParams(vmem_limit_bytes=VMEM_SMALL),
    )(place, keep, got)


def join_kernel(place, *refs):
    blocks, out = refs[:NX], refs[NX]
    width = blocks[0].shape[1]
    for step, block in enumerate(blocks):
        span = pl.ds(pl.multiple_of((place[X_AT] + step) % NX * width, 128), width)
        out[:, span] = block[...]


def join(place, blocks):
    vmem = pl.BlockSpec(memory_space=pltpu.VMEM)
    rows, width = blocks[0].shape
    return pl.pallas_call(
        join_kernel,
        out_shape=jax.ShapeDtypeStruct((rows, NX * width), blocks[0].dtype),
        in_specs=[pl.BlockSpec(memory_space=pltpu.SMEM)] + [vmem] * NX,
        out_specs=vmem,
        compiler_params=pltpu.CompilerParams(vmem_limit_bytes=VMEM_SMALL),
    )(place, *blocks)


def attend_kernel(place, *refs):
    groups = (refs[0:3], refs[3:6])
    mine, theirs = refs[6:10], refs[10:14]
    outs, acc, states = refs[14:18], refs[18], refs[19]
    for step in range(NY):
        span = pl.ds(pl.multiple_of((place[Y_AT] + step) % NY * SPLIT, SPLIT), SPLIT)
        states[1 - place[SAME], span, :] = mine[step][...]
        states[place[SAME], span, :] = theirs[step][...]
    for number, (query, conv, gain) in enumerate(groups):
        state = states.at[number]
        acc[...] = jnp.zeros_like(acc)
        totals = state[FROWS : FROWS + 16, :FROWS]
        for head in range(GROUP):
            feat = features(query[head * FEAT : (head + 1) * FEAT, :], 2.0)
            denom = jnp.dot(totals, feat.astype(jnp.bfloat16), preferred_element_type=jnp.float32)
            scale = 1.0 / denom[head : head + 1, :]
            scaled = (feat * scale).astype(jnp.bfloat16)
            start, stop = window_of(head)
            part = state[:FROWS, start:stop]
            part = jnp.where(head_mask(head, FROWS), part, jnp.zeros_like(part))
            acc[:, start:stop] += lax.dot_general(
                scaled, part, (((0,), (0,)), ((), ())), preferred_element_type=jnp.float32
            )
        low = place[Y_LOW]
        spot = low if number == 0 else 1 - low
        span = pl.ds(pl.multiple_of(spot * VCOLS, VCOLS), VCOLS)
        for block, slot in enumerate(SLOTS):
            rows = slice(block * BLOCK, (block + 1) * BLOCK)
            mixed = acc[rows, :] * gain[3:4, :] + conv[rows, :].astype(jnp.float32)
            outs[slot][:, span] = mixed.astype(jnp.bfloat16)


def attend(place, groups, mine, theirs):
    vmem = pl.BlockSpec(memory_space=pltpu.VMEM)
    return pl.pallas_call(
        attend_kernel,
        out_shape=[jax.ShapeDtypeStruct((BLOCK, 2 * VCOLS), jnp.bfloat16)] * 4,
        in_specs=[pl.BlockSpec(memory_space=pltpu.SMEM)] + [vmem] * 14,
        out_specs=[vmem] * 4,
        scratch_shapes=[
            pltpu.VMEM((ROWS, VCOLS), jnp.float32),
            pltpu.VMEM((2, MROWS, VCOLS), jnp.bfloat16),
        ],
        compiler_params=pltpu.CompilerParams(vmem_limit_bytes=VMEM_SMALL),
    )(place, *[array for group in groups for array in group], *mine, *theirs)


def body(tokens, query_weight, key_weight, value_weight, conv_taps, norm_gain):
    tensor, seq = lax.axis_index("tensor"), lax.axis_index("seq")
    x_at, y_low = tensor // 2, tensor % 2
    core, z_odd = seq % 2, (seq // 2) % 2
    y_at = (seq // 16) * 2 + y_low
    rows = tokens.reshape(BLOCK, tokens.shape[-1])
    weights = (query_weight, key_weight, value_weight)
    half = rows.shape[1] // 2

    base = core * half
    mixed_z = z_odd * 2 * PIECE
    flip = 2 * PIECE - mixed_z
    parts = (mixed_z, mixed_z + PIECE, flip, flip + PIECE, jnp.full_like(z_odd, 4 * PIECE))
    control = jnp.stack(
        [start + shift for start in (base, half - base) for shift in parts]
        + [x_at, y_low, (core == y_low).astype(x_at.dtype), y_at]
    ).astype(jnp.int32)
    part = BLOCK // 2

    def from_side(array):
        return receive(array, lambda x, y, z, c: (x, y + 2 * c - 1, z, c))

    def from_other(array):
        return receive(array, lambda x, y, z, c: (x, y ^ 1, z, c))

    one = from_x(rows, 1)
    three = from_x(rows, -1)
    two_top = from_x(one[:part], 1)
    two_low = from_x(three[part:], -1)

    packed = pack(control, weights, (0, 1, 4))
    side = [from_side(array) for array in packed]
    side_z = [receive(array, lambda x, y, z, c: (x, y, z + 2 * c - 1, c)) for array in side[:2]]
    mine = [side[0], side[1], *side_z, side[2]]
    theirs = [from_core(array) for array in mine]

    blocks = (rows, one, three, two_top, two_low)
    value_early, query_key_early, edge_early, small = project_early(
        blocks[:3], weights, conv_taps, norm_gain[None], ()
    )
    small_other = from_other(small)
    value_late, value_other, query_key_late, query_key_other, edge = project(
        control, blocks, weights, (*mine, *theirs), edge_early, arrived(two_top, two_low, small_other)
    )
    conv_own, conv_other, query_own, query_other, keep, give = states_of(
        control,
        (value_early, value_late, value_other),
        (query_key_early, query_key_late, query_key_other),
        from_other(edge),
        from_far(edge),
        (small, small_other),
    )

    total, *lows = split(control, keep, from_core(give))
    for step, low in zip((1, 2, 3), lows):
        total = total + from_y(low, -step).astype(jnp.float32)
    low = total.astype(jnp.bfloat16)
    for step in (1, -1, 2):
        total = total + from_z(low, step).astype(jnp.float32)
    low = total.astype(jnp.bfloat16)
    quarter = (total + from_z(low, 4).astype(jnp.float32)).astype(jnp.bfloat16)
    mine = [quarter] + [from_y(quarter, step) for step in (1, 2, 3)]
    theirs = [from_core(array) for array in mine]

    out = attend(
        control,
        ((query_own, conv_own, small), (query_other, conv_other, small_other)),
        mine,
        theirs,
    )
    result = join(control, [out[0], from_x(out[3], 1), from_x(out[2], 2), from_x(out[1], -1)])
    return result.reshape(tokens.shape)


def solution(mesh):
    return jax.shard_map(
        body,
        mesh=mesh,
        in_specs=(
            P("seq", "tensor", None),
            P(None, "tensor"),
            P(None, "tensor"),
            P(None, "tensor"),
            P(None, "tensor"),
            P("tensor"),
        ),
        out_specs=P("seq", "tensor", None),
        check_vma=False,
    )
```
